128 devices in a mesh: fsdp: 8 (over x, y_hi), tile: 8 (over z, core), dp: 2 (over y_lo).
Axes of the slice: x: 4, y: 4 (y_hi: 2, y_lo: 2; y = y_hi * 2 + y_lo), z: 4, core: 2. Of those that a mesh axis runs over, the one named last changes fastest.
Arguments:
- features: bfloat16 [16, 16, 384, 512], P(('fsdp', 'dp'), 'tile'), may hold values from -6 to 6
- frame_table: bfloat16 [600, 512], replicated, may hold values from -6 to 6
- frame_ids: int32 [16], P(('fsdp', 'dp')), may hold values from 0 to 599
- conv_weight: bfloat16 [1024, 4608], P('fsdp'), may hold values from -0.09375 to 0.09375
- cotangent: bfloat16 [16, 32, 768, 256], P(('fsdp', 'dp'), 'tile'), may hold values from -6 to 6
Outputs:
- upsampled: bfloat16 [16, 32, 768, 256], P(('fsdp', 'dp'), 'tile')
- grad_weight: float32 [1024, 4608], P('fsdp')
- grad_features: bfloat16 [16, 16, 384, 512], P(('fsdp', 'dp'), 'tile')
- grad_table: float32 [600, 512], replicated
The draws below stay inside these ranges and needn't reach their ends.
All inputs are finite; a program needn't handle non-finite values.
Results may differ from the reference program's by a relative error of at most 0.0061.
Values may be sent and summed in bfloat16 or wider, within the bound.
A program may use at most 256 MiB of HBM per device.

```python
import jax
import jax.numpy as jnp
from jax import lax

CIN = 512
COUT = 256
VIDEO = 600
WIDTH = 384
FRAMES = 16
HEIGHT = 16


def set_ends(result, key, smallest, top_value):
    longest = result.shape.index(max(result.shape))
    spots = []
    for shift in (0, 1):
        where = [jax.random.randint(jax.random.fold_in(key, axis), (), 0, length) for axis, length in enumerate(result.shape)]
        where[longest] = (where[longest] + shift) % result.shape[longest]
        spots.append(tuple(where))
    return result.at[spots[0]].set(smallest).at[spots[1]].set(top_value)


def shard_levels(own_key, shape, cuts, smallest, high):
    def one(axis_at, parts):
        draws = jax.random.uniform(jax.random.fold_in(jax.random.fold_in(own_key, 6), axis_at), (parts,), jnp.float32, smallest / len(cuts), high / len(cuts))
        return jnp.repeat(jnp.exp(draws), shape[axis_at] // parts).reshape((-1,) + (1,) * (len(shape) - axis_at - 1))

    factor_of = one(*cuts[0])
    for cut in cuts[1:]:
        factor_of = factor_of * one(*cut)
    return factor_of


def noise(own_key, extent, deviation, limit, cuts=(), held_as=jnp.bfloat16):
    entries = jax.random.normal(own_key, extent, jnp.float32) * deviation
    if len(cuts) > 0:
        entries = shard_levels(own_key, extent, cuts, -0.22, 0.18) * entries
    return jnp.clip(entries, min=-limit, max=limit).astype(held_as)


def setup_inputs(seed: int = 0) -> dict:
    splits = jax.random.split(jax.random.key(seed), 6)
    features = noise(splits[0], (FRAMES, HEIGHT, WIDTH, CIN), 1.0, 6.0, ((0, 16), (1, 8)))
    frame_table = noise(splits[1], (VIDEO, CIN), 1.0, 6.0)
    frame_ids = set_ends(jax.random.randint(splits[2], (FRAMES,), 0, VIDEO), jax.random.fold_in(splits[2], 1), 0, VIDEO - 1).astype(jnp.int32)
    conv_weight = noise(splits[3], (4 * COUT, 9 * CIN), (9 * CIN) ** -0.5, 0.09375, ((0, 8),))
    cotangent = noise(splits[4], (FRAMES, 2 * HEIGHT, 2 * WIDTH, COUT), 1.0, 6.0, ((0, 16), (1, 8)))
    return dict(features=features, frame_table=frame_table, frame_ids=frame_ids, conv_weight=conv_weight, cotangent=cotangent)


inv_root_two = 0.7071067811865476
inv_root_tau = 0.3989422804014327


def gelu_value(values):
    return 0.5 * values * (1.0 + lax.erf(values * inv_root_two))


def gelu_slope(values):
    return 0.5 * (1.0 + lax.erf(values * inv_root_two)) + values * jnp.exp(-0.5 * values * values) * inv_root_tau


def pad_frame(blocks):
    return jnp.pad(blocks, ((0, 0), (1, 1), (1, 1), (0, 0)))


def shuffle(blocks):
    count, row_count, col_count, channels = blocks.shape
    narrow = channels // 4
    spread = blocks.reshape(count, row_count, col_count, 2, 2, narrow).transpose(0, 1, 3, 2, 4, 5)
    return spread.reshape(count, 2 * row_count, 2 * col_count, narrow)


def unshuffle(image):
    count, tall, broad, narrow = image.shape
    split = image.reshape(count, tall // 2, 2, broad // 2, 2, narrow).transpose(0, 1, 3, 2, 4, 5)
    return split.reshape(count, tall // 2, broad // 2, 4 * narrow)


def conv_rows(padded, weight_rows):
    row_count = padded.shape[1] - 2
    col_count = padded.shape[2] - 2
    chan_in = padded.shape[3]
    summed = None
    for tap_index in range(9):
        row_off, col_off = tap_index // 3, tap_index % 3
        window = padded[:, row_off:row_off + row_count, col_off:col_off + col_count, :]
        taps = weight_rows[:, tap_index * chan_in:(tap_index + 1) * chan_in]
        partial_sum = lax.dot_general(window, taps, (((3,), (1,)), ((), ())), preferred_element_type=jnp.float32)
        summed = partial_sum if summed is None else summed + partial_sum
    return summed


def weight_term(padded, slopes):
    row_count = slopes.shape[1]
    col_count = slopes.shape[2]
    pieces = []
    for tap_index in range(9):
        row_off, col_off = tap_index // 3, tap_index % 3
        window = padded[:, row_off:row_off + row_count, col_off:col_off + col_count, :]
        pieces.append(lax.dot_general(slopes, window, (((0, 1, 2), (0, 1, 2)), ((), ())), preferred_element_type=jnp.float32))
    return jnp.concatenate(pieces, axis=1)


def input_term(slope_pad, weight_rows):
    row_count = slope_pad.shape[1] - 2
    col_count = slope_pad.shape[2] - 2
    chan_in = weight_rows.shape[1] // 9
    summed = None
    for tap_index in range(9):
        row_off, col_off = tap_index // 3, tap_index % 3
        window = slope_pad[:, 2 - row_off:2 - row_off + row_count, 2 - col_off:2 - col_off + col_count, :]
        taps = weight_rows[:, tap_index * chan_in:(tap_index + 1) * chan_in]
        partial_sum = lax.dot_general(window, taps, (((3,), (0,)), ((), ())), preferred_element_type=jnp.float32)
        summed = partial_sum if summed is None else summed + partial_sum
    return summed


def reference(features, frame_table, frame_ids, conv_weight, cotangent):
    frame_shift = jnp.take(frame_table, frame_ids, axis=0).astype(jnp.float32)
    inputs = (features.astype(jnp.float32) + frame_shift[:, None, None, :]).astype(jnp.bfloat16)
    padded = pad_frame(inputs)
    conv_out = conv_rows(padded, conv_weight)
    upsampled = shuffle(gelu_value(conv_out).astype(jnp.bfloat16))
    slopes = (unshuffle(cotangent).astype(jnp.float32) * gelu_slope(conv_out)).astype(jnp.bfloat16)
    grad_weight = weight_term(padded, slopes)
    input_grad = input_term(pad_frame(slopes), conv_weight)
    frame_sums = jnp.sum(input_grad, axis=(1, 2))
    grad_table = jnp.zeros(frame_table.shape, jnp.float32).at[frame_ids].add(frame_sums)
    return upsampled, grad_weight, input_grad.astype(jnp.bfloat16), grad_table
```

```python
import jax
import jax.numpy as jnp
from jax import lax
from jax.experimental import pallas as pl
from jax.experimental.pallas import tpu as pltpu
from jax.sharding import PartitionSpec as P

inv_root_two = 0.7071067811865476
inv_root_tau = 0.3989422804014327

WIDTH = 384
CIN = 512
HALF = 512
PARTS = 6
PCOLS = 768
CHUNKS = 18

DIMS = 6

GATHER = [
    (0, (3, 4, 5), (2, 1, 0)),
    (1, (3, 4, 5), (0, 2, 1)),
    (2, (3, 4, 5), (1, 0, 2)),
    (3, (), (2, 1, 0, 5, 4, 3)),
    (4, (3,), (2, 1, 0, 5, 4)),
    (5, (4, 3), (2, 1, 0, 5)),
]
REDUCE = [tuple((i + k) % DIMS for k in range(DIMS)) for i in range(PARTS)]
SPREAD = [((3, 4, 5)[g:] + (3, 4, 5)[:g]) for g in range(3)]

G_STEPS = sum(len(order) for _, _, order in GATHER)
MESH = pl.DeviceIdType.MESH


def kernel(
    feat, weight, cot, id_row,
    up_out, gw_out, gf_out, tab_out,
    xs, ss, st, wall, gwb, rcv, fin, ctv, upb, wide_a, wide_b, acc, igp, igr, gfb,
    trow, tpeer, tall,
    loc_sem, x_send, x_recv, g_send, g_recv, s_send, s_recv, r_send, r_recv,
    f_send, f_recv, u_send, u_recv, i_send, i_recv, t_send, t_recv, v_send, v_recv,
):
    f = lax.axis_index("fsdp")
    t = lax.axis_index("tile")
    lo = lax.axis_index("dp")
    x, h = f // 2, f % 2
    z, c = t // 2, t % 2
    xa, xb = x // 2, x % 2
    xe = (xa + xb) % 2
    ye = (h + lo) % 2
    za = z // 2
    ze = (za + z % 2) % 2
    keep = (c + xe) % 2
    active = c == xa
    mine = {1: keep, 2: h, 3: ye, 4: za, 5: ze}
    x_flip = x + 1 - 2 * xb
    z_flip = z + 1 - 2 * (z % 2)
    partner = {
        0: {"fsdp": (3 - x) * 2 + h},
        1: {"fsdp": x_flip * 2 + h},
        2: {"fsdp": x * 2 + 1 - h, "dp": 1 - lo},
        3: {"dp": 1 - lo},
        4: {"tile": (3 - z) * 2 + c},
        5: {"tile": z_flip * 2 + c},
    }
    other_core = {"tile": 2 * z + 1 - c}

    def remote(src, dst, send_sem, recv_sem, device):
        return pltpu.make_async_remote_copy(
            src_ref=src, dst_ref=dst, send_sem=send_sem, recv_sem=recv_sem,
            device_id=device, device_id_type=MESH,
        )

    barrier = pltpu.get_barrier_semaphore()
    for k in range(1, 8):
        pl.semaphore_signal(barrier, inc=1, device_id={"tile": (t + k) % 8}, device_id_type=MESH)
    frame = f * 2 + lo
    for k in range(1, 16):
        to = (frame + k) % 16
        pl.semaphore_signal(
            barrier, inc=1, device_id={"fsdp": to // 2, "dp": to % 2}, device_id_type=MESH
        )

    own_x = pltpu.make_async_copy(feat, xs.at[1, pl.ds(1 + 2 * c, 2)], loc_sem.at[0])
    own_x.start()
    own_w = []
    for part, full, order in GATHER:
        at = [slice(None) if d in full else mine[d] for d in (3, 4, 5)]
        own_w.append(
            pltpu.make_async_copy(
                weight.at[at[0], at[1], at[2], :, pl.ds(PCOLS * part, PCOLS)],
                wall.at[part, keep, h, at[0], at[1], at[2]],
                loc_sem.at[1 + part],
            )
        )

    @pl.when(active)
    def _():
        for copy in own_w:
            copy.start()

    own_ct = []
    for k in range(2):
        own_ct.append(
            pltpu.make_async_copy(cot.at[2 * k + c], ctv.at[2 * c + k], loc_sem.at[7 + k])
        )
        own_ct[-1].start()

    pl.semaphore_wait(barrier, 22)

    copies = {}
    base = 0
    for part, full, order in GATHER:
        done = set(full)
        for k, dim in enumerate(order):
            at = (part,) + tuple(slice(None) if d in done else mine[d] for d in range(1, 6))
            copies[part, k] = remote(
                wall.at[at], wall.at[at], g_send.at[base + k], g_recv.at[base + k], partner[dim]
            )
            done.add(dim)
        base += len(order)

    def when(condition, body):
        if condition is None:
            body()
        else:
            pl.when(condition)(body)

    def g_sends(order, k):
        return None if 0 in order[:k] else active

    def g_recvs(order, k):
        if order[k] == 0:
            return c != xa
        return None if 0 in order[:k] else active

    def gather_step(k):
        for part, _, order in GATHER:
            if k > 0 and k - 1 < len(order):
                when(g_recvs(order, k - 1), copies[part, k - 1].wait_recv)
            if k < len(order):
                if k == 0:
                    def first(part=part):
                        own_w[part].wait()
                        copies[part, 0].start()
                    when(active, first)
                else:
                    when(g_sends(order, k), copies[part, k].start)

    gather_step(0)

    own_x.wait()
    x_pair = remote(
        xs.at[1, pl.ds(1 + 2 * c, 2)], xs.at[1, pl.ds(1 + 2 * c, 2)], x_send.at[0], x_recv.at[0], other_core
    )
    x_pair.start()
    x_pair_in = remote(
        xs.at[1, pl.ds(3 - 2 * c, 2)], xs.at[1, pl.ds(3 - 2 * c, 2)], x_send.at[0], x_recv.at[0], other_core
    )
    sends_rim = jnp.where(c == 0, z > 0, z < 3)
    z_rim = jnp.where(c == 0, jnp.maximum(z - 1, 0), jnp.minimum(z + 1, 3))
    rim_out = [
        remote(xs.at[1, 1 + 3 * c], xs.at[1, 5 - 5 * c], x_send.at[1 + k], x_recv.at[1 + c], {"tile": 2 * z_rim + k})
        for k in range(2)
    ]

    @pl.when(sends_rim)
    def _():
        for copy in rim_out:
            copy.start()

    top_in = remote(xs.at[1, 0], xs.at[1, 0], x_send.at[1], x_recv.at[2], other_core)
    bottom_in = remote(xs.at[1, 5], xs.at[1, 5], x_send.at[1], x_recv.at[1], other_core)

    ct_pair = []
    for k in range(2):
        ct_pair.append(
            remote(cot.at[2 * k + 1 - c], ctv.at[2 * c + k], x_send.at[3 + k], x_recv.at[3 + k], other_core)
        )
        ct_pair[-1].start()

    gather_step(1)

    @pl.when(z == 0)
    def _():
        xs[1, 0] = jnp.zeros((WIDTH, CIN), jnp.bfloat16)
        ss[1, 0] = jnp.zeros((WIDTH, HALF), jnp.bfloat16)

    @pl.when(z == 3)
    def _():
        xs[1, 5] = jnp.zeros((WIDTH, CIN), jnp.bfloat16)
        ss[1, 5] = jnp.zeros((WIDTH, HALF), jnp.bfloat16)

    column = lax.broadcasted_iota(jnp.int32, (WIDTH, 128), 0)

    def shift_row(ref, row):
        for lane in range(4):
            at = pl.ds(128 * lane, 128)
            values = ref[1, row, :, at].astype(jnp.float32)
            right = jnp.where(column == 0, 0.0, pltpu.roll(values, 1, 0))
            left = jnp.where(column == WIDTH - 1, 0.0, pltpu.roll(values, WIDTH - 1, 0))
            ref[0, row, :, at] = right.astype(jnp.bfloat16)
            ref[2, row, :, at] = left.astype(jnp.bfloat16)

    def shift_rows(ref, first, count):
        @pl.loop(0, count)
        def _(k):
            shift_row(ref, first + k)

    shift_rows(xs, 1 + 2 * c, 2)
    gather_step(2)
    x_pair_in.wait_recv()
    shift_rows(xs, 3 - 2 * c, 2)
    gather_step(3)
    pl.when(z > 0)(top_in.wait_recv)
    pl.when(z < 3)(bottom_in.wait_recv)
    shift_rows(xs, 0, 1)
    shift_rows(xs, 5, 1)
    gather_step(4)
    for copy in own_ct:
        copy.wait()
    for copy in ct_pair:
        copy.wait_recv()
    gather_step(5)
    gather_step(6)

    def weight_rows(v):
        return jnp.concatenate(
            [
                wall[kk // 3, v, :, :, :, :, :, 256 * (kk % 3) : 256 * (kk % 3) + 256].reshape(256, 256)
                for kk in range(CHUNKS)
            ],
            axis=1,
        )

    def forward_row(r):
        lhs = jnp.concatenate(
            [
                xs[(kk // 2) % 3, r + kk // 6, :, 256 * (kk % 2) : 256 * (kk % 2) + 256]
                for kk in range(CHUNKS)
            ],
            axis=1,
        )
        for v in range(2):
            acc[:, 256 * v : 256 * v + 256] = lax.dot_general(
                lhs, weight_rows(v), (((1,), (1,)), ((), ())), preferred_element_type=jnp.float32
            )
        for lane in range(2):
            wide_a[lane] = ctv[r, :, 128 * lane : 128 * lane + 128].astype(jnp.float32)

        @pl.loop(0, WIDTH // 32)
        def _(j):
            j = pl.multiple_of(j * 32, 32)
            for v in range(2):
                for lane in range(2):
                    at = pl.ds(256 * v + 128 * lane, 128)
                    value = acc[pl.ds(j, 32), at]
                    grown = 0.5 * (1.0 + lax.erf(value * inv_root_two))
                    slope = grown + value * jnp.exp(-0.5 * value * value) * inv_root_tau
                    spots = pl.ds(2 * j + v, 32, 2)
                    wide_b[lane, spots, :] = value * grown
                    ss[1, r + 1, pl.ds(j, 32), at] = (wide_a[lane, spots, :] * slope).astype(jnp.bfloat16)

        for lane in range(2):
            upb[r, :, 128 * lane : 128 * lane + 128] = wide_b[lane].astype(jnp.bfloat16)

    @pl.loop(0, 2)
    def _(k):
        forward_row(3 * k)

    slope_up = remote(ss.at[1, 1], ss.at[1, 5], s_send.at[0], s_recv.at[0], {"tile": 2 * jnp.maximum(z - 1, 0) + c})
    slope_down = remote(ss.at[1, 4], ss.at[1, 0], s_send.at[1], s_recv.at[1], {"tile": 2 * jnp.minimum(z + 1, 3) + c})
    pl.when(z > 0)(slope_up.start)
    pl.when(z < 3)(slope_down.start)

    @pl.loop(0, 2)
    def _(k):
        forward_row(2 - k)

    up_own, up_pair = [], []
    for k in range(2):
        up_own.append(pltpu.make_async_copy(upb.at[2 * c + k], up_out.at[2 * k + c], loc_sem.at[9 + k]))
        up_pair.append(
            remote(upb.at[2 * (1 - c) + k], up_out.at[2 * k + c], u_send.at[k], u_recv.at[k], other_core)
        )
        up_own[-1].start()
        up_pair[-1].start()

    for r in range(4):
        st[:, WIDTH * r : WIDTH * r + WIDTH] = ss[1, r + 1].T

    sums = {}
    for part, order in enumerate(REDUCE):
        earlier = []
        for k, dim in enumerate(order):
            src = [part]
            dst = [part, 1 if 0 in earlier else 0]
            here = [part]
            got = [part, 1 if 0 in earlier else 0]
            for d in range(1, 6):
                if d in earlier:
                    src.append(mine[d])
                    here.append(mine[d])
                    dst.append(1 - mine[d])
                    got.append(1 - mine[d])
                elif d == dim:
                    src.append(1 - mine[d])
                    here.append(mine[d])
                    dst.append(1 - mine[d])
                    got.append(mine[d])
                else:
                    for at in (src, dst, here, got):
                        at.append(slice(None))
            copy = remote(
                gwb.at[tuple(src)], rcv.at[tuple(dst)], r_send.at[part, k], r_recv.at[part, k], partner[dim]
            )
            sums[part, k] = (copy, tuple(here), tuple(got))
            earlier.append(dim)

    def r_sends(order, k):
        if order[k] == 0:
            return c != xa
        return active if 0 in order[:k] else None

    def r_recvs(order, k):
        return active if 0 in order[: k + 1] else None

    def reduce_step(part, k):
        order = REDUCE[part]
        if k > 0:
            copy, here, got = sums[part, k - 1]

            def add():
                copy.wait_recv()
                total = gwb[here].astype(jnp.float32) + rcv[got].astype(jnp.float32)
                total = total.astype(jnp.bfloat16)
                if k < DIMS:
                    gwb[here] = total
                else:
                    fin[part, ye, za, ze] = total

            when(r_recvs(order, k - 1), add)
        if k < DIMS:
            when(r_sends(order, k), sums[part, k][0].start)

    for part in range(PARTS):
        for j in range(3):
            kk = 3 * part + j
            window = xs[(kk // 2) % 3, kk // 6 : kk // 6 + 4, :, 256 * (kk % 2) : 256 * (kk % 2) + 256]
            term = jnp.dot(
                st[...], window.reshape(4 * WIDTH, 256), preferred_element_type=jnp.float32
            )
            gwb[part, :, :, :, :, :, :, 256 * j : 256 * j + 256] = term.astype(jnp.bfloat16).reshape(
                2, 2, 2, 2, 2, 16, 256
            )
        reduce_step(part, 0)

    pl.when(z > 0)(lambda: remote(ss.at[1, 0], ss.at[1, 0], s_send.at[1], s_recv.at[1], other_core).wait_recv())
    pl.when(z < 3)(lambda: remote(ss.at[1, 5], ss.at[1, 5], s_send.at[0], s_recv.at[0], other_core).wait_recv())
    shift_rows(ss, 0, 6)

    def input_row(r, out):
        lhs = jnp.concatenate([ss[2 - tap % 3, r + 2 - tap // 3] for tap in range(9)], axis=1)
        for e in range(2):
            chunks = []
            for tap in range(9):
                kk = 2 * tap + e
                chunks.append(
                    wall[kk // 3, :, :, :, :, :, :, 256 * (kk % 3) : 256 * (kk % 3) + 256].reshape(512, 256)
                )
            out[:, 256 * e : 256 * e + 256] = jnp.dot(
                lhs, jnp.concatenate(chunks, axis=0), preferred_element_type=jnp.float32
            )

    @pl.loop(0, 2)
    def _(k):
        input_row(2 * (1 - c) + k, igp.at[k])

    ig_pair = remote(igp, igr, i_send.at[0], i_recv.at[0], other_core)
    ig_pair.start()
    for part in range(PARTS):
        reduce_step(part, 1)

    trow[4:8, :] = id_row[4:8, :]
    trow[0:4, :] = jnp.zeros((4, 128), jnp.float32)

    @pl.loop(0, 2)
    def _(k):
        input_row(2 * c + k, acc)

        @pl.when(k == 0)
        def _():
            ig_pair.wait_recv()

        total = acc[...] + igr[k]
        gfb[k] = total.astype(jnp.bfloat16)
        column_sum = jnp.sum(total, axis=0, keepdims=True)
        for lane in range(4):
            trow[lane : lane + 1, :] += column_sum[:, 128 * lane : 128 * lane + 128]

    gf_copy = pltpu.make_async_copy(gfb, gf_out, loc_sem.at[11])
    gf_copy.start()

    t_copies = []
    for k in range(1, 8):
        copy = remote(trow, tpeer.at[k - 1], t_send.at[k - 1], t_recv.at[k - 1], {"tile": (t + k) % 8})
        copy.start()
        t_copies.append(copy)

    for part in range(PARTS):
        reduce_step(part, 2)

    for copy in t_copies:
        copy.wait_recv()
    for copy in t_copies:
        copy.wait_send()
    total = trow[0:4, :]
    for k in range(7):
        total = total + tpeer[k, 0:4, :]
    tall[0, 0:4, :] = total
    tall[0, 4:8, :] = trow[4:8, :]
    v_copies = []
    for k in range(1, 16):
        to = (frame + k) % 16
        copy = remote(
            tall.at[0], tall.at[k], v_send.at[k - 1], v_recv.at[k - 1], {"fsdp": to // 2, "dp": to % 2}
        )
        copy.start()
        v_copies.append(copy)

    for k in range(3, 7):
        for part in range(PARTS):
            reduce_step(part, k)

    spreads = {}
    for g, order in enumerate(SPREAD):
        done = set()
        for k, dim in enumerate(order):
            at = (pl.ds(2 * g, 2),) + tuple(slice(None) if d in done else mine[d] for d in (3, 4, 5))
            spreads[g, k] = remote(fin.at[at], fin.at[at], f_send.at[g, k], f_recv.at[g, k], partner[dim])
            done.add(dim)

    to_pair = [
        remote(fin.at[pl.ds(2 * g, 2)], gw_out.at[pl.ds(2 * g, 2)], i_send.at[1 + g], i_recv.at[1 + g], other_core)
        for g in range(3)
    ]
    to_self = [
        pltpu.make_async_copy(fin.at[pl.ds(2 * g, 2)], gw_out.at[pl.ds(2 * g, 2)], loc_sem.at[12 + g])
        for g in range(3)
    ]

    @pl.when(active)
    def _():
        for k in range(4):
            for g in range(3):
                if k > 0:
                    spreads[g, k - 1].wait_recv()
                if k < 3:
                    spreads[g, k].start()
                else:
                    to_pair[g].start()
                    to_self[g].start()
        for g in range(3):
            to_self[g].wait()
            to_pair[g].wait_send()
            for k in range(3):
                spreads[g, k].wait_send()

    @pl.when(c != xa)
    def _():
        for g in range(3):
            to_pair[g].wait_recv()

    for copy in v_copies:
        copy.wait()
    tab_copy = pltpu.make_async_copy(tall, tab_out, loc_sem.at[15])
    tab_copy.start()

    for part, _, order in GATHER:
        for k in range(len(order)):
            when(g_sends(order, k), copies[part, k].wait_send)
    for part, order in enumerate(REDUCE):
        for k in range(DIMS):
            when(r_sends(order, k), sums[part, k][0].wait_send)
    x_pair.wait_send()

    @pl.when(sends_rim)
    def _():
        for copy in rim_out:
            copy.wait_send()

    for copy in ct_pair:
        copy.wait_send()
    pl.when(z > 0)(slope_up.wait_send)
    pl.when(z < 3)(slope_down.wait_send)
    for k in range(2):
        up_own[k].wait()
        up_pair[k].wait()
    ig_pair.wait_send()
    gf_copy.wait()
    tab_copy.wait()


def fused(inputs, weight, cot, id_row):
    any_space = pl.BlockSpec(memory_space=pl.ANY)
    vmem = pl.BlockSpec(memory_space=pltpu.VMEM)
    bf16, f32 = jnp.bfloat16, jnp.float32
    dma = pltpu.SemaphoreType.DMA
    return pl.pallas_call(
        kernel,
        out_shape=(
            jax.ShapeDtypeStruct((4, 2 * WIDTH, 256), bf16),
            jax.ShapeDtypeStruct((PARTS, 2, 2, 2, 16, PCOLS), bf16),
            jax.ShapeDtypeStruct((2, WIDTH, CIN), bf16),
            jax.ShapeDtypeStruct((16, 8, 128), f32),
        ),
        in_specs=[any_space, any_space, any_space, vmem],
        out_specs=[any_space] * 4,
        scratch_shapes=[
            pltpu.VMEM((3, 6, WIDTH, CIN), bf16),
            pltpu.VMEM((3, 6, WIDTH, HALF), bf16),
            pltpu.VMEM((HALF, 4 * WIDTH), bf16),
            pltpu.VMEM((PARTS, 2, 2, 2, 2, 2, 16, PCOLS), bf16),
            pltpu.VMEM((PARTS, 2, 2, 2, 2, 2, 16, PCOLS), bf16),
            pltpu.VMEM((PARTS, 2, 2, 2, 2, 2, 2, 16, PCOLS), bf16),
            pltpu.VMEM((PARTS, 2, 2, 2, 16, PCOLS), bf16),
            pltpu.VMEM((4, 2 * WIDTH, 256), bf16),
            pltpu.VMEM((4, 2 * WIDTH, 256), bf16),
            pltpu.VMEM((2, 2 * WIDTH, 128), f32),
            pltpu.VMEM((2, 2 * WIDTH, 128), f32),
            pltpu.VMEM((WIDTH, 512), f32),
            pltpu.VMEM((2, WIDTH, CIN), f32),
            pltpu.VMEM((2, WIDTH, CIN), f32),
            pltpu.VMEM((2, WIDTH, CIN), bf16),
            pltpu.VMEM((8, 128), f32),
            pltpu.VMEM((7, 8, 128), f32),
            pltpu.VMEM((16, 8, 128), f32),
            dma((16,)),
            dma((5,)),
            dma((5,)),
            dma((G_STEPS,)),
            dma((G_STEPS,)),
            dma((2,)),
            dma((2,)),
            dma((PARTS, DIMS)),
            dma((PARTS, DIMS)),
            dma((3, 3)),
            dma((3, 3)),
            dma((2,)),
            dma((2,)),
            dma((4,)),
            dma((4,)),
            dma((7,)),
            dma((7,)),
            dma((15,)),
            dma((15,)),
        ],
        compiler_params=pltpu.CompilerParams(
            collective_id=0, has_side_effects=True, vmem_limit_bytes=60 * 2**20
        ),
        cost_estimate=pl.CostEstimate(
            flops=6 * 768 * 4608 * 1024, bytes_accessed=2 * 10**7, transcendentals=3 * 768 * 1024
        ),
        name="conv_block",
    )(inputs, weight, cot, id_row)


def shards(features, frame_table, frame_ids, conv_weight, cotangent):
    video_len = frame_table.shape[0]
    shift = lax.dynamic_slice_in_dim(frame_table, frame_ids[0], 1, axis=0).astype(jnp.float32)
    inputs = (features[0].astype(jnp.float32) + shift[None]).astype(jnp.bfloat16)
    id_row = jnp.broadcast_to(frame_ids.astype(jnp.float32)[:, None], (8, 128))
    up, gw, gf, tab = fused(
        inputs, conv_weight.reshape(2, 2, 2, 16, 9 * CIN), cotangent[0], id_row
    )
    sums = tab[:, :4].reshape(16, CIN)
    frames = tab[:, 4, 0]
    picker = (frames[:, None] == jnp.arange(video_len, dtype=jnp.float32)[None, :]).astype(jnp.float32)
    grad_table = lax.dot_general(
        picker, sums, (((0,), (0,)), ((), ())),
        precision=lax.Precision.HIGHEST, preferred_element_type=jnp.float32,
    )
    grad_weight = gw.reshape(PARTS, 128, PCOLS).transpose(1, 0, 2).reshape(128, 9 * CIN).astype(jnp.float32)
    return (up[None], grad_weight, gf[None], grad_table)


def solution(mesh):
    return jax.shard_map(
        shards,
        mesh=mesh,
        in_specs=(
            P(("fsdp", "dp"), "tile", None, None),
            P(),
            P(("fsdp", "dp")),
            P("fsdp", None),
            P(("fsdp", "dp"), "tile", None, None),
        ),
        out_specs=(
            P(("fsdp", "dp"), "tile", None, None),
            P("fsdp", None),
            P(("fsdp", "dp"), "tile", None, None),
            P(),
        ),
        check_vma=False,
    )
```

```python
import jax
import jax.numpy as jnp
from jax import lax
from jax.experimental import pallas as pl
from jax.experimental.pallas import tpu as pltpu
from jax.sharding import PartitionSpec as P

inv_root_two = 0.7071067811865476
inv_root_tau = 0.3989422804014327

WIDTH = 384
CIN = 512
HALF = 512
PARTS = 6
PCOLS = 768
CHUNKS = 18

DIMS = 6

REDUCE = [tuple((i + k) % DIMS for k in range(DIMS)) for i in range(PARTS)]
MESH = pl.DeviceIdType.MESH


def kernel(
    feat, weight, cot, shift_row, id_row,
    up_out, gw_out, gf_out, tab_out,
    xs, ss, st, wall, gwb, rcv, fin, ctv, cts, actv, upb, wide, acc, igp, igr, gfb,
    trow, tpeer, tall,
    loc_sem, x_send, x_recv, o_send, o_recv, n_send, n_recv, q_send, q_recv, s_send, s_recv,
    r_send, r_recv, f_send, f_recv, u_send, u_recv, i_send, i_recv, t_send, t_recv, v_send, v_recv,
):
    f = lax.axis_index("fsdp")
    t = lax.axis_index("tile")
    lo = lax.axis_index("dp")
    x, h = f // 2, f % 2
    z, c = t // 2, t % 2
    xa, xb = x // 2, x % 2
    xe = (xa + xb) % 2
    ye = (h + lo) % 2
    za = z // 2
    ze = (za + z % 2) % 2
    keep = (c + xe) % 2
    active = c == xa
    mine = {1: keep, 2: h, 3: ye, 4: za, 5: ze}
    x_flip = x + 1 - 2 * xb
    z_flip = z + 1 - 2 * (z % 2)
    partner = {
        0: {"fsdp": (3 - x) * 2 + h},
        1: {"fsdp": x_flip * 2 + h},
        2: {"fsdp": x * 2 + 1 - h, "dp": 1 - lo},
        3: {"dp": 1 - lo},
        4: {"tile": (3 - z) * 2 + c},
        5: {"tile": z_flip * 2 + c},
    }
    other_core = {"tile": 2 * z + 1 - c}
    two_away = {"fsdp": (x + 2) % 4 * 2 + h}
    quarter = (z + 2 * ye) % 4
    holders = [
        {"tile": (z + k // 2) % 4 * 2 + c, "dp": (lo + k % 2) % 2} for k in range(1, 8)
    ]

    def remote(src, dst, send_sem, recv_sem, device):
        return pltpu.make_async_remote_copy(
            src_ref=src, dst_ref=dst, send_sem=send_sem, recv_sem=recv_sem,
            device_id=device, device_id_type=MESH,
        )

    barrier = pltpu.get_barrier_semaphore()
    for k in range(1, 8):
        pl.semaphore_signal(barrier, inc=1, device_id={"tile": (t + k) % 8}, device_id_type=MESH)
    frame = f * 2 + lo
    for k in range(1, 16):
        to = (frame + k) % 16
        pl.semaphore_signal(
            barrier, inc=1, device_id={"fsdp": to // 2, "dp": to % 2}, device_id_type=MESH
        )

    for k in (3, 5, 7):
        pl.semaphore_signal(barrier, inc=1, device_id=holders[k - 1], device_id_type=MESH)

    near, far = keep, 1 - keep
    own_x = pltpu.make_async_copy(feat, xs.at[1, pl.ds(1 + 2 * c, 2)], loc_sem.at[0])
    own_x.start()
    own_w = [
        pltpu.make_async_copy(
            weight.at[:, :, :, :, pl.ds(PCOLS * part, PCOLS)], wall.at[part, near, h], loc_sem.at[1 + part]
        )
        for part in range(PARTS)
    ]

    @pl.when(active)
    def _():
        for copy in own_w:
            copy.start()

    own_ct = []
    for k in range(2):
        own_ct.append(
            pltpu.make_async_copy(cot.at[2 * k + c], ctv.at[2 * c + k], loc_sem.at[7 + k])
        )
        own_ct[-1].start()

    own_x.wait()
    for k in range(2):
        for lane in range(4):
            at = pl.ds(128 * lane, 128)
            row = xs[1, 1 + 2 * c + k, :, at].astype(jnp.float32) + shift_row[:, at]
            xs[1, 1 + 2 * c + k, :, at] = row.astype(jnp.bfloat16)

    pl.semaphore_wait(barrier, 25)

    def piece(pair, half, number):
        return wall.at[:, pair, half, number // 2, number % 2]

    def same(pair, half, number, send_sem, recv_sem, device):
        return remote(piece(pair, half, number), piece(pair, half, number), send_sem, recv_sem, device)

    turn = [(quarter + k) % 4 for k in range(4)]
    to_flip = [same(near, h, turn[k], o_send.at[k], o_recv.at[k], partner[1]) for k in range(4)]
    to_turn = [same(near, h, turn[k], o_send.at[4 + k], o_recv.at[4 + k], partner[0]) for k in range(4)]
    to_far = same(near, h, quarter, o_send.at[8], o_recv.at[8], two_away)
    from_flip = [same(far, h, turn[k], o_send.at[k], o_recv.at[k], partner[1]) for k in range(4)]
    from_turn = to_turn
    from_far = same(far, h, quarter, o_send.at[8], o_recv.at[8], two_away)
    across = [same(pair, h, quarter, n_send.at[k], n_recv.at[k], partner[2]) for k, pair in enumerate((near, far))]
    crossed = [same(pair, 1 - h, quarter, n_send.at[k], n_recv.at[k], partner[2]) for k, pair in enumerate((near, far))]
    passed = {}
    theirs = {3: (quarter + 2) % 4, 4: (3 - z + 2 * ye) % 4, 5: (z_flip + 2 * ye) % 4}
    for k, (pair, half) in enumerate(((near, 1 - h), (far, 1 - h), (far, h))):
        for j, dim in enumerate((3, 4, 5)):
            passed[k, j] = (
                same(pair, half, quarter, q_send.at[k, j], q_recv.at[k, j], partner[dim]),
                same(pair, half, theirs[dim], q_send.at[k, j], q_recv.at[k, j], partner[dim]),
            )

    def pass_on(k):
        for j in range(3):
            passed[k, j][0].start()

    def passed_in(k):
        for j in range(3):
            passed[k, j][1].wait_recv()

    @pl.when(active)
    def _():
        for copy in own_w:
            copy.wait()
        to_turn[0].start()
        to_flip[0].start()
        across[0].start()
        to_far.start()
        for k in range(1, 4):
            to_turn[k].start()
            to_flip[k].start()

    x_pair = remote(
        xs.at[1, pl.ds(1 + 2 * c, 2)], xs.at[1, pl.ds(1 + 2 * c, 2)], x_send.at[0], x_recv.at[0], other_core
    )
    x_pair_in = remote(
        xs.at[1, pl.ds(3 - 2 * c, 2)], xs.at[1, pl.ds(3 - 2 * c, 2)], x_send.at[0], x_recv.at[0], other_core
    )
    rim_cols = WIDTH // 2
    sends_rim = jnp.where(c == 0, z > 0, z < 3)
    z_rim = jnp.where(c == 0, jnp.maximum(z - 1, 0), jnp.minimum(z + 1, 3))
    rim_out = [
        remote(
            xs.at[1, 1 + 3 * c, pl.ds(rim_cols * k, rim_cols)],
            xs.at[1, 5 - 5 * c, pl.ds(rim_cols * k, rim_cols)],
            x_send.at[1 + k], x_recv.at[1 + c], {"tile": 2 * z_rim + k},
        )
        for k in range(2)
    ]

    def rim_part(row, core, sem):
        at = xs.at[1, row, pl.ds(pl.multiple_of(rim_cols * core, rim_cols), rim_cols)]
        return remote(at, at, x_send.at[sem], x_recv.at[sem], other_core)

    top_in, bottom_in = rim_part(0, c, 2), rim_part(5, c, 1)
    top_swap, bottom_swap = rim_part(0, c, 5), rim_part(5, c, 6)
    top_swapped, bottom_swapped = rim_part(0, 1 - c, 5), rim_part(5, 1 - c, 6)

    @pl.when(sends_rim)
    def _():
        for copy in rim_out:
            copy.start()

    x_pair.start()

    ct_pair = []
    for k in range(2):
        ct_pair.append(
            remote(cot.at[2 * k + 1 - c], ctv.at[2 * c + k], x_send.at[3 + k], x_recv.at[3 + k], other_core)
        )
        ct_pair[-1].start()

    @pl.when(z == 0)
    def _():
        xs[1, 0] = jnp.zeros((WIDTH, CIN), jnp.bfloat16)
        ss[1, 0] = jnp.zeros((WIDTH, HALF), jnp.bfloat16)

    @pl.when(z == 3)
    def _():
        xs[1, 5] = jnp.zeros((WIDTH, CIN), jnp.bfloat16)
        ss[1, 5] = jnp.zeros((WIDTH, HALF), jnp.bfloat16)

    column = lax.broadcasted_iota(jnp.int32, (WIDTH, 128), 0)

    def shift_row(ref, row):
        for lane in range(4):
            at = pl.ds(128 * lane, 128)
            values = ref[1, row, :, at].astype(jnp.float32)
            right = jnp.where(column == 0, 0.0, pltpu.roll(values, 1, 0))
            left = jnp.where(column == WIDTH - 1, 0.0, pltpu.roll(values, WIDTH - 1, 0))
            ref[0, row, :, at] = right.astype(jnp.bfloat16)
            ref[2, row, :, at] = left.astype(jnp.bfloat16)

    def shift_rows(ref, first, count):
        @pl.loop(0, count)
        def _(k):
            shift_row(ref, first + k)

    shift_rows(xs, 1 + 2 * c, 2)

    @pl.when(active)
    def _():
        from_flip[0].wait_recv()

    @pl.when(c != xa)
    def _():
        from_turn[0].wait_recv()
        across[0].start()
        from_far.wait_recv()

    across[1].start()
    pl.when(c != xa)(lambda: pass_on(2))

    x_pair_in.wait_recv()
    shift_rows(xs, 3 - 2 * c, 2)

    @pl.when(z > 0)
    def _():
        top_in.wait_recv()
        top_swap.start()

    @pl.when(z < 3)
    def _():
        bottom_in.wait_recv()
        bottom_swap.start()

    crossed[0].wait_recv()
    pass_on(0)

    for copy in own_ct:
        copy.wait()
    for copy in ct_pair:
        copy.wait_recv()

    @pl.loop(0, 4)
    def _(r):
        for lane in range(2):
            wide[lane] = ctv[r, :, 128 * lane : 128 * lane + 128].astype(jnp.float32)
        for v in range(2):
            for lane in range(2):
                cts[v, r, :, 128 * lane : 128 * lane + 128] = wide[lane, pl.ds(v, WIDTH, 2), :].astype(jnp.bfloat16)

    crossed[1].wait_recv()
    pass_on(1)

    @pl.when(z > 0)
    def _():
        top_swapped.wait_recv()

    @pl.when(z < 3)
    def _():
        bottom_swapped.wait_recv()

    shift_rows(xs, 0, 1)
    shift_rows(xs, 5, 1)

    def forward_row(v, r):
        lhs = jnp.concatenate(
            [
                xs[(kk // 2) % 3, r + kk // 6, :, 256 * (kk % 2) : 256 * (kk % 2) + 256]
                for kk in range(CHUNKS)
            ],
            axis=1,
        )
        rhs = jnp.concatenate(
            [
                wall[kk // 3, v, :, :, :, :, :, 256 * (kk % 3) : 256 * (kk % 3) + 256].reshape(256, 256)
                for kk in range(CHUNKS)
            ],
            axis=1,
        )
        acc[:, :256] = lax.dot_general(
            lhs, rhs, (((1,), (1,)), ((), ())), preferred_element_type=jnp.float32
        )

        @pl.loop(0, WIDTH // 32)
        def _(j):
            rows = pl.ds(pl.multiple_of(j * 32, 32), 32)
            value = acc[rows, :256]
            grown = 0.5 * (1.0 + lax.erf(value * inv_root_two))
            slope = grown + value * jnp.exp(-0.5 * value * value) * inv_root_tau
            actv[v, r, rows] = (value * grown).astype(jnp.bfloat16)
            out = pl.ds(pl.multiple_of(256 * v, 256), 256)
            ss[1, r + 1, rows, out] = (cts[v, r, rows].astype(jnp.float32) * slope).astype(jnp.bfloat16)

    passed_in(0)

    @pl.when(c != xa)
    def _():
        for k in range(1, 4):
            from_turn[k].wait_recv()

    @pl.loop(0, 4)
    def _(r):
        forward_row(near, r)

    passed_in(1)

    @pl.when(c != xa)
    def _():
        passed_in(2)

    @pl.when(active)
    def _():
        for k in range(1, 4):
            from_flip[k].wait_recv()

    @pl.loop(0, 2)
    def _(k):
        forward_row(far, 3 * k)

    slope_up = remote(ss.at[1, 1], ss.at[1, 5], s_send.at[0], s_recv.at[0], {"tile": 2 * jnp.maximum(z - 1, 0) + c})
    slope_down = remote(ss.at[1, 4], ss.at[1, 0], s_send.at[1], s_recv.at[1], {"tile": 2 * jnp.minimum(z + 1, 3) + c})
    pl.when(z > 0)(slope_up.start)
    pl.when(z < 3)(slope_down.start)

    @pl.loop(0, 2)
    def _(k):
        forward_row(far, 2 - k)

    for r in range(4):
        st[:, WIDTH * r : WIDTH * r + WIDTH] = ss[1, r + 1].T

    sums = {}
    for part, order in enumerate(REDUCE):
        earlier = []
        for k, dim in enumerate(order):
            src = [part]
            dst = [part, 1 if 0 in earlier else 0]
            here = [part]
            got = [part, 1 if 0 in earlier else 0]
            for d in range(1, 6):
                if d in earlier:
                    src.append(mine[d])
                    here.append(mine[d])
                    dst.append(1 - mine[d])
                    got.append(1 - mine[d])
                elif d == dim:
                    src.append(1 - mine[d])
                    here.append(mine[d])
                    dst.append(1 - mine[d])
                    got.append(mine[d])
                else:
                    for at in (src, dst, here, got):
                        at.append(slice(None))
            copy = remote(
                gwb.at[tuple(src)], rcv.at[tuple(dst)], r_send.at[part, k], r_recv.at[part, k], partner[dim]
            )
            sums[part, k] = (copy, tuple(here), tuple(got))
            earlier.append(dim)

    def when(condition, body):
        if condition is None:
            body()
        else:
            pl.when(condition)(body)

    def r_sends(order, k):
        if order[k] == 0:
            return c != xa
        return active if 0 in order[:k] else None

    def r_recvs(order, k):
        return active if 0 in order[: k + 1] else None

    def reduce_step(part, k):
        order = REDUCE[part]
        if k > 0:
            copy, here, got = sums[part, k - 1]

            def add():
                copy.wait_recv()
                total = gwb[here].astype(jnp.float32) + rcv[got].astype(jnp.float32)
                total = total.astype(jnp.bfloat16)
                if k < DIMS:
                    gwb[here] = total
                else:
                    fin[part, ye, za, ze] = total

            when(r_recvs(order, k - 1), add)
        if k < DIMS:
            when(r_sends(order, k), sums[part, k][0].start)

    for part in range(PARTS):
        for j in range(3):
            kk = 3 * part + j
            window = xs[(kk // 2) % 3, kk // 6 : kk // 6 + 4, :, 256 * (kk % 2) : 256 * (kk % 2) + 256]
            term = jnp.dot(
                st[...], window.reshape(4 * WIDTH, 256), preferred_element_type=jnp.float32
            )
            gwb[part, :, :, :, :, :, :, 256 * j : 256 * j + 256] = term.astype(jnp.bfloat16).reshape(
                2, 2, 2, 2, 2, 16, 256
            )
        reduce_step(part, 0)

    pl.when(z > 0)(lambda: remote(ss.at[1, 0], ss.at[1, 0], s_send.at[1], s_recv.at[1], other_core).wait_recv())
    pl.when(z < 3)(lambda: remote(ss.at[1, 5], ss.at[1, 5], s_send.at[0], s_recv.at[0], other_core).wait_recv())
    shift_rows(ss, 0, 6)

    def input_row(r, out):
        lhs = jnp.concatenate([ss[2 - tap % 3, r + 2 - tap // 3] for tap in range(9)], axis=1)
        for e in range(2):
            chunks = []
            for tap in range(9):
                kk = 2 * tap + e
                chunks.append(
                    wall[kk // 3, :, :, :, :, :, :, 256 * (kk % 3) : 256 * (kk % 3) + 256].reshape(512, 256)
                )
            out[:, 256 * e : 256 * e + 256] = jnp.dot(
                lhs, jnp.concatenate(chunks, axis=0), preferred_element_type=jnp.float32
            )

    @pl.loop(0, 2)
    def _(k):
        input_row(2 * (1 - c) + k, igp.at[k])

    ig_pair = remote(igp, igr, i_send.at[0], i_recv.at[0], other_core)
    ig_pair.start()
    for part in range(PARTS):
        reduce_step(part, 1)

    trow[4:8, :] = id_row[4:8, :]
    trow[0:4, :] = jnp.zeros((4, 128), jnp.float32)

    @pl.loop(0, 2)
    def _(k):
        input_row(2 * c + k, acc)

        @pl.when(k == 0)
        def _():
            ig_pair.wait_recv()

        total = acc[...] + igr[k]
        gfb[k] = total.astype(jnp.bfloat16)
        column_sum = jnp.sum(total, axis=0, keepdims=True)
        for lane in range(4):
            trow[lane : lane + 1, :] += column_sum[:, 128 * lane : 128 * lane + 128]

    gf_copy = pltpu.make_async_copy(gfb, gf_out, loc_sem.at[11])
    gf_copy.start()

    t_copies = []
    for k in range(1, 8):
        copy = remote(trow, tpeer.at[k - 1], t_send.at[k - 1], t_recv.at[k - 1], {"tile": (t + k) % 8})
        copy.start()
        t_copies.append(copy)

    for part in range(PARTS):
        reduce_step(part, 2)

    for copy in t_copies:
        copy.wait_recv()
    for copy in t_copies:
        copy.wait_send()
    total = trow[0:4, :]
    for k in range(7):
        total = total + tpeer[k, 0:4, :]
    tall[0, 0:4, :] = total
    tall[0, 4:8, :] = trow[4:8, :]
    v_copies = []
    for k in range(1, 16):
        to = (frame + k) % 16
        copy = remote(
            tall.at[0], tall.at[k], v_send.at[k - 1], v_recv.at[k - 1], {"fsdp": to // 2, "dp": to % 2}
        )
        copy.start()
        v_copies.append(copy)

    @pl.loop(0, 4)
    def _(r):
        for lane in range(2):
            lanes = pl.ds(128 * lane, 128)
            for v in range(2):
                wide[lane, pl.ds(v, WIDTH, 2), :] = actv[v, r, :, lanes].astype(jnp.float32)
            upb[r, :, lanes] = wide[lane].astype(jnp.bfloat16)

    up_own, up_pair = [], []
    for k in range(2):
        up_own.append(pltpu.make_async_copy(upb.at[2 * c + k], up_out.at[2 * k + c], loc_sem.at[9 + k]))
        up_pair.append(
            remote(upb.at[2 * (1 - c) + k], up_out.at[2 * k + c], u_send.at[k], u_recv.at[k], other_core)
        )
        up_own[-1].start()
        up_pair[-1].start()

    for k in range(3, 6):
        for part in range(PARTS):
            reduce_step(part, k)

    spreads, to_pair, to_self = [], [], []
    for g in range(2):
        parts = pl.ds(3 * g, 3)
        at = fin.at[parts, ye, za, ze]
        spreads.append(
            [remote(at, at, f_send.at[g, k], f_recv.at[g, k], holders[k]) for k in range(7)]
        )
        to_pair.append(remote(fin.at[parts], gw_out.at[parts], i_send.at[1 + g], i_recv.at[1 + g], other_core))
        to_self.append(pltpu.make_async_copy(fin.at[parts], gw_out.at[parts], loc_sem.at[12 + g]))

    for g in range(2):
        for part in range(3 * g, 3 * g + 3):
            reduce_step(part, 6)

        @pl.when(active)
        def _(g=g):
            for copy in spreads[g]:
                copy.start()

    @pl.when(active)
    def _():
        for g in range(2):
            for copy in spreads[g]:
                copy.wait_recv()
            to_pair[g].start()
            to_self[g].start()
        for g in range(2):
            for copy in spreads[g]:
                copy.wait_send()
            to_self[g].wait()
            to_pair[g].wait_send()

    @pl.when(c != xa)
    def _():
        for g in range(2):
            to_pair[g].wait_recv()

    for copy in v_copies:
        copy.wait()
    tab_copy = pltpu.make_async_copy(tall, tab_out, loc_sem.at[15])
    tab_copy.start()

    @pl.when(active)
    def _():
        for copy in to_turn + to_flip + [to_far]:
            copy.wait_send()

    @pl.when(c != xa)
    def _():
        for j in range(3):
            passed[2, j][0].wait_send()

    for k in range(2):
        across[k].wait_send()
        for j in range(3):
            passed[k, j][0].wait_send()

    @pl.when(z > 0)
    def _():
        top_swap.wait_send()

    @pl.when(z < 3)
    def _():
        bottom_swap.wait_send()

    for part, order in enumerate(REDUCE):
        for k in range(DIMS):
            when(r_sends(order, k), sums[part, k][0].wait_send)
    x_pair.wait_send()

    @pl.when(sends_rim)
    def _():
        for copy in rim_out:
            copy.wait_send()

    for copy in ct_pair:
        copy.wait_send()
    pl.when(z > 0)(slope_up.wait_send)
    pl.when(z < 3)(slope_down.wait_send)
    for k in range(2):
        up_own[k].wait()
        up_pair[k].wait()
    ig_pair.wait_send()
    gf_copy.wait()
    tab_copy.wait()


def fused(features, weight, cot, shift_row, id_row):
    any_space = pl.BlockSpec(memory_space=pl.ANY)
    vmem = pl.BlockSpec(memory_space=pltpu.VMEM)
    bf16, f32 = jnp.bfloat16, jnp.float32
    dma = pltpu.SemaphoreType.DMA
    return pl.pallas_call(
        kernel,
        out_shape=(
            jax.ShapeDtypeStruct((4, 2 * WIDTH, 256), bf16),
            jax.ShapeDtypeStruct((PARTS, 2, 2, 2, 16, PCOLS), bf16),
            jax.ShapeDtypeStruct((2, WIDTH, CIN), bf16),
            jax.ShapeDtypeStruct((16, 8, 128), f32),
        ),
        in_specs=[any_space, any_space, any_space, vmem, vmem],
        out_specs=[any_space] * 4,
        scratch_shapes=[
            pltpu.VMEM((3, 6, WIDTH, CIN), bf16),
            pltpu.VMEM((3, 6, WIDTH, HALF), bf16),
            pltpu.VMEM((HALF, 4 * WIDTH), bf16),
            pltpu.VMEM((PARTS, 2, 2, 2, 2, 2, 16, PCOLS), bf16),
            pltpu.VMEM((PARTS, 2, 2, 2, 2, 2, 16, PCOLS), bf16),
            pltpu.VMEM((PARTS, 2, 2, 2, 2, 2, 2, 16, PCOLS), bf16),
            pltpu.VMEM((PARTS, 2, 2, 2, 16, PCOLS), bf16),
            pltpu.VMEM((4, 2 * WIDTH, 256), bf16),
            pltpu.VMEM((2, 4, WIDTH, 256), bf16),
            pltpu.VMEM((2, 4, WIDTH, 256), bf16),
            pltpu.VMEM((4, 2 * WIDTH, 256), bf16),
            pltpu.VMEM((2, 2 * WIDTH, 128), f32),
            pltpu.VMEM((WIDTH, 512), f32),
            pltpu.VMEM((2, WIDTH, CIN), f32),
            pltpu.VMEM((2, WIDTH, CIN), f32),
            pltpu.VMEM((2, WIDTH, CIN), bf16),
            pltpu.VMEM((8, 128), f32),
            pltpu.VMEM((7, 8, 128), f32),
            pltpu.VMEM((16, 8, 128), f32),
            dma((16,)),
            dma((7,)),
            dma((7,)),
            dma((9,)),
            dma((9,)),
            dma((2,)),
            dma((2,)),
            dma((3, 3)),
            dma((3, 3)),
            dma((2,)),
            dma((2,)),
            dma((PARTS, DIMS)),
            dma((PARTS, DIMS)),
            dma((2, 7)),
            dma((2, 7)),
            dma((2,)),
            dma((2,)),
            dma((3,)),
            dma((3,)),
            dma((7,)),
            dma((7,)),
            dma((15,)),
            dma((15,)),
        ],
        compiler_params=pltpu.CompilerParams(
            collective_id=0, has_side_effects=True, vmem_limit_bytes=60 * 2**20
        ),
        cost_estimate=pl.CostEstimate(
            flops=6 * 768 * 4608 * 1024, bytes_accessed=2 * 10**7, transcendentals=3 * 768 * 1024
        ),
        name="conv_block",
    )(features, weight, cot, shift_row, id_row)


def shards(features, frame_table, frame_ids, conv_weight, cotangent):
    video_len = frame_table.shape[0]
    shift = lax.dynamic_slice_in_dim(frame_table, frame_ids[0], 1, axis=0).astype(jnp.float32)
    id_row = jnp.broadcast_to(frame_ids.astype(jnp.float32)[:, None], (8, 128))
    up, gw, gf, tab = fused(
        features[0], conv_weight.reshape(2, 2, 2, 16, 9 * CIN), cotangent[0], shift, id_row
    )
    sums = tab[:, :4].reshape(16, CIN)
    frames = tab[:, 4, 0]
    picker = (frames[:, None] == jnp.arange(video_len, dtype=jnp.float32)[None, :]).astype(jnp.float32)
    grad_table = lax.dot_general(
        picker, sums, (((0,), (0,)), ((), ())),
        precision=lax.Precision.HIGHEST, preferred_element_type=jnp.float32,
    )
    grad_weight = gw.reshape(PARTS, 128, PCOLS).transpose(1, 0, 2).reshape(128, 9 * CIN).astype(jnp.float32)
    return (up[None], grad_weight, gf[None], grad_table)


def solution(mesh):
    return jax.shard_map(
        shards,
        mesh=mesh,
        in_specs=(
            P(("fsdp", "dp"), "tile", None, None),
            P(),
            P(("fsdp", "dp")),
            P("fsdp", None),
            P(("fsdp", "dp"), "tile", None, None),
        ),
        out_specs=(
            P(("fsdp", "dp"), "tile", None, None),
            P("fsdp", None),
            P(("fsdp", "dp"), "tile", None, None),
            P(),
        ),
        check_vma=False,
    )
```

```python
import jax
import jax.numpy as jnp
from jax import lax
from jax.experimental import pallas as pl
from jax.experimental.pallas import tpu as pltpu
from jax.sharding import PartitionSpec as P

inv_root_two = 0.7071067811865476
inv_root_tau = 0.3989422804014327

WIDTH = 384
CIN = 512
HALF = 512
PARTS = 6
PCOLS = 768
CHUNKS = 18

DIMS = 6

FIRST = [(0, 1), (1, 0), (2, 3), (3, 2), (4, 5), (5, 4)]
NEAR_ORDER = (0, 2, 3, 4, 5, 1)
FAR_ORDER = (1, 0, 2, 3, 4, 5)

MESH = pl.DeviceIdType.MESH


def kernel(
    feat, weight, cot, shift_row, id_row,
    up_out, gw_out, gf_out, tab_out,
    xs, ss, st, wall, gwb, got0, got1, got2, got3, fin, ctv, cts, actv, upb, wide, acc, igp, igr, gfb,
    trow, tpeer, tall,
    loc_sem, x_send, x_recv, o_send, o_recv, n_send, n_recv, q_send, q_recv, s_send, s_recv,
    r_send, r_recv, f_send, f_recv, u_send, u_recv, i_send, i_recv, t_send, t_recv, v_send, v_recv,
):
    f = lax.axis_index("fsdp")
    t = lax.axis_index("tile")
    lo = lax.axis_index("dp")
    x, h = f // 2, f % 2
    z, c = t // 2, t % 2
    xa, xb = x // 2, x % 2
    xe = (xa + xb) % 2
    ye = (h + lo) % 2
    za = z // 2
    ze = (za + z % 2) % 2
    keep = (c + xe) % 2
    active = c == xa
    mine = {1: keep, 2: h, 3: ye, 4: za, 5: ze}
    x_flip = x + 1 - 2 * xb
    z_flip = z + 1 - 2 * (z % 2)
    partner = {
        0: {"fsdp": (3 - x) * 2 + h},
        1: {"fsdp": x_flip * 2 + h},
        2: {"fsdp": x * 2 + 1 - h, "dp": 1 - lo},
        3: {"dp": 1 - lo},
        4: {"tile": (3 - z) * 2 + c},
        5: {"tile": z_flip * 2 + c},
    }
    other_core = {"tile": 2 * z + 1 - c}
    two_away = {"fsdp": (x + 2) % 4 * 2 + h}
    quarter = (z + 2 * ye) % 4
    holders = [
        {"tile": (z + k // 2) % 4 * 2 + c, "dp": (lo + k % 2) % 2} for k in range(1, 8)
    ]

    def remote(src, dst, send_sem, recv_sem, device):
        return pltpu.make_async_remote_copy(
            src_ref=src, dst_ref=dst, send_sem=send_sem, recv_sem=recv_sem,
            device_id=device, device_id_type=MESH,
        )

    barrier = pltpu.get_barrier_semaphore()
    for k in range(1, 8):
        pl.semaphore_signal(barrier, inc=1, device_id={"tile": (t + k) % 8}, device_id_type=MESH)
    frame = f * 2 + lo
    for k in range(1, 16):
        to = (frame + k) % 16
        pl.semaphore_signal(
            barrier, inc=1, device_id={"fsdp": to // 2, "dp": to % 2}, device_id_type=MESH
        )

    for k in (3, 5, 7):
        pl.semaphore_signal(barrier, inc=1, device_id=holders[k - 1], device_id_type=MESH)

    near, far = keep, 1 - keep
    own_x = pltpu.make_async_copy(feat, xs.at[1, pl.ds(1 + 2 * c, 2)], loc_sem.at[0])
    own_x.start()
    own_w = [
        pltpu.make_async_copy(
            weight.at[:, :, :, :, pl.ds(PCOLS * part, PCOLS)], wall.at[part, near, h], loc_sem.at[1 + part]
        )
        for part in range(PARTS)
    ]

    @pl.when(active)
    def _():
        for copy in own_w:
            copy.start()

    own_ct = []
    for k in range(2):
        own_ct.append(
            pltpu.make_async_copy(cot.at[2 * k + c], ctv.at[2 * c + k], loc_sem.at[7 + k])
        )
        own_ct[-1].start()

    own_x.wait()
    for k in range(2):
        for lane in range(4):
            at = pl.ds(128 * lane, 128)
            row = xs[1, 1 + 2 * c + k, :, at].astype(jnp.float32) + shift_row[:, at]
            xs[1, 1 + 2 * c + k, :, at] = row.astype(jnp.bfloat16)

    pl.semaphore_wait(barrier, 25)

    def piece(pair, half, number):
        return wall.at[:, pair, half, number // 2, number % 2]

    def same(pair, half, number, send_sem, recv_sem, device):
        return remote(piece(pair, half, number), piece(pair, half, number), send_sem, recv_sem, device)

    turn = [(quarter + k) % 4 for k in range(4)]
    to_flip = [same(near, h, turn[k], o_send.at[k], o_recv.at[k], partner[1]) for k in range(4)]
    to_turn = [same(near, h, turn[k], o_send.at[4 + k], o_recv.at[4 + k], partner[0]) for k in range(4)]
    to_far = same(near, h, quarter, o_send.at[8], o_recv.at[8], two_away)
    from_flip = [same(far, h, turn[k], o_send.at[k], o_recv.at[k], partner[1]) for k in range(4)]
    from_turn = to_turn
    from_far = same(far, h, quarter, o_send.at[8], o_recv.at[8], two_away)
    across = [same(pair, h, quarter, n_send.at[k], n_recv.at[k], partner[2]) for k, pair in enumerate((near, far))]
    crossed = [same(pair, 1 - h, quarter, n_send.at[k], n_recv.at[k], partner[2]) for k, pair in enumerate((near, far))]
    passed = {}
    theirs = {3: (quarter + 2) % 4, 4: (3 - z + 2 * ye) % 4, 5: (z_flip + 2 * ye) % 4}
    for k, (pair, half) in enumerate(((near, 1 - h), (far, 1 - h), (far, h))):
        for j, dim in enumerate((3, 4, 5)):
            passed[k, j] = (
                same(pair, half, quarter, q_send.at[k, j], q_recv.at[k, j], partner[dim]),
                same(pair, half, theirs[dim], q_send.at[k, j], q_recv.at[k, j], partner[dim]),
            )

    def pass_on(k):
        for j in range(3):
            passed[k, j][0].start()

    def passed_in(k):
        for j in range(3):
            passed[k, j][1].wait_recv()

    @pl.when(active)
    def _():
        for copy in own_w:
            copy.wait()
        to_turn[0].start()
        to_flip[0].start()
        across[0].start()
        to_far.start()

    x_pair = remote(
        xs.at[1, pl.ds(1 + 2 * c, 2)], xs.at[1, pl.ds(1 + 2 * c, 2)], x_send.at[0], x_recv.at[0], other_core
    )
    x_pair_in = remote(
        xs.at[1, pl.ds(3 - 2 * c, 2)], xs.at[1, pl.ds(3 - 2 * c, 2)], x_send.at[0], x_recv.at[0], other_core
    )
    rim_cols = WIDTH // 2
    sends_rim = jnp.where(c == 0, z > 0, z < 3)
    z_rim = jnp.where(c == 0, jnp.maximum(z - 1, 0), jnp.minimum(z + 1, 3))
    rim_out = [
        remote(
            xs.at[1, 1 + 3 * c, pl.ds(rim_cols * k, rim_cols)],
            xs.at[1, 5 - 5 * c, pl.ds(rim_cols * k, rim_cols)],
            x_send.at[1 + k], x_recv.at[1 + c], {"tile": 2 * z_rim + k},
        )
        for k in range(2)
    ]

    def rim_part(row, core, sem):
        at = xs.at[1, row, pl.ds(pl.multiple_of(rim_cols * core, rim_cols), rim_cols)]
        return remote(at, at, x_send.at[sem], x_recv.at[sem], other_core)

    top_in, bottom_in = rim_part(0, c, 2), rim_part(5, c, 1)
    top_swap, bottom_swap = rim_part(0, c, 5), rim_part(5, c, 6)
    top_swapped, bottom_swapped = rim_part(0, 1 - c, 5), rim_part(5, 1 - c, 6)

    @pl.when(sends_rim)
    def _():
        for copy in rim_out:
            copy.start()

    x_pair.start()

    ct_pair = []
    for k in range(2):
        ct_pair.append(
            remote(cot.at[2 * k + 1 - c], ctv.at[2 * c + k], x_send.at[3 + k], x_recv.at[3 + k], other_core)
        )
        ct_pair[-1].start()

    @pl.when(z == 0)
    def _():
        xs[1, 0] = jnp.zeros((WIDTH, CIN), jnp.bfloat16)
        ss[1, 0] = jnp.zeros((WIDTH, HALF), jnp.bfloat16)

    @pl.when(z == 3)
    def _():
        xs[1, 5] = jnp.zeros((WIDTH, CIN), jnp.bfloat16)
        ss[1, 5] = jnp.zeros((WIDTH, HALF), jnp.bfloat16)

    column = lax.broadcasted_iota(jnp.int32, (WIDTH, 128), 0)

    def shift_row(ref, row):
        for lane in range(4):
            at = pl.ds(128 * lane, 128)
            values = ref[1, row, :, at].astype(jnp.float32)
            right = jnp.where(column == 0, 0.0, pltpu.roll(values, 1, 0))
            left = jnp.where(column == WIDTH - 1, 0.0, pltpu.roll(values, WIDTH - 1, 0))
            ref[0, row, :, at] = right.astype(jnp.bfloat16)
            ref[2, row, :, at] = left.astype(jnp.bfloat16)

    def shift_rows(ref, first, count):
        @pl.loop(0, count)
        def _(k):
            shift_row(ref, first + k)

    @pl.when(active)
    def _():
        to_turn[0].wait_send()
        to_flip[0].wait_send()
        to_turn[1].start()
        to_flip[1].start()

    shift_rows(xs, 1 + 2 * c, 2)

    @pl.when(active)
    def _():
        from_flip[0].wait_recv()
        across[1].start()
        for k in range(2, 4):
            to_turn[k].start()
            to_flip[k].start()

    @pl.when(c != xa)
    def _():
        from_turn[0].wait_recv()
        across[0].start()
        from_far.wait_recv()
        across[1].start()
        pass_on(2)

    x_pair_in.wait_recv()
    shift_rows(xs, 3 - 2 * c, 2)

    @pl.when(z > 0)
    def _():
        top_in.wait_recv()
        top_swap.start()

    @pl.when(z < 3)
    def _():
        bottom_in.wait_recv()
        bottom_swap.start()

    crossed[0].wait_recv()
    pass_on(0)

    for copy in own_ct:
        copy.wait()
    for copy in ct_pair:
        copy.wait_recv()

    @pl.loop(0, 4)
    def _(r):
        for lane in range(2):
            wide[lane] = ctv[r, :, 128 * lane : 128 * lane + 128].astype(jnp.float32)
        for v in range(2):
            for lane in range(2):
                cts[v, r, :, 128 * lane : 128 * lane + 128] = wide[lane, pl.ds(v, WIDTH, 2), :].astype(jnp.bfloat16)

    crossed[1].wait_recv()
    pass_on(1)

    @pl.when(z > 0)
    def _():
        top_swapped.wait_recv()

    @pl.when(z < 3)
    def _():
        bottom_swapped.wait_recv()

    shift_rows(xs, 0, 1)
    shift_rows(xs, 5, 1)

    def forward_row(v, r):
        lhs = jnp.concatenate(
            [
                xs[(kk // 2) % 3, r + kk // 6, :, 256 * (kk % 2) : 256 * (kk % 2) + 256]
                for kk in range(CHUNKS)
            ],
            axis=1,
        )
        rhs = jnp.concatenate(
            [
                wall[kk // 3, v, :, :, :, :, :, 256 * (kk % 3) : 256 * (kk % 3) + 256].reshape(256, 256)
                for kk in range(CHUNKS)
            ],
            axis=1,
        )
        acc[:, :256] = lax.dot_general(
            lhs, rhs, (((1,), (1,)), ((), ())), preferred_element_type=jnp.float32
        )

        @pl.loop(0, WIDTH // 32)
        def _(j):
            rows = pl.ds(pl.multiple_of(j * 32, 32), 32)
            value = acc[rows, :256]
            grown = 0.5 * (1.0 + lax.erf(value * inv_root_two))
            slope = grown + value * jnp.exp(-0.5 * value * value) * inv_root_tau
            actv[v, r, rows] = (value * grown).astype(jnp.bfloat16)
            out = pl.ds(pl.multiple_of(256 * v, 256), 256)
            ss[1, r + 1, rows, out] = (cts[v, r, rows].astype(jnp.float32) * slope).astype(jnp.bfloat16)

    def at(part, fixed):
        return (part,) + tuple(fixed.get(d, slice(None)) for d in range(1, 6))

    def when(condition, body):
        if condition is None:
            body()
        else:
            pl.when(condition)(body)

    passive = c != xa
    two_y = {"fsdp": x * 2 + 1 - h}
    two_z = {"tile": (z + 2) % 4 * 2 + c}

    halves, seconds, thirds, fourths = {}, {}, {}, {}
    for part, (one, two) in enumerate(FIRST):
        kept = {} if one == 0 else {one: mine[one]}
        sends = passive if one == 0 else None
        for n, pair in enumerate((near, far)):
            if one == 1 and n == 0:
                continue
            there = {1: pair} if one < 2 else {1: pair, one: 1 - mine[one]}
            here = {1: near} if one == 1 else ({1: pair} if one == 0 else {1: pair, one: mine[one]})
            halves[part, n] = (
                sends,
                remote(
                    gwb.at[at(part, there)], got0.at[at(part, there)],
                    r_send.at[part, n], r_recv.at[part, n], partner[one],
                ),
                active if one == 0 else None,
                at(part, here),
            )
        there = dict(kept) if two == 0 else {**kept, two: 1 - mine[two]}
        kept = dict(kept) if two == 0 else {**kept, two: mine[two]}
        seconds[part] = (
            passive if two == 0 else (active if one == 0 else None),
            remote(
                gwb.at[at(part, there)], got1.at[at(part, there)],
                r_send.at[part, 2], r_recv.at[part, 2], partner[two],
            ),
            active if 0 in (one, two) else None,
            at(part, kept),
        )
        done_x = 0 in (one, two)
        for step, table in ((1, thirds), (2, fourths)):
            axis = (part // 2 + step) % 3
            slots = got2 if step == 1 else got3
            sem = 3 * step
            copies = []
            if axis == 0:
                for j, (cond, pair, device) in enumerate(
                    ((active, far, partner[1]), (passive, near, partner[0]), (passive, far, two_away))
                ):
                    copies.append((cond, {**kept, 1: pair}, device))
                kept = {**kept, 1: near}
                done_x = True
                receives = active
            else:
                da, db = 2 * axis, 2 * axis + 1
                cond = active if done_x else None
                for flip_a, flip_b, device in (
                    (1, 0, partner[da]), (0, 1, partner[db]), (1, 1, two_y if axis == 1 else two_z)
                ):
                    there = {
                        **kept,
                        da: 1 - mine[da] if flip_a else mine[da],
                        db: 1 - mine[db] if flip_b else mine[db],
                    }
                    copies.append((cond, there, device))
                kept = {**kept, da: mine[da], db: mine[db]}
                receives = cond
            rest = 5 - len(kept)
            entry = []
            for j, (cond, there, device) in enumerate(copies):
                slot = (part, j) if step == 2 or rest == 2 else (part, j, 0)
                entry.append(
                    (
                        cond,
                        remote(
                            gwb.at[at(part, there)], slots.at[slot],
                            r_send.at[part, sem + j], r_recv.at[part, sem + j], device,
                        ),
                        slot,
                    )
                )
            table[part] = (entry, receives, at(part, kept))

    def add_half(part):
        for n in range(2):
            if (part, n) in halves:
                _, copy, receives, here = halves[part, n]

                def add(copy=copy, here=here):
                    copy.wait_recv()
                    total = gwb[here].astype(jnp.float32) + got0[here].astype(jnp.float32)
                    gwb[here] = total.astype(jnp.bfloat16)

                when(receives, add)
        when(seconds[part][0], seconds[part][1].start)

    def start_all(entry):
        for cond, copy, _ in entry:
            when(cond, copy.start)

    def add_second(part):
        _, copy, receives, here = seconds[part]

        def add():
            copy.wait_recv()
            total = gwb[here].astype(jnp.float32) + got1[here].astype(jnp.float32)
            gwb[here] = total.astype(jnp.bfloat16)

        when(receives, add)
        start_all(thirds[part][0])

    def add_third(part):
        entry, receives, here = thirds[part]

        def add():
            total = gwb[here].astype(jnp.float32)
            for _, copy, slot in entry:
                copy.wait_recv()
                total = total + got2[slot].astype(jnp.float32)
            gwb[here] = total.astype(jnp.bfloat16)

        when(receives, add)
        start_all(fourths[part][0])

    def add_fourth(part):
        entry, _, here = fourths[part]

        def add():
            total = gwb[here].astype(jnp.float32)
            for _, copy, slot in entry:
                copy.wait_recv()
                total = total + got3[slot].astype(jnp.float32)
            fin[ye, za, ze, :, PCOLS * part : PCOLS * part + PCOLS] = total.astype(jnp.bfloat16)

        pl.when(active)(add)

    def weight_gradient(pair, order):
        lanes = pl.ds(pl.multiple_of(256 * pair, 256), 256)
        for r in range(4):
            st[:, WIDTH * r : WIDTH * r + WIDTH] = ss[1, r + 1, :, lanes].T
        for part in order:
            for j in range(3):
                kk = 3 * part + j
                window = xs[(kk // 2) % 3, kk // 6 : kk // 6 + 4, :, 256 * (kk % 2) : 256 * (kk % 2) + 256]
                term = jnp.dot(
                    st[...], window.reshape(4 * WIDTH, 256), preferred_element_type=jnp.float32
                )
                gwb[part, pair, :, :, :, :, :, 256 * j : 256 * j + 256] = term.astype(jnp.bfloat16).reshape(
                    2, 2, 2, 2, 16, 256
                )
            n = 0 if pair is near else 1
            if (part, n) in halves:
                when(halves[part, n][0], halves[part, n][1].start)

    passed_in(0)

    @pl.when(c != xa)
    def _():
        for k in range(1, 4):
            from_turn[k].wait_recv()

    @pl.loop(0, 4)
    def _(r):
        forward_row(near, r)

    weight_gradient(near, NEAR_ORDER)

    passed_in(1)

    @pl.when(c != xa)
    def _():
        passed_in(2)

    @pl.when(active)
    def _():
        for k in range(1, 4):
            from_flip[k].wait_recv()

    @pl.loop(0, 2)
    def _(k):
        forward_row(far, 3 * k)

    slope_up = remote(ss.at[1, 1], ss.at[1, 5], s_send.at[0], s_recv.at[0], {"tile": 2 * jnp.maximum(z - 1, 0) + c})
    slope_down = remote(ss.at[1, 4], ss.at[1, 0], s_send.at[1], s_recv.at[1], {"tile": 2 * jnp.minimum(z + 1, 3) + c})
    pl.when(z > 0)(slope_up.start)
    pl.when(z < 3)(slope_down.start)

    @pl.loop(0, 2)
    def _(k):
        forward_row(far, 2 - k)

    weight_gradient(far, FAR_ORDER)

    pl.when(z > 0)(lambda: remote(ss.at[1, 0], ss.at[1, 0], s_send.at[1], s_recv.at[1], other_core).wait_recv())
    pl.when(z < 3)(lambda: remote(ss.at[1, 5], ss.at[1, 5], s_send.at[0], s_recv.at[0], other_core).wait_recv())
    shift_rows(ss, 0, 6)

    def input_row(r, out):
        lhs = jnp.concatenate([ss[2 - tap % 3, r + 2 - tap // 3] for tap in range(9)], axis=1)
        for e in range(2):
            chunks = []
            for tap in range(9):
                kk = 2 * tap + e
                chunks.append(
                    wall[kk // 3, :, :, :, :, :, :, 256 * (kk % 3) : 256 * (kk % 3) + 256].reshape(512, 256)
                )
            out[:, 256 * e : 256 * e + 256] = jnp.dot(
                lhs, jnp.concatenate(chunks, axis=0), preferred_element_type=jnp.float32
            )

    @pl.loop(0, 2)
    def _(k):
        input_row(2 * (1 - c) + k, igp.at[k])

    ig_pair = remote(igp, igr, i_send.at[0], i_recv.at[0], other_core)
    ig_pair.start()
    for part in FAR_ORDER:
        add_half(part)

    trow[4:8, :] = id_row[4:8, :]
    trow[0:4, :] = jnp.zeros((4, 128), jnp.float32)

    @pl.loop(0, 2)
    def _(k):
        input_row(2 * c + k, acc)

        @pl.when(k == 0)
        def _():
            ig_pair.wait_recv()

        total = acc[...] + igr[k]
        gfb[k] = total.astype(jnp.bfloat16)
        column_sum = jnp.sum(total, axis=0, keepdims=True)
        for lane in range(4):
            trow[lane : lane + 1, :] += column_sum[:, 128 * lane : 128 * lane + 128]

    gf_copy = pltpu.make_async_copy(gfb, gf_out, loc_sem.at[11])
    gf_copy.start()

    t_copies = []
    for k in range(1, 8):
        copy = remote(trow, tpeer.at[k - 1], t_send.at[k - 1], t_recv.at[k - 1], {"tile": (t + k) % 8})
        copy.start()
        t_copies.append(copy)

    for part in FAR_ORDER:
        add_second(part)

    for copy in t_copies:
        copy.wait_recv()
    for copy in t_copies:
        copy.wait_send()
    total = trow[0:4, :]
    for k in range(7):
        total = total + tpeer[k, 0:4, :]
    tall[0, 0:4, :] = total
    tall[0, 4:8, :] = trow[4:8, :]
    v_copies = []
    for k in range(1, 16):
        to = (frame + k) % 16
        copy = remote(
            tall.at[0], tall.at[k], v_send.at[k - 1], v_recv.at[k - 1], {"fsdp": to // 2, "dp": to % 2}
        )
        copy.start()
        v_copies.append(copy)

    @pl.loop(0, 4)
    def _(r):
        for lane in range(2):
            lanes = pl.ds(128 * lane, 128)
            for v in range(2):
                wide[lane, pl.ds(v, WIDTH, 2), :] = actv[v, r, :, lanes].astype(jnp.float32)
            upb[r, :, lanes] = wide[lane].astype(jnp.bfloat16)

    up_own, up_pair = [], []
    for k in range(2):
        up_own.append(pltpu.make_async_copy(upb.at[2 * c + k], up_out.at[2 * k + c], loc_sem.at[9 + k]))
        up_pair.append(
            remote(upb.at[2 * (1 - c) + k], up_out.at[2 * k + c], u_send.at[k], u_recv.at[k], other_core)
        )
        up_own[-1].start()
        up_pair[-1].start()

    for part in FAR_ORDER:
        add_third(part)

    spreads, to_pair, to_self = [], [], []
    for g in range(2):
        cols = pl.ds(3 * PCOLS * g, 3 * PCOLS)
        piece_at = fin.at[ye, za, ze, :, cols]
        spreads.append(
            [remote(piece_at, piece_at, f_send.at[g, k], f_recv.at[g, k], holders[k]) for k in range(7)]
        )
        half_at, half_out = fin.at[:, :, :, :, cols], gw_out.at[:, :, :, :, cols]
        to_pair.append(remote(half_at, half_out, i_send.at[1 + g], i_recv.at[1 + g], other_core))
        to_self.append(pltpu.make_async_copy(half_at, half_out, loc_sem.at[12 + g]))

    for g in range(2):
        for part in range(3 * g, 3 * g + 3):
            add_fourth(part)

        @pl.when(active)
        def _(g=g):
            for copy in spreads[g]:
                copy.start()

    @pl.when(active)
    def _():
        for g in range(2):
            for copy in spreads[g]:
                copy.wait_recv()
            to_pair[g].start()
            to_self[g].start()
        for g in range(2):
            for copy in spreads[g]:
                copy.wait_send()
            to_self[g].wait()
            to_pair[g].wait_send()

    @pl.when(c != xa)
    def _():
        for g in range(2):
            to_pair[g].wait_recv()

    for copy in v_copies:
        copy.wait()
    tab_copy = pltpu.make_async_copy(tall, tab_out, loc_sem.at[15])
    tab_copy.start()

    @pl.when(active)
    def _():
        for copy in to_turn[1:] + to_flip[1:] + [to_far]:
            copy.wait_send()

    @pl.when(c != xa)
    def _():
        for j in range(3):
            passed[2, j][0].wait_send()

    for k in range(2):
        across[k].wait_send()
        for j in range(3):
            passed[k, j][0].wait_send()

    @pl.when(z > 0)
    def _():
        top_swap.wait_send()

    @pl.when(z < 3)
    def _():
        bottom_swap.wait_send()

    for sends, copy, _, _ in list(halves.values()) + list(seconds.values()):
        when(sends, copy.wait_send)
    for entry, _, _ in list(thirds.values()) + list(fourths.values()):
        for sends, copy, _ in entry:
            when(sends, copy.wait_send)
    x_pair.wait_send()

    @pl.when(sends_rim)
    def _():
        for copy in rim_out:
            copy.wait_send()

    for copy in ct_pair:
        copy.wait_send()
    pl.when(z > 0)(slope_up.wait_send)
    pl.when(z < 3)(slope_down.wait_send)
    for k in range(2):
        up_own[k].wait()
        up_pair[k].wait()
    ig_pair.wait_send()
    gf_copy.wait()
    tab_copy.wait()


def fused(features, weight, cot, shift_row, id_row):
    any_space = pl.BlockSpec(memory_space=pl.ANY)
    vmem = pl.BlockSpec(memory_space=pltpu.VMEM)
    bf16, f32 = jnp.bfloat16, jnp.float32
    dma = pltpu.SemaphoreType.DMA
    return pl.pallas_call(
        kernel,
        out_shape=(
            jax.ShapeDtypeStruct((4, 2 * WIDTH, 256), bf16),
            jax.ShapeDtypeStruct((2, 2, 2, 16, 9 * CIN), bf16),
            jax.ShapeDtypeStruct((2, WIDTH, CIN), bf16),
            jax.ShapeDtypeStruct((16, 8, 128), f32),
        ),
        in_specs=[any_space, any_space, any_space, vmem, vmem],
        out_specs=[any_space] * 4,
        scratch_shapes=[
            pltpu.VMEM((3, 6, WIDTH, CIN), bf16),
            pltpu.VMEM((3, 6, WIDTH, HALF), bf16),
            pltpu.VMEM((256, 4 * WIDTH), bf16),
            pltpu.VMEM((PARTS, 2, 2, 2, 2, 2, 16, PCOLS), bf16),
            pltpu.VMEM((PARTS, 2, 2, 2, 2, 2, 16, PCOLS), bf16),
            pltpu.VMEM((PARTS, 2, 2, 2, 2, 2, 16, PCOLS), bf16),
            pltpu.VMEM((PARTS, 2, 2, 2, 2, 2, 16, PCOLS), bf16),
            pltpu.VMEM((PARTS, 3, 2, 2, 16, PCOLS), bf16),
            pltpu.VMEM((PARTS, 3, 16, PCOLS), bf16),
            pltpu.VMEM((2, 2, 2, 16, 9 * CIN), bf16),
            pltpu.VMEM((4, 2 * WIDTH, 256), bf16),
            pltpu.VMEM((2, 4, WIDTH, 256), bf16),
            pltpu.VMEM((2, 4, WIDTH, 256), bf16),
            pltpu.VMEM((4, 2 * WIDTH, 256), bf16),
            pltpu.VMEM((2, 2 * WIDTH, 128), f32),
            pltpu.VMEM((WIDTH, 512), f32),
            pltpu.VMEM((2, WIDTH, CIN), f32),
            pltpu.VMEM((2, WIDTH, CIN), f32),
            pltpu.VMEM((2, WIDTH, CIN), bf16),
            pltpu.VMEM((8, 128), f32),
            pltpu.VMEM((7, 8, 128), f32),
            pltpu.VMEM((16, 8, 128), f32),
            dma((16,)),
            dma((7,)),
            dma((7,)),
            dma((9,)),
            dma((9,)),
            dma((2,)),
            dma((2,)),
            dma((3, 3)),
            dma((3, 3)),
            dma((2,)),
            dma((2,)),
            dma((PARTS, 9)),
            dma((PARTS, 9)),
            dma((2, 7)),
            dma((2, 7)),
            dma((2,)),
            dma((2,)),
            dma((3,)),
            dma((3,)),
            dma((7,)),
            dma((7,)),
            dma((15,)),
            dma((15,)),
        ],
        compiler_params=pltpu.CompilerParams(
            collective_id=0, has_side_effects=True, vmem_limit_bytes=60 * 2**20
        ),
        cost_estimate=pl.CostEstimate(
            flops=6 * 768 * 4608 * 1024, bytes_accessed=2 * 10**7, transcendentals=3 * 768 * 1024
        ),
        name="conv_block",
    )(features, weight, cot, shift_row, id_row)


def shards(features, frame_table, frame_ids, conv_weight, cotangent):
    video_len = frame_table.shape[0]
    shift = lax.dynamic_slice_in_dim(frame_table, frame_ids[0], 1, axis=0).astype(jnp.float32)
    id_row = jnp.broadcast_to(frame_ids.astype(jnp.float32)[:, None], (8, 128))
    up, gw, gf, tab = fused(
        features[0], conv_weight.reshape(2, 2, 2, 16, 9 * CIN), cotangent[0], shift, id_row
    )
    sums = tab[:, :4].reshape(16, CIN)
    frames = tab[:, 4, 0]
    picker = (frames[:, None] == jnp.arange(video_len, dtype=jnp.float32)[None, :]).astype(jnp.float32)
    grad_table = lax.dot_general(
        picker, sums, (((0,), (0,)), ((), ())),
        precision=lax.Precision.HIGHEST, preferred_element_type=jnp.float32,
    )
    grad_weight = gw.reshape(128, 9 * CIN).astype(jnp.float32)
    return (up[None], grad_weight, gf[None], grad_table)


def solution(mesh):
    return jax.shard_map(
        shards,
        mesh=mesh,
        in_specs=(
            P(("fsdp", "dp"), "tile", None, None),
            P(),
            P(("fsdp", "dp")),
            P("fsdp", None),
            P(("fsdp", "dp"), "tile", None, None),
        ),
        out_specs=(
            P(("fsdp", "dp"), "tile", None, None),
            P("fsdp", None),
            P(("fsdp", "dp"), "tile", None, None),
            P(),
        ),
        check_vma=False,
    )
```

```python
import jax
import jax.numpy as jnp
from jax import lax
from jax.experimental import pallas as pl
from jax.experimental.pallas import tpu as pltpu
from jax.sharding import PartitionSpec as P

inv_root_two = 0.7071067811865476
inv_root_tau = 0.3989422804014327

WIDTH = 384
CIN = 512
HALF = 512
PARTS = 6
PCOLS = 768
CHUNKS = 18

DIMS = 6

FIRST = [(0, 1), (1, 0), (2, 3), (3, 2), (4, 5), (5, 4)]
NEAR_ORDER = (0, 2, 3, 4, 5, 1)
FAR_ORDER = (1, 0, 2, 3, 4, 5)

MESH = pl.DeviceIdType.MESH


def kernel(
    feat, weight, cot, shift_row, id_row,
    up_out, gw_out, gf_out, tab_out,
    xs, ss, st, wall, gwb, got0, got1, got2, got3, fin, ctv, cts, actv, upb, wide, acc, igp, igr, gfb,
    trow, tpeer, tall,
    loc_sem, x_send, x_recv, o_send, o_recv, n_send, n_recv, q_send, q_recv, s_send, s_recv,
    r_send, r_recv, f_send, f_recv, u_send, u_recv, i_send, i_recv, t_send, t_recv, v_send, v_recv,
):
    f = lax.axis_index("fsdp")
    t = lax.axis_index("tile")
    lo = lax.axis_index("dp")
    x, h = f // 2, f % 2
    z, c = t // 2, t % 2
    xa, xb = x // 2, x % 2
    xe = (xa + xb) % 2
    ye = (h + lo) % 2
    za = z // 2
    ze = (za + z % 2) % 2
    keep = (c + xe) % 2
    active, passive = c == xa, c != xa
    mine = {1: keep, 2: h, 3: ye, 4: za, 5: ze}
    x_flip = x + 1 - 2 * xb
    z_flip = z + 1 - 2 * (z % 2)
    partner = {
        0: {"fsdp": (3 - x) * 2 + h},
        1: {"fsdp": x_flip * 2 + h},
        2: {"fsdp": x * 2 + 1 - h, "dp": 1 - lo},
        3: {"dp": 1 - lo},
        4: {"tile": (3 - z) * 2 + c},
        5: {"tile": z_flip * 2 + c},
    }
    other_core = {"tile": 2 * z + 1 - c}
    two_away = {"fsdp": (x + 2) % 4 * 2 + h}
    quarter = (z + 2 * ye) % 4
    holders = [
        {"tile": (z + k // 2) % 4 * 2 + c, "dp": (lo + k % 2) % 2} for k in range(1, 8)
    ]

    def remote(src, dst, send_sem, recv_sem, device):
        return pltpu.make_async_remote_copy(
            src_ref=src, dst_ref=dst, send_sem=send_sem, recv_sem=recv_sem,
            device_id=device, device_id_type=MESH,
        )

    barrier = pltpu.get_barrier_semaphore()
    for k in range(1, 8):
        pl.semaphore_signal(barrier, inc=1, device_id={"tile": (t + k) % 8}, device_id_type=MESH)
    frame = f * 2 + lo
    for k in range(1, 16):
        to = (frame + k) % 16
        pl.semaphore_signal(
            barrier, inc=1, device_id={"fsdp": to // 2, "dp": to % 2}, device_id_type=MESH
        )

    for k in (3, 5, 7):
        pl.semaphore_signal(barrier, inc=1, device_id=holders[k - 1], device_id_type=MESH)

    near, far = keep, 1 - keep
    own_x = pltpu.make_async_copy(feat, xs.at[1, pl.ds(1 + 2 * c, 2)], loc_sem.at[0])
    own_x.start()
    own_w = [
        pltpu.make_async_copy(
            weight.at[:, :, :, :, pl.ds(PCOLS * part, PCOLS)], wall.at[part, near, h], loc_sem.at[1 + part]
        )
        for part in range(PARTS)
    ]

    @pl.when(active)
    def _():
        for copy in own_w:
            copy.start()

    own_ct = []
    for k in range(2):
        own_ct.append(
            pltpu.make_async_copy(cot.at[2 * k + c], ctv.at[2 * c + k], loc_sem.at[7 + k])
        )
        own_ct[-1].start()

    own_x.wait()
    for k in range(2):
        for lane in range(4):
            at = pl.ds(128 * lane, 128)
            row = xs[1, 1 + 2 * c + k, :, at].astype(jnp.float32) + shift_row[:, at]
            xs[1, 1 + 2 * c + k, :, at] = row.astype(jnp.bfloat16)

    pl.semaphore_wait(barrier, 25)

    def same(pair, half, number, send_sem, recv_sem, device, eighth=None):
        place = wall.at[:, pair, half, number // 2, number % 2]
        if eighth is not None:
            place = wall.at[:, pair, half, number // 2, number % 2, eighth]
        return remote(place, place, send_sem, recv_sem, device)

    turn = [(quarter + k) % 4 for k in range(4)]
    to_flip = [same(near, h, turn[k], o_send.at[k], o_recv.at[k], partner[1]) for k in range(4)]
    to_turn = [same(near, h, turn[k], o_send.at[4 + k], o_recv.at[4 + k], partner[0]) for k in range(1, 4)]
    to_far = same(near, h, quarter, o_send.at[8], o_recv.at[8], two_away)
    first_turn = [same(near, h, quarter, o_send.at[9 + e], o_recv.at[9 + e], partner[0], e) for e in range(2)]
    from_flip = [same(far, h, turn[k], o_send.at[k], o_recv.at[k], partner[1]) for k in range(4)]
    from_far = same(far, h, quarter, o_send.at[8], o_recv.at[8], two_away)
    across = [same(near, h, quarter, n_send.at[e], n_recv.at[e], partner[2], e) for e in range(2)]
    crossed = [same(near, 1 - h, quarter, n_send.at[e], n_recv.at[e], partner[2], e) for e in range(2)]
    across_far = same(far, h, quarter, n_send.at[2], n_recv.at[2], partner[2])
    crossed_far = same(far, 1 - h, quarter, n_send.at[2], n_recv.at[2], partner[2])
    passed = {}
    theirs = {3: (quarter + 2) % 4, 4: (3 - z + 2 * ye) % 4, 5: (z_flip + 2 * ye) % 4}
    for k, (pair, half, e) in enumerate(((near, 1 - h, 0), (near, 1 - h, 1), (far, 1 - h, None), (far, h, None))):
        for j, dim in enumerate((3, 4, 5)):
            passed[k, j] = (
                same(pair, half, quarter, q_send.at[k, j], q_recv.at[k, j], partner[dim], e),
                same(pair, half, theirs[dim], q_send.at[k, j], q_recv.at[k, j], partner[dim], e),
            )

    def pass_on(k):
        for j in range(3):
            passed[k, j][0].start()

    def passed_in(k):
        for j in range(3):
            passed[k, j][1].wait_recv()

    @pl.when(active)
    def _():
        for copy in own_w:
            copy.wait()
        for e in range(2):
            first_turn[e].start()
            across[e].start()
        to_flip[0].start()

    x_pair = remote(
        xs.at[1, pl.ds(1 + 2 * c, 2)], xs.at[1, pl.ds(1 + 2 * c, 2)], x_send.at[0], x_recv.at[0], other_core
    )
    x_pair_in = remote(
        xs.at[1, pl.ds(3 - 2 * c, 2)], xs.at[1, pl.ds(3 - 2 * c, 2)], x_send.at[0], x_recv.at[0], other_core
    )
    rim_cols = WIDTH // 2
    sends_rim = jnp.where(c == 0, z > 0, z < 3)
    z_rim = jnp.where(c == 0, jnp.maximum(z - 1, 0), jnp.minimum(z + 1, 3))
    rim_out = [
        remote(
            xs.at[1, 1 + 3 * c, pl.ds(rim_cols * k, rim_cols)],
            xs.at[1, 5 - 5 * c, pl.ds(rim_cols * k, rim_cols)],
            x_send.at[1 + k], x_recv.at[1 + c], {"tile": 2 * z_rim + k},
        )
        for k in range(2)
    ]

    def rim_part(row, core, sem):
        at = xs.at[1, row, pl.ds(pl.multiple_of(rim_cols * core, rim_cols), rim_cols)]
        return remote(at, at, x_send.at[sem], x_recv.at[sem], other_core)

    top_in, bottom_in = rim_part(0, c, 2), rim_part(5, c, 1)
    top_swap, bottom_swap = rim_part(0, c, 5), rim_part(5, c, 6)
    top_swapped, bottom_swapped = rim_part(0, 1 - c, 5), rim_part(5, 1 - c, 6)

    @pl.when(sends_rim)
    def _():
        for copy in rim_out:
            copy.start()

    x_pair.start()

    ct_pair = []
    for k in range(2):
        ct_pair.append(
            remote(cot.at[2 * k + 1 - c], ctv.at[2 * c + k], x_send.at[3 + k], x_recv.at[3 + k], other_core)
        )
        ct_pair[-1].start()

    @pl.when(z == 0)
    def _():
        xs[1, 0] = jnp.zeros((WIDTH, CIN), jnp.bfloat16)
        ss[1, 0] = jnp.zeros((WIDTH, HALF), jnp.bfloat16)

    @pl.when(z == 3)
    def _():
        xs[1, 5] = jnp.zeros((WIDTH, CIN), jnp.bfloat16)
        ss[1, 5] = jnp.zeros((WIDTH, HALF), jnp.bfloat16)

    column = lax.broadcasted_iota(jnp.int32, (WIDTH, 128), 0)

    def shift_row(ref, row):
        for lane in range(4):
            at = pl.ds(128 * lane, 128)
            values = ref[1, row, :, at].astype(jnp.float32)
            right = jnp.where(column == 0, 0.0, pltpu.roll(values, 1, 0))
            left = jnp.where(column == WIDTH - 1, 0.0, pltpu.roll(values, WIDTH - 1, 0))
            ref[0, row, :, at] = right.astype(jnp.bfloat16)
            ref[2, row, :, at] = left.astype(jnp.bfloat16)

    def shift_rows(ref, first, count):
        @pl.loop(0, count)
        def _(k):
            shift_row(ref, first + k)

    @pl.when(active)
    def _():
        for e in range(2):
            first_turn[e].wait_send()
        to_turn[0].start()
        to_flip[1].start()

    shift_rows(xs, 1 + 2 * c, 2)

    @pl.when(active)
    def _():
        for e in range(2):
            crossed[e].wait_recv()
            pass_on(e)
        to_far.start()
        for k in range(1, 3):
            to_turn[k].start()
            to_flip[k + 1].start()

    @pl.when(passive)
    def _():
        for e in range(2):
            first_turn[e].wait_recv()
            across[e].start()

    x_pair_in.wait_recv()
    shift_rows(xs, 3 - 2 * c, 2)

    @pl.when(z > 0)
    def _():
        top_in.wait_recv()
        top_swap.start()

    @pl.when(z < 3)
    def _():
        bottom_in.wait_recv()
        bottom_swap.start()

    @pl.when(passive)
    def _():
        for e in range(2):
            crossed[e].wait_recv()
            pass_on(e)

    for copy in own_ct:
        copy.wait()
    for copy in ct_pair:
        copy.wait_recv()

    @pl.loop(0, 4)
    def _(r):
        for lane in range(2):
            wide[lane] = ctv[r, :, 128 * lane : 128 * lane + 128].astype(jnp.float32)
        for v in range(2):
            for lane in range(2):
                cts[v, r, :, 128 * lane : 128 * lane + 128] = wide[lane, pl.ds(v, WIDTH, 2), :].astype(jnp.bfloat16)

    @pl.when(z > 0)
    def _():
        top_swapped.wait_recv()

    @pl.when(z < 3)
    def _():
        bottom_swapped.wait_recv()

    shift_rows(xs, 0, 1)
    shift_rows(xs, 5, 1)

    @pl.when(active)
    def _():
        from_flip[0].wait_recv()
        across_far.start()

    @pl.when(passive)
    def _():
        from_far.wait_recv()
        across_far.start()
        pass_on(3)

    def forward_row(v, r):
        lhs = jnp.concatenate(
            [
                xs[(kk // 2) % 3, r + kk // 6, :, 256 * (kk % 2) : 256 * (kk % 2) + 256]
                for kk in range(CHUNKS)
            ],
            axis=1,
        )
        rhs = jnp.concatenate(
            [
                wall[kk // 3, v, :, :, :, :, :, 256 * (kk % 3) : 256 * (kk % 3) + 256].reshape(256, 256)
                for kk in range(CHUNKS)
            ],
            axis=1,
        )
        acc[:, :256] = lax.dot_general(
            lhs, rhs, (((1,), (1,)), ((), ())), preferred_element_type=jnp.float32
        )

        @pl.loop(0, WIDTH // 32)
        def _(j):
            rows = pl.ds(pl.multiple_of(j * 32, 32), 32)
            value = acc[rows, :256]
            grown = 0.5 * (1.0 + lax.erf(value * inv_root_two))
            slope = grown + value * jnp.exp(-0.5 * value * value) * inv_root_tau
            actv[v, r, rows] = (value * grown).astype(jnp.bfloat16)
            out = pl.ds(pl.multiple_of(256 * v, 256), 256)
            ss[1, r + 1, rows, out] = (cts[v, r, rows].astype(jnp.float32) * slope).astype(jnp.bfloat16)

    def at(part, fixed):
        return (part,) + tuple(fixed.get(d, slice(None)) for d in range(1, 6))

    def when(condition, body):
        if condition is None:
            body()
        else:
            pl.when(condition)(body)

    two_y = {"fsdp": x * 2 + 1 - h}
    two_z = {"tile": (z + 2) % 4 * 2 + c}

    halves, seconds, thirds, fourths = {}, {}, {}, {}

    def half_copies(part, n, dim, there, sends):
        place = at(part, there)
        return [
            (
                sends,
                remote(
                    gwb.at[place + (slice(None), pl.ds(256 * j, 256))],
                    got0.at[place + (slice(None), pl.ds(256 * j, 256))],
                    r_send.at[part, 3 * n + j], r_recv.at[part, 3 * n + j], partner[dim],
                ),
            )
            for j in range(3)
        ]

    def second_copy(part, n, dim, there, sends):
        place = at(part, there)
        return (
            sends,
            remote(
                gwb.at[place], got1.at[place], r_send.at[part, 6 + n], r_recv.at[part, 6 + n], partner[dim]
            ),
        )

    def slot_copy(part, there, slots, slot, sem, device, sends):
        return (
            sends,
            remote(
                gwb.at[at(part, there)], slots.at[slot], r_send.at[part, sem], r_recv.at[part, sem], device
            ),
            slot,
        )

    def flips(axis):
        da, db = 2 * axis, 2 * axis + 1
        there = {da: 1 - mine[da], db: 1 - mine[db]}
        return (
            ({da: there[da], db: mine[db]}, partner[da]),
            ({da: mine[da], db: there[db]}, partner[db]),
            (there, two_y if axis == 1 else two_z),
        )

    def along_x(part, kept, slots, sem):
        return [
            slot_copy(part, {**kept, 1: pair}, slots, (part, j), sem + j, device, sends)
            for j, (sends, pair, device) in enumerate(
                ((passive, near, partner[0]), (active, far, partner[1]), (passive, far, two_away))
            )
        ]

    for n, pair in enumerate((near, far)):
        halves[0, n] = (half_copies(0, n, 0, {1: pair}, passive), active, at(0, {1: pair}))
    halves[1, 1] = (half_copies(1, 1, 1, {1: far}, None), None, at(1, {1: near}))
    seconds[0, 1] = (second_copy(0, 1, 1, {1: far}, active), active, at(0, {1: near}))
    seconds[1, 1] = (second_copy(1, 1, 0, {1: near}, passive), active, at(1, {1: near}))
    for part in (0, 1):
        thirds[part, 1] = (
            [
                slot_copy(part, {1: near, **there}, got2, (part, j), 11 + j, device, active)
                for j, (there, device) in enumerate(flips(1))
            ],
            active, at(part, {1: near, 2: h, 3: ye}),
        )
        fourths[part] = [
            slot_copy(part, {1: near, 2: h, 3: ye, **there}, got3, (part, j), 14 + j, device, active)
            for j, (there, device) in enumerate(flips(2))
        ]
    for part in range(2, 6):
        one, two = FIRST[part]
        first = {one: mine[one]}
        both = {**first, two: mine[two]}
        for n, pair in enumerate((near, far)):
            halves[part, n] = (
                half_copies(part, n, one, {1: pair, one: 1 - mine[one]}, None),
                None, at(part, {1: pair, **first}),
            )
            seconds[part, n] = (
                second_copy(part, n, two, {1: pair, **first, two: 1 - mine[two]}, None),
                None, at(part, {1: pair, **both}),
            )
            if part < 4:
                thirds[part, n] = (
                    [
                        slot_copy(
                            part, {1: pair, **both, **there}, got2, (part, j, 0, pair), 8 + 3 * n + j, device, None
                        )
                        for j, (there, device) in enumerate(flips(2))
                    ],
                    None, at(part, {1: pair, **both, 4: za, 5: ze}),
                )
        if part < 4:
            fourths[part] = along_x(part, {**both, 4: za, 5: ze}, got3, 14)
        else:
            copies = along_x(part, both, got2, 8)
            thirds[part, 0] = ([copies[0]], None, None)
            thirds[part, 1] = (copies, active, at(part, {**both, 1: near}))
            fourths[part] = [
                slot_copy(part, {1: near, **both, **there}, got3, (part, j), 14 + j, device, active)
                for j, (there, device) in enumerate(flips(1))
            ]

    def add_half(part, n):
        if (part, n) in halves:
            copies, receives, here = halves[part, n]

            def add():
                for _, copy in copies:
                    copy.wait_recv()
                total = gwb[here].astype(jnp.float32) + got0[here].astype(jnp.float32)
                gwb[here] = total.astype(jnp.bfloat16)

            when(receives, add)
        if (part, n) in seconds:
            when(seconds[part, n][0][0], seconds[part, n][0][1].start)

    def add_second(part, n):
        if (part, n) not in seconds:
            return
        (_, copy), receives, here = seconds[part, n]

        def add():
            copy.wait_recv()
            total = gwb[here].astype(jnp.float32) + got1[here].astype(jnp.float32)
            gwb[here] = total.astype(jnp.bfloat16)

        when(receives, add)
        entry = thirds[part, n][0]
        for sends, copy, _ in entry[1:] if part >= 4 and n == 1 else entry:
            when(sends, copy.start)

    def add_third(part):
        for n in range(2):
            if (part, n) in thirds and thirds[part, n][2] is not None:
                entry, receives, here = thirds[part, n]

                def add(entry=entry, here=here):
                    total = gwb[here].astype(jnp.float32)
                    for _, copy, slot in entry:
                        copy.wait_recv()
                        total = total + got2[slot].astype(jnp.float32)
                    gwb[here] = total.astype(jnp.bfloat16)

                when(receives, add)
        for sends, copy, _ in fourths[part]:
            when(sends, copy.start)

    def add_fourth(part):
        here = at(part, {1: near, 2: h, 3: ye, 4: za, 5: ze})

        def add():
            total = gwb[here].astype(jnp.float32)
            for _, copy, slot in fourths[part]:
                copy.wait_recv()
                total = total + got3[slot].astype(jnp.float32)
            total = total.astype(jnp.bfloat16)
            for j in range(3):
                lane = 3 * PCOLS * (part // 3) + PCOLS * j + 256 * (part % 3)
                fin[ye, za, ze, :, lane : lane + 256] = total[:, 256 * j : 256 * j + 256]

        pl.when(active)(add)

    def weight_gradient(pair, order):
        n = 0 if pair is near else 1
        lanes = pl.ds(pl.multiple_of(256 * pair, 256), 256)
        for r in range(4):
            st[:, WIDTH * r : WIDTH * r + WIDTH] = ss[1, r + 1, :, lanes].T
        for j in range(3):
            for part in order:
                kk = part + PARTS * j
                window = xs[(kk // 2) % 3, kk // 6 : kk // 6 + 4, :, 256 * (kk % 2) : 256 * (kk % 2) + 256]
                term = jnp.dot(
                    st[...], window.reshape(4 * WIDTH, 256), preferred_element_type=jnp.float32
                )
                gwb[part, pair, :, :, :, :, :, 256 * j : 256 * j + 256] = term.astype(jnp.bfloat16).reshape(
                    2, 2, 2, 2, 16, 256
                )
                if (part, n) in halves:
                    sends, copy = halves[part, n][0][j]
                    when(sends, copy.start)

    passed_in(0)
    passed_in(1)

    @pl.when(passive)
    def _():
        for copy in to_turn:
            copy.wait_recv()

    @pl.loop(0, 3)
    def _(r):
        forward_row(near, r)

    crossed_far.wait_recv()
    pass_on(2)
    forward_row(near, 3)
    weight_gradient(near, NEAR_ORDER)

    passed_in(2)

    @pl.when(passive)
    def _():
        passed_in(3)

    @pl.when(active)
    def _():
        for k in range(1, 4):
            from_flip[k].wait_recv()

    @pl.loop(0, 2)
    def _(k):
        forward_row(far, 3 * k)

    slope_up = remote(ss.at[1, 1], ss.at[1, 5], s_send.at[0], s_recv.at[0], {"tile": 2 * jnp.maximum(z - 1, 0) + c})
    slope_down = remote(ss.at[1, 4], ss.at[1, 0], s_send.at[1], s_recv.at[1], {"tile": 2 * jnp.minimum(z + 1, 3) + c})
    pl.when(z > 0)(slope_up.start)
    pl.when(z < 3)(slope_down.start)

    @pl.loop(0, 2)
    def _(k):
        forward_row(far, 2 - k)

    for part in (0, 2, 3, 4, 5):
        add_half(part, 0)
    weight_gradient(far, FAR_ORDER)
    for part in range(2, 6):
        add_second(part, 0)

    pl.when(z > 0)(lambda: remote(ss.at[1, 0], ss.at[1, 0], s_send.at[1], s_recv.at[1], other_core).wait_recv())
    pl.when(z < 3)(lambda: remote(ss.at[1, 5], ss.at[1, 5], s_send.at[0], s_recv.at[0], other_core).wait_recv())
    shift_rows(ss, 0, 6)

    def input_row(r, out):
        lhs = jnp.concatenate([ss[2 - tap % 3, r + 2 - tap // 3] for tap in range(9)], axis=1)
        for e in range(2):
            chunks = []
            for tap in range(9):
                kk = 2 * tap + e
                chunks.append(
                    wall[kk // 3, :, :, :, :, :, :, 256 * (kk % 3) : 256 * (kk % 3) + 256].reshape(512, 256)
                )
            out[:, 256 * e : 256 * e + 256] = jnp.dot(
                lhs, jnp.concatenate(chunks, axis=0), preferred_element_type=jnp.float32
            )

    @pl.loop(0, 2)
    def _(k):
        input_row(2 * (1 - c) + k, igp.at[k])

    ig_pair = remote(igp, igr, i_send.at[0], i_recv.at[0], other_core)
    ig_pair.start()
    for part in FAR_ORDER:
        add_half(part, 1)

    trow[4:8, :] = id_row[4:8, :]
    trow[0:4, :] = jnp.zeros((4, 128), jnp.float32)

    @pl.loop(0, 2)
    def _(k):
        input_row(2 * c + k, acc)

        @pl.when(k == 0)
        def _():
            ig_pair.wait_recv()

        total = acc[...] + igr[k]
        gfb[k] = total.astype(jnp.bfloat16)
        column_sum = jnp.sum(total, axis=0, keepdims=True)
        for lane in range(4):
            trow[lane : lane + 1, :] += column_sum[:, 128 * lane : 128 * lane + 128]

    gf_copy = pltpu.make_async_copy(gfb, gf_out, loc_sem.at[11])
    gf_copy.start()

    t_copies = []
    for k in range(1, 8):
        copy = remote(trow, tpeer.at[k - 1], t_send.at[k - 1], t_recv.at[k - 1], {"tile": (t + k) % 8})
        copy.start()
        t_copies.append(copy)

    for part in FAR_ORDER:
        add_second(part, 1)

    @pl.loop(0, 4)
    def _(r):
        for lane in range(2):
            lanes = pl.ds(128 * lane, 128)
            for v in range(2):
                wide[lane, pl.ds(v, WIDTH, 2), :] = actv[v, r, :, lanes].astype(jnp.float32)
            upb[r, :, lanes] = wide[lane].astype(jnp.bfloat16)

    up_own, up_pair = [], []
    for k in range(2):
        up_own.append(pltpu.make_async_copy(upb.at[2 * c + k], up_out.at[2 * k + c], loc_sem.at[9 + k]))
        up_pair.append(
            remote(upb.at[2 * (1 - c) + k], up_out.at[2 * k + c], u_send.at[k], u_recv.at[k], other_core)
        )
        up_own[-1].start()
        up_pair[-1].start()

    for part in FAR_ORDER:
        add_third(part)

    for copy in t_copies:
        copy.wait_recv()
    for copy in t_copies:
        copy.wait_send()
    total = trow[0:4, :]
    for k in range(7):
        total = total + tpeer[k, 0:4, :]
    tall[0, 0:4, :] = total
    tall[0, 4:8, :] = trow[4:8, :]
    v_copies = []
    for k in range(1, 16):
        to = (frame + k) % 16
        copy = remote(
            tall.at[0], tall.at[k], v_send.at[k - 1], v_recv.at[k - 1], {"fsdp": to // 2, "dp": to % 2}
        )
        copy.start()
        v_copies.append(copy)

    spreads, to_pair, to_self = [], [], []
    for g in range(2):
        cols = pl.ds(3 * PCOLS * g, 3 * PCOLS)
        piece_at = fin.at[ye, za, ze, :, cols]
        spreads.append(
            [remote(piece_at, piece_at, f_send.at[g, k], f_recv.at[g, k], holders[k]) for k in range(7)]
        )
        for j in range(3):
            held = fin.at[:, :, :, :, pl.ds(3 * PCOLS * g + PCOLS * j, PCOLS)]
            out = gw_out.at[:, :, :, :, pl.ds(2 * PCOLS * j + PCOLS * g, PCOLS)]
            n = 3 * g + j
            to_pair.append(remote(held, out, i_send.at[1 + n], i_recv.at[1 + n], other_core))
            to_self.append(pltpu.make_async_copy(held, out, loc_sem.at[12 + n]))

    for g in range(2):
        for part in range(3 * g, 3 * g + 3):
            add_fourth(part)

        @pl.when(active)
        def _(g=g):
            for copy in spreads[g]:
                copy.start()

    @pl.when(active)
    def _():
        for g in range(2):
            for copy in spreads[g]:
                copy.wait_recv()
            for j in range(3):
                to_pair[3 * g + j].start()
                to_self[3 * g + j].start()
        for g in range(2):
            for copy in spreads[g]:
                copy.wait_send()
        for j in range(6):
            to_self[j].wait()
            to_pair[j].wait_send()

    @pl.when(c != xa)
    def _():
        for j in range(6):
            to_pair[j].wait_recv()

    for copy in v_copies:
        copy.wait()
    tab_copy = pltpu.make_async_copy(tall, tab_out, loc_sem.at[18])
    tab_copy.start()

    @pl.when(active)
    def _():
        for copy in to_turn + to_flip + [to_far]:
            copy.wait_send()

    @pl.when(passive)
    def _():
        for j in range(3):
            passed[3, j][0].wait_send()

    for copy in across + [across_far]:
        copy.wait_send()
    for k in range(3):
        for j in range(3):
            passed[k, j][0].wait_send()

    @pl.when(z > 0)
    def _():
        top_swap.wait_send()

    @pl.when(z < 3)
    def _():
        bottom_swap.wait_send()

    for copies, _, _ in halves.values():
        for sends, copy in copies:
            when(sends, copy.wait_send)
    for (sends, copy), _, _ in seconds.values():
        when(sends, copy.wait_send)
    for (part, n), (entry, _, _) in thirds.items():
        for sends, copy, _ in entry[1:] if part >= 4 and n == 1 else entry:
            when(sends, copy.wait_send)
    for entry in fourths.values():
        for sends, copy, _ in entry:
            when(sends, copy.wait_send)
    x_pair.wait_send()

    @pl.when(sends_rim)
    def _():
        for copy in rim_out:
            copy.wait_send()

    for copy in ct_pair:
        copy.wait_send()
    pl.when(z > 0)(slope_up.wait_send)
    pl.when(z < 3)(slope_down.wait_send)
    for k in range(2):
        up_own[k].wait()
        up_pair[k].wait()
    ig_pair.wait_send()
    gf_copy.wait()
    tab_copy.wait()


def fused(features, weight, cot, shift_row, id_row):
    any_space = pl.BlockSpec(memory_space=pl.ANY)
    vmem = pl.BlockSpec(memory_space=pltpu.VMEM)
    bf16, f32 = jnp.bfloat16, jnp.float32
    dma = pltpu.SemaphoreType.DMA
    return pl.pallas_call(
        kernel,
        out_shape=(
            jax.ShapeDtypeStruct((4, 2 * WIDTH, 256), bf16),
            jax.ShapeDtypeStruct((2, 2, 2, 16, 9 * CIN), bf16),
            jax.ShapeDtypeStruct((2, WIDTH, CIN), bf16),
            jax.ShapeDtypeStruct((16, 8, 128), f32),
        ),
        in_specs=[any_space, any_space, any_space, vmem, vmem],
        out_specs=[any_space] * 4,
        scratch_shapes=[
            pltpu.VMEM((3, 6, WIDTH, CIN), bf16),
            pltpu.VMEM((3, 6, WIDTH, HALF), bf16),
            pltpu.VMEM((256, 4 * WIDTH), bf16),
            pltpu.VMEM((PARTS, 2, 2, 2, 2, 2, 16, PCOLS), bf16),
            pltpu.VMEM((PARTS, 2, 2, 2, 2, 2, 16, PCOLS), bf16),
            pltpu.VMEM((PARTS, 2, 2, 2, 2, 2, 16, PCOLS), bf16),
            pltpu.VMEM((PARTS, 2, 2, 2, 2, 2, 16, PCOLS), bf16),
            pltpu.VMEM((PARTS, 3, 2, 2, 16, PCOLS), bf16),
            pltpu.VMEM((PARTS, 3, 16, PCOLS), bf16),
            pltpu.VMEM((2, 2, 2, 16, 9 * CIN), bf16),
            pltpu.VMEM((4, 2 * WIDTH, 256), bf16),
            pltpu.VMEM((2, 4, WIDTH, 256), bf16),
            pltpu.VMEM((2, 4, WIDTH, 256), bf16),
            pltpu.VMEM((4, 2 * WIDTH, 256), bf16),
            pltpu.VMEM((2, 2 * WIDTH, 128), f32),
            pltpu.VMEM((WIDTH, 512), f32),
            pltpu.VMEM((2, WIDTH, CIN), f32),
            pltpu.VMEM((2, WIDTH, CIN), f32),
            pltpu.VMEM((2, WIDTH, CIN), bf16),
            pltpu.VMEM((8, 128), f32),
            pltpu.VMEM((7, 8, 128), f32),
            pltpu.VMEM((16, 8, 128), f32),
            dma((19,)),
            dma((7,)),
            dma((7,)),
            dma((11,)),
            dma((11,)),
            dma((3,)),
            dma((3,)),
            dma((4, 3)),
            dma((4, 3)),
            dma((2,)),
            dma((2,)),
            dma((PARTS, 17)),
            dma((PARTS, 17)),
            dma((2, 7)),
            dma((2, 7)),
            dma((2,)),
            dma((2,)),
            dma((7,)),
            dma((7,)),
            dma((7,)),
            dma((7,)),
            dma((15,)),
            dma((15,)),
        ],
        compiler_params=pltpu.CompilerParams(
            collective_id=0, has_side_effects=True, vmem_limit_bytes=60 * 2**20
        ),
        cost_estimate=pl.CostEstimate(
            flops=6 * 768 * 4608 * 1024, bytes_accessed=2 * 10**7, transcendentals=3 * 768 * 1024
        ),
        name="conv_block",
    )(features, weight, cot, shift_row, id_row)


def shards(features, frame_table, frame_ids, conv_weight, cotangent):
    video_len = frame_table.shape[0]
    shift = lax.dynamic_slice_in_dim(frame_table, frame_ids[0], 1, axis=0).astype(jnp.float32)
    id_row = jnp.broadcast_to(frame_ids.astype(jnp.float32)[:, None], (8, 128))
    up, gw, gf, tab = fused(
        features[0], conv_weight.reshape(2, 2, 2, 16, 9 * CIN), cotangent[0], shift, id_row
    )
    sums = tab[:, :4].reshape(16, CIN)
    frames = tab[:, 4, 0]
    picker = (frames[:, None] == jnp.arange(video_len, dtype=jnp.float32)[None, :]).astype(jnp.float32)
    grad_table = lax.dot_general(
        picker, sums, (((0,), (0,)), ((), ())),
        precision=lax.Precision.HIGHEST, preferred_element_type=jnp.float32,
    )
    grad_weight = gw.reshape(128, 9 * CIN).astype(jnp.float32)
    return (up[None], grad_weight, gf[None], grad_table)


def solution(mesh):
    return jax.shard_map(
        shards,
        mesh=mesh,
        in_specs=(
            P(("fsdp", "dp"), "tile", None, None),
            P(),
            P(("fsdp", "dp")),
            P("fsdp", None),
            P(("fsdp", "dp"), "tile", None, None),
        ),
        out_specs=(
            P(("fsdp", "dp"), "tile", None, None),
            P("fsdp", None),
            P(("fsdp", "dp"), "tile", None, None),
            P(),
        ),
        check_vma=False,
    )
```

```python
import jax
import jax.numpy as jnp
from jax import lax
from jax.experimental import pallas as pl
from jax.experimental.pallas import tpu as pltpu
from jax.sharding import PartitionSpec as P

inv_root_two = 0.7071067811865476
inv_root_tau = 0.3989422804014327

WIDTH = 384
CIN = 512
HALF = 512
PARTS = 6
PCOLS = 768
CHUNKS = 18

DIMS = 6

FIRST = [(0, 1), (1, 0), (2, 3), (3, 2), (4, 5), (5, 4)]
NEAR_RUNS = ((0, 1, 2, 3, 4, 5),)
FAR_RUNS = ((1, 0), (2, 3), (4, 5))
ORDER = (0, 2, 3, 4, 5, 1)

MESH = pl.DeviceIdType.MESH


def kernel(
    feat, weight, cot, shift_row, id_row,
    up_out, gw_out, gf_out, tab_out,
    xs, ss, st, wall, gwb, got0, got1, got2, got3, fin, ctv, cts, actv, upb, wide, acc, igp, igo, igr, gfb,
    trow, tpeer, tall,
    loc_sem, x_send, x_recv, o_send, o_recv, n_send, n_recv, q_send, q_recv, s_send, s_recv,
    r_send, r_recv, f_send, f_recv, u_send, u_recv, i_send, i_recv, t_send, t_recv, v_send, v_recv,
):
    f = lax.axis_index("fsdp")
    t = lax.axis_index("tile")
    lo = lax.axis_index("dp")
    x, h = f // 2, f % 2
    z, c = t // 2, t % 2
    xa, xb = x // 2, x % 2
    xe = (xa + xb) % 2
    ye = (h + lo) % 2
    za = z // 2
    ze = (za + z % 2) % 2
    keep = (c + xe) % 2
    active, passive = c == xa, c != xa
    mine = {1: keep, 2: h, 3: ye, 4: za, 5: ze}
    x_flip = x + 1 - 2 * xb
    z_flip = z + 1 - 2 * (z % 2)
    partner = {
        0: {"fsdp": (3 - x) * 2 + h},
        1: {"fsdp": x_flip * 2 + h},
        2: {"fsdp": x * 2 + 1 - h, "dp": 1 - lo},
        3: {"dp": 1 - lo},
        4: {"tile": (3 - z) * 2 + c},
        5: {"tile": z_flip * 2 + c},
    }
    other_core = {"tile": 2 * z + 1 - c}
    two_away = {"fsdp": (x + 2) % 4 * 2 + h}
    quarter = (z + 2 * ye) % 4
    holders = [
        {"tile": (z + k // 2) % 4 * 2 + c, "dp": (lo + k % 2) % 2} for k in range(1, 8)
    ]

    def remote(src, dst, send_sem, recv_sem, device):
        return pltpu.make_async_remote_copy(
            src_ref=src, dst_ref=dst, send_sem=send_sem, recv_sem=recv_sem,
            device_id=device, device_id_type=MESH,
        )

    barrier = pltpu.get_barrier_semaphore()
    for k in range(1, 8):
        pl.semaphore_signal(barrier, inc=1, device_id={"tile": (t + k) % 8}, device_id_type=MESH)
    frame = f * 2 + lo
    for k in range(1, 16):
        to = (frame + k) % 16
        pl.semaphore_signal(
            barrier, inc=1, device_id={"fsdp": to // 2, "dp": to % 2}, device_id_type=MESH
        )

    for k in (3, 5, 7):
        pl.semaphore_signal(barrier, inc=1, device_id=holders[k - 1], device_id_type=MESH)

    near, far = keep, 1 - keep
    own_x = pltpu.make_async_copy(feat, xs.at[1, pl.ds(1 + 2 * c, 2)], loc_sem.at[0])
    own_x.start()
    own_w = [
        pltpu.make_async_copy(
            weight.at[:, :, :, :, pl.ds(PCOLS * part, PCOLS)], wall.at[part, near, h], loc_sem.at[1 + part]
        )
        for part in range(PARTS)
    ]

    @pl.when(active)
    def _():
        for copy in own_w:
            copy.start()

    own_ct = []
    for k in range(2):
        own_ct.append(
            pltpu.make_async_copy(cot.at[2 * k + c], ctv.at[2 * c + k], loc_sem.at[7 + k])
        )
        own_ct[-1].start()

    own_x.wait()
    for k in range(2):
        for lane in range(4):
            at = pl.ds(128 * lane, 128)
            row = xs[1, 1 + 2 * c + k, :, at].astype(jnp.float32) + shift_row[:, at]
            xs[1, 1 + 2 * c + k, :, at] = row.astype(jnp.bfloat16)

    pl.semaphore_wait(barrier, 25)

    def same(pair, half, number, send_sem, recv_sem, device, eighth=None):
        place = wall.at[:, pair, half, number // 2, number % 2]
        if eighth is not None:
            place = wall.at[:, pair, half, number // 2, number % 2, eighth]
        return remote(place, place, send_sem, recv_sem, device)

    turn = [(quarter + k) % 4 for k in range(4)]
    to_flip = [same(near, h, turn[k], o_send.at[k], o_recv.at[k], partner[1]) for k in range(4)]
    to_turn = [same(near, h, turn[k], o_send.at[3 + k], o_recv.at[3 + k], partner[0]) for k in range(1, 4)]
    first_turn = [same(near, h, quarter, o_send.at[9 + e], o_recv.at[9 + e], partner[0], e) for e in range(2)]
    relay = [same(near, h, quarter, o_send.at[7 + e], o_recv.at[7 + e], partner[1], e) for e in range(2)]
    from_flip = [same(far, h, turn[k], o_send.at[k], o_recv.at[k], partner[1]) for k in range(4)]
    from_far = [same(far, h, quarter, o_send.at[7 + e], o_recv.at[7 + e], partner[1], e) for e in range(2)]
    across = [same(near, h, quarter, n_send.at[e], n_recv.at[e], partner[2], e) for e in range(2)]
    crossed = [same(near, 1 - h, quarter, n_send.at[e], n_recv.at[e], partner[2], e) for e in range(2)]
    across_far = same(far, h, quarter, n_send.at[2], n_recv.at[2], partner[2])
    crossed_far = same(far, 1 - h, quarter, n_send.at[2], n_recv.at[2], partner[2])
    passed = {}
    theirs = {3: (quarter + 2) % 4, 4: (3 - z + 2 * ye) % 4, 5: (z_flip + 2 * ye) % 4}
    for k, (pair, half, e) in enumerate(((near, 1 - h, 0), (near, 1 - h, 1), (far, 1 - h, None), (far, h, None))):
        for j, dim in enumerate((3, 4, 5)):
            passed[k, j] = (
                same(pair, half, quarter, q_send.at[k, j], q_recv.at[k, j], partner[dim], e),
                same(pair, half, theirs[dim], q_send.at[k, j], q_recv.at[k, j], partner[dim], e),
            )

    def pass_on(k):
        for j in range(3):
            passed[k, j][0].start()

    def passed_in(k):
        for j in range(3):
            passed[k, j][1].wait_recv()

    @pl.when(active)
    def _():
        for copy in own_w:
            copy.wait()
        for e in range(2):
            first_turn[e].start()
            across[e].start()
        to_flip[0].start()

    x_pair = remote(
        xs.at[1, pl.ds(1 + 2 * c, 2)], xs.at[1, pl.ds(1 + 2 * c, 2)], x_send.at[0], x_recv.at[0], other_core
    )
    x_pair_in = remote(
        xs.at[1, pl.ds(3 - 2 * c, 2)], xs.at[1, pl.ds(3 - 2 * c, 2)], x_send.at[0], x_recv.at[0], other_core
    )
    rim_cols = WIDTH // 2
    sends_rim = jnp.where(c == 0, z > 0, z < 3)
    z_rim = jnp.where(c == 0, jnp.maximum(z - 1, 0), jnp.minimum(z + 1, 3))
    rim_out = [
        remote(
            xs.at[1, 1 + 3 * c, pl.ds(rim_cols * k, rim_cols)],
            xs.at[1, 5 - 5 * c, pl.ds(rim_cols * k, rim_cols)],
            x_send.at[1 + k], x_recv.at[1 + c], {"tile": 2 * z_rim + k},
        )
        for k in range(2)
    ]

    def rim_part(row, core, sem):
        at = xs.at[1, row, pl.ds(pl.multiple_of(rim_cols * core, rim_cols), rim_cols)]
        return remote(at, at, x_send.at[sem], x_recv.at[sem], other_core)

    top_in, bottom_in = rim_part(0, c, 2), rim_part(5, c, 1)
    top_swap, bottom_swap = rim_part(0, c, 5), rim_part(5, c, 6)
    top_swapped, bottom_swapped = rim_part(0, 1 - c, 5), rim_part(5, 1 - c, 6)

    @pl.when(sends_rim)
    def _():
        for copy in rim_out:
            copy.start()

    x_pair.start()

    ct_pair = []
    for k in range(2):
        ct_pair.append(
            remote(cot.at[2 * k + 1 - c], ctv.at[2 * c + k], x_send.at[3 + k], x_recv.at[3 + k], other_core)
        )
        ct_pair[-1].start()

    @pl.when(z == 0)
    def _():
        xs[1, 0] = jnp.zeros((WIDTH, CIN), jnp.bfloat16)
        ss[1, 0] = jnp.zeros((WIDTH, HALF), jnp.bfloat16)

    @pl.when(z == 3)
    def _():
        xs[1, 5] = jnp.zeros((WIDTH, CIN), jnp.bfloat16)
        ss[1, 5] = jnp.zeros((WIDTH, HALF), jnp.bfloat16)

    column = lax.broadcasted_iota(jnp.int32, (WIDTH, 128), 0)

    def shift_row(ref, row):
        for lane in range(4):
            at = pl.ds(128 * lane, 128)
            values = ref[1, row, :, at].astype(jnp.float32)
            right = jnp.where(column == 0, 0.0, pltpu.roll(values, 1, 0))
            left = jnp.where(column == WIDTH - 1, 0.0, pltpu.roll(values, WIDTH - 1, 0))
            ref[0, row, :, at] = right.astype(jnp.bfloat16)
            ref[2, row, :, at] = left.astype(jnp.bfloat16)

    def shift_rows(ref, first, count):
        @pl.loop(0, count)
        def _(k):
            shift_row(ref, first + k)

    @pl.when(active)
    def _():
        for e in range(2):
            first_turn[e].wait_send()
        to_turn[0].start()

    shift_rows(xs, 1 + 2 * c, 2)

    @pl.when(active)
    def _():
        for e in range(2):
            crossed[e].wait_recv()
            pass_on(e)
        for k in range(1, 3):
            to_turn[k].start()
        to_flip[1].start()

    @pl.when(passive)
    def _():
        for e in range(2):
            first_turn[e].wait_recv()
            across[e].start()
            relay[e].start()

    x_pair_in.wait_recv()
    shift_rows(xs, 3 - 2 * c, 2)

    @pl.when(z > 0)
    def _():
        top_in.wait_recv()
        top_swap.start()

    @pl.when(z < 3)
    def _():
        bottom_in.wait_recv()
        bottom_swap.start()

    @pl.when(passive)
    def _():
        for e in range(2):
            crossed[e].wait_recv()
            pass_on(e)

    for copy in own_ct:
        copy.wait()
    for copy in ct_pair:
        copy.wait_recv()

    @pl.loop(0, 4)
    def _(r):
        for lane in range(2):
            wide[lane] = ctv[r, :, 128 * lane : 128 * lane + 128].astype(jnp.float32)
        for v in range(2):
            for lane in range(2):
                cts[v, r, :, 128 * lane : 128 * lane + 128] = wide[lane, pl.ds(v, WIDTH, 2), :].astype(jnp.bfloat16)

    @pl.when(z > 0)
    def _():
        top_swapped.wait_recv()

    @pl.when(z < 3)
    def _():
        bottom_swapped.wait_recv()

    shift_rows(xs, 0, 1)
    shift_rows(xs, 5, 1)

    @pl.when(active)
    def _():
        from_flip[0].wait_recv()
        across_far.start()
        for k in range(2, 4):
            to_flip[k].start()

    @pl.when(passive)
    def _():
        for copy in from_far:
            copy.wait_recv()
        across_far.start()
        pass_on(3)

    def forward_row(v, r):
        lhs = jnp.concatenate(
            [
                xs[(kk // 2) % 3, r + kk // 6, :, 256 * (kk % 2) : 256 * (kk % 2) + 256]
                for kk in range(CHUNKS)
            ],
            axis=1,
        )
        rhs = jnp.concatenate(
            [
                wall[kk // 3, v, :, :, :, :, :, 256 * (kk % 3) : 256 * (kk % 3) + 256].reshape(256, 256)
                for kk in range(CHUNKS)
            ],
            axis=1,
        )
        acc[...] = lax.dot_general(
            lhs, rhs, (((1,), (1,)), ((), ())), preferred_element_type=jnp.float32
        )

        @pl.loop(0, WIDTH // 32)
        def _(j):
            rows = pl.ds(pl.multiple_of(j * 32, 32), 32)
            value = acc[rows]
            grown = 0.5 * (1.0 + lax.erf(value * inv_root_two))
            slope = grown + value * jnp.exp(-0.5 * value * value) * inv_root_tau
            actv[v, r, rows] = (value * grown).astype(jnp.bfloat16)
            out = pl.ds(pl.multiple_of(256 * v, 256), 256)
            ss[1, r + 1, rows, out] = (cts[v, r, rows].astype(jnp.float32) * slope).astype(jnp.bfloat16)

    def at(part, fixed):
        return (part,) + tuple(fixed.get(d, slice(None)) for d in range(1, 6))

    def when(condition, body):
        if condition is None:
            body()
        else:
            pl.when(condition)(body)

    two_y = {"fsdp": x * 2 + 1 - h}
    two_z = {"tile": (z + 2) % 4 * 2 + c}

    halves, seconds, thirds, fourths = {}, {}, {}, {}

    def half_copy(part, n, dim, there, sends):
        place = at(part, there)
        return (
            sends,
            remote(gwb.at[place], got0.at[place], r_send.at[part, n], r_recv.at[part, n], partner[dim]),
        )

    def second_copy(part, n, dim, there, sends):
        place = at(part, there)
        return (
            sends,
            remote(
                gwb.at[place], got1.at[place], r_send.at[part, 2 + n], r_recv.at[part, 2 + n], partner[dim]
            ),
        )

    def slot_copy(part, there, slots, slot, sem, device, sends):
        return (
            sends,
            remote(
                gwb.at[at(part, there)], slots.at[slot], r_send.at[part, sem], r_recv.at[part, sem], device
            ),
            slot,
        )

    def flips(axis):
        da, db = 2 * axis, 2 * axis + 1
        there = {da: 1 - mine[da], db: 1 - mine[db]}
        return (
            ({da: there[da], db: mine[db]}, partner[da]),
            ({da: mine[da], db: there[db]}, partner[db]),
            (there, two_y if axis == 1 else two_z),
        )

    def along_x(part, kept, slots, sem):
        return [
            slot_copy(part, {**kept, 1: pair}, slots, (part, j), sem + j, device, sends)
            for j, (sends, pair, device) in enumerate(
                ((passive, near, partner[0]), (active, far, partner[1]), (passive, far, two_away))
            )
        ]

    for n, pair in enumerate((near, far)):
        halves[0, n] = (half_copy(0, n, 0, {1: pair}, passive), active, at(0, {1: pair}))
    seconds[0, 1] = (second_copy(0, 1, 1, {1: far}, active), active, at(0, {1: near}))
    across_x = [
        (
            sends,
            remote(
                gwb.at[at(1, {1: pair})], slots.at[at(1, {1: place})], r_send.at[1, j], r_recv.at[1, j], device
            ),
        )
        for j, (sends, pair, device, slots, place) in enumerate(
            (
                (passive, near, partner[0], got0, near),
                (active, far, partner[1], got1, far),
                (passive, far, two_away, got0, near),
            )
        )
    ]
    for part in (0, 1):
        thirds[part, 1] = (
            [
                slot_copy(part, {1: near, **there}, got2, (part, j), 7 + j, device, active)
                for j, (there, device) in enumerate(flips(1))
            ],
            active, at(part, {1: near, 2: h, 3: ye}),
        )
        fourths[part] = [
            slot_copy(part, {1: near, 2: h, 3: ye, **there}, got3, (part, j), 10 + j, device, active)
            for j, (there, device) in enumerate(flips(2))
        ]
    for part in range(2, 6):
        one, two = FIRST[part]
        first = {one: mine[one]}
        both = {**first, two: mine[two]}
        for n, pair in enumerate((near, far)):
            halves[part, n] = (
                half_copy(part, n, one, {1: pair, one: 1 - mine[one]}, None),
                None, at(part, {1: pair, **first}),
            )
            seconds[part, n] = (
                second_copy(part, n, two, {1: pair, **first, two: 1 - mine[two]}, None),
                None, at(part, {1: pair, **both}),
            )
            if part < 4:
                thirds[part, n] = (
                    [
                        slot_copy(
                            part, {1: pair, **both, **there}, got2, (part, j, 0, pair), 4 + 3 * n + j, device, None
                        )
                        for j, (there, device) in enumerate(flips(2))
                    ],
                    None, at(part, {1: pair, **both, 4: za, 5: ze}),
                )
        if part < 4:
            fourths[part] = along_x(part, {**both, 4: za, 5: ze}, got3, 10)
        else:
            copies = along_x(part, both, got2, 4)
            thirds[part, 0] = ([copies[0]], None, None)
            thirds[part, 1] = (copies, active, at(part, {**both, 1: near}))
            fourths[part] = [
                slot_copy(part, {1: near, **both, **there}, got3, (part, j), 10 + j, device, active)
                for j, (there, device) in enumerate(flips(1))
            ]

    def add_across():
        def add():
            for _, copy in across_x:
                copy.wait_recv()
            here, there = at(1, {1: near}), at(1, {1: far})
            total = gwb[here].astype(jnp.float32) + got0[here].astype(jnp.float32)
            total = total + got1[here].astype(jnp.float32) + got0[there].astype(jnp.float32)
            gwb[here] = total.astype(jnp.bfloat16)

        pl.when(active)(add)
        for sends, copy, _ in thirds[1, 1][0]:
            when(sends, copy.start)

    def add_half(part, n):
        if (part, n) in halves:
            (_, copy), receives, here = halves[part, n]

            def add():
                copy.wait_recv()
                total = gwb[here].astype(jnp.float32) + got0[here].astype(jnp.float32)
                gwb[here] = total.astype(jnp.bfloat16)

            when(receives, add)
        if (part, n) in seconds:
            when(seconds[part, n][0][0], seconds[part, n][0][1].start)

    def add_second(part, n):
        if (part, n) not in seconds:
            return
        (_, copy), receives, here = seconds[part, n]

        def add():
            copy.wait_recv()
            total = gwb[here].astype(jnp.float32) + got1[here].astype(jnp.float32)
            gwb[here] = total.astype(jnp.bfloat16)

        when(receives, add)
        entry = thirds[part, n][0]
        for sends, copy, _ in entry[1:] if part >= 4 and n == 1 else entry:
            when(sends, copy.start)

    def add_third(part):
        for n in range(2):
            if (part, n) in thirds and thirds[part, n][2] is not None:
                entry, receives, here = thirds[part, n]

                def add(entry=entry, here=here):
                    total = gwb[here].astype(jnp.float32)
                    for _, copy, slot in entry:
                        copy.wait_recv()
                        total = total + got2[slot].astype(jnp.float32)
                    gwb[here] = total.astype(jnp.bfloat16)

                when(receives, add)
        for sends, copy, _ in fourths[part]:
            when(sends, copy.start)

    def add_fourth(part):
        here = at(part, {1: near, 2: h, 3: ye, 4: za, 5: ze})

        def add():
            total = gwb[here].astype(jnp.float32)
            for _, copy, slot in fourths[part]:
                copy.wait_recv()
                total = total + got3[slot].astype(jnp.float32)
            total = total.astype(jnp.bfloat16)
            fin[ye, za, ze, :, PCOLS * part : PCOLS * part + PCOLS] = total

        pl.when(active)(add)

    def weight_gradient(pair, order):
        n = 0 if pair is near else 1
        lanes = pl.ds(pl.multiple_of(256 * pair, 256), 256)
        for r in range(4):
            st[:, WIDTH * r : WIDTH * r + WIDTH] = ss[1, r + 1, :, lanes].T
        for run in order:
            for part in run:
                for j in range(3):
                    kk = 3 * part + j
                    window = xs[(kk // 2) % 3, kk // 6 : kk // 6 + 4, :, 256 * (kk % 2) : 256 * (kk % 2) + 256]
                    term = jnp.dot(
                        st[...], window.reshape(4 * WIDTH, 256), preferred_element_type=jnp.float32
                    )
                    gwb[part, pair, :, :, :, :, :, 256 * j : 256 * j + 256] = term.astype(jnp.bfloat16).reshape(
                        2, 2, 2, 2, 16, 256
                    )
            for part in run:
                if (part, n) in halves:
                    sends, copy = halves[part, n][0]
                    when(sends, copy.start)
                if part == 1:
                    for sends, copy in across_x[1:] if n else across_x[:1]:
                        when(sends, copy.start)

    passed_in(0)
    passed_in(1)

    @pl.when(passive)
    def _():
        for copy in to_turn:
            copy.wait_recv()

    @pl.loop(0, 4)
    def _(r):
        @pl.when(r == jnp.where(active, 2, 1))
        def _():
            crossed_far.wait_recv()
            pass_on(2)

        forward_row(near, r)

    weight_gradient(near, NEAR_RUNS)

    passed_in(2)

    @pl.when(passive)
    def _():
        passed_in(3)

    @pl.when(active)
    def _():
        for k in range(1, 4):
            from_flip[k].wait_recv()

    @pl.loop(0, 2)
    def _(k):
        forward_row(far, 3 * k)

    slope_up = remote(ss.at[1, 1], ss.at[1, 5], s_send.at[0], s_recv.at[0], {"tile": 2 * jnp.maximum(z - 1, 0) + c})
    slope_down = remote(ss.at[1, 4], ss.at[1, 0], s_send.at[1], s_recv.at[1], {"tile": 2 * jnp.minimum(z + 1, 3) + c})
    pl.when(z > 0)(slope_up.start)
    pl.when(z < 3)(slope_down.start)

    @pl.loop(0, 2)
    def _(k):
        forward_row(far, 2 - k)

    for part in (0, 2, 3, 4, 5):
        add_half(part, 0)
    weight_gradient(far, FAR_RUNS)

    pl.when(z > 0)(lambda: remote(ss.at[1, 0], ss.at[1, 0], s_send.at[1], s_recv.at[1], other_core).wait_recv())
    pl.when(z < 3)(lambda: remote(ss.at[1, 5], ss.at[1, 5], s_send.at[0], s_recv.at[0], other_core).wait_recv())
    shift_rows(ss, 0, 6)

    def input_row(r, out):
        lhs = jnp.concatenate([ss[2 - tap % 3, r + 2 - tap // 3] for tap in range(9)], axis=1)
        for e in range(2):
            chunks = []
            for tap in range(9):
                kk = 2 * tap + e
                chunks.append(
                    wall[kk // 3, :, :, :, :, :, :, 256 * (kk % 3) : 256 * (kk % 3) + 256].reshape(512, 256)
                )
            out[:, 256 * e : 256 * e + 256] = jnp.dot(
                lhs, jnp.concatenate(chunks, axis=0), preferred_element_type=jnp.float32
            )

    @pl.loop(0, 2)
    def _(k):
        input_row(2 * (1 - c) + k, igp.at[k])

    ig_pair = remote(igp, igr, i_send.at[0], i_recv.at[0], other_core)
    ig_pair.start()
    for part in range(2, 6):
        add_second(part, 0)
    for part in (0, 2, 3, 4, 5):
        add_half(part, 1)
    add_across()

    trow[4:8, :] = id_row[4:8, :]
    trow[0:4, :] = jnp.zeros((4, 128), jnp.float32)

    @pl.loop(0, 2)
    def _(k):
        input_row(2 * c + k, igo.at[k])

    for part in ORDER:
        add_second(part, 1)

    ig_pair.wait_recv()

    @pl.loop(0, 2)
    def _(k):
        total = igo[k] + igr[k]
        gfb[k] = total.astype(jnp.bfloat16)
        column_sum = jnp.sum(total, axis=0, keepdims=True)
        for lane in range(4):
            trow[lane : lane + 1, :] += column_sum[:, 128 * lane : 128 * lane + 128]

    gf_copy = pltpu.make_async_copy(gfb, gf_out, loc_sem.at[11])
    gf_copy.start()

    t_copies = []
    for k in range(1, 8):
        copy = remote(trow, tpeer.at[k - 1], t_send.at[k - 1], t_recv.at[k - 1], {"tile": (t + k) % 8})
        copy.start()
        t_copies.append(copy)

    @pl.loop(0, 4)
    def _(r):
        for lane in range(2):
            lanes = pl.ds(128 * lane, 128)
            for v in range(2):
                wide[lane, pl.ds(v, WIDTH, 2), :] = actv[v, r, :, lanes].astype(jnp.float32)
            upb[r, :, lanes] = wide[lane].astype(jnp.bfloat16)

    up_own, up_pair = [], []
    for k in range(2):
        up_own.append(pltpu.make_async_copy(upb.at[2 * c + k], up_out.at[2 * k + c], loc_sem.at[9 + k]))
        up_pair.append(
            remote(upb.at[2 * (1 - c) + k], up_out.at[2 * k + c], u_send.at[k], u_recv.at[k], other_core)
        )
        up_own[-1].start()
        up_pair[-1].start()

    for part in ORDER:
        add_third(part)

    for copy in t_copies:
        copy.wait_recv()
    for copy in t_copies:
        copy.wait_send()
    total = trow[0:4, :]
    for k in range(7):
        total = total + tpeer[k, 0:4, :]
    tall[0, 0:4, :] = total
    tall[0, 4:8, :] = trow[4:8, :]
    y = 2 * h + lo
    v_copies = []
    for k in range(1, 4):
        to = (y + k) % 4
        v_copies.append(
            remote(tall.at[0], tall.at[k], v_send.at[k - 1], v_recv.at[k - 1], {"fsdp": 2 * x + to // 2, "dp": to % 2})
        )
    for k in range(1, 4):
        to = (x + k) % 4
        v_copies.append(
            remote(
                tall.at[pl.ds(0, 4)], tall.at[pl.ds(4 * k, 4)], v_send.at[2 + k], v_recv.at[2 + k], {"fsdp": 2 * to + h}
            )
        )
    for copy in v_copies[:3]:
        copy.start()

    spreads, to_pair, to_self = [], [], []
    for g in range(2):
        cols = pl.ds(3 * PCOLS * g, 3 * PCOLS)
        piece_at = fin.at[ye, za, ze, :, cols]
        spreads.append(
            [remote(piece_at, piece_at, f_send.at[g, k], f_recv.at[g, k], holders[k]) for k in range(7)]
        )
        held, out = fin.at[:, :, :, :, cols], gw_out.at[:, :, :, :, cols]
        to_pair.append(remote(held, out, i_send.at[1 + g], i_recv.at[1 + g], other_core))
        to_self.append(pltpu.make_async_copy(held, out, loc_sem.at[12 + g]))

    for g in range(2):
        for part in range(3 * g, 3 * g + 3):
            add_fourth(part)

        @pl.when(active)
        def _(g=g):
            for copy in spreads[g]:
                copy.start()

    for copy in v_copies[:3]:
        copy.wait_recv()
    for copy in v_copies[3:]:
        copy.start()

    @pl.when(active)
    def _():
        for g in range(2):
            for copy in spreads[g]:
                copy.wait_recv()
            to_pair[g].start()
            to_self[g].start()
        for g in range(2):
            for copy in spreads[g]:
                copy.wait_send()
            to_self[g].wait()
            to_pair[g].wait_send()

    @pl.when(c != xa)
    def _():
        for g in range(2):
            to_pair[g].wait_recv()

    for copy in v_copies[3:]:
        copy.wait_recv()
    for copy in v_copies:
        copy.wait_send()
    tab_copy = pltpu.make_async_copy(tall, tab_out, loc_sem.at[14])
    tab_copy.start()

    @pl.when(active)
    def _():
        for copy in to_turn + to_flip:
            copy.wait_send()

    @pl.when(passive)
    def _():
        for copy in relay:
            copy.wait_send()
        for j in range(3):
            passed[3, j][0].wait_send()

    for copy in across + [across_far]:
        copy.wait_send()
    for k in range(3):
        for j in range(3):
            passed[k, j][0].wait_send()

    @pl.when(z > 0)
    def _():
        top_swap.wait_send()

    @pl.when(z < 3)
    def _():
        bottom_swap.wait_send()

    for (sends, copy), _, _ in list(halves.values()) + list(seconds.values()):
        when(sends, copy.wait_send)
    for sends, copy in across_x:
        when(sends, copy.wait_send)
    for (part, n), (entry, _, _) in thirds.items():
        for sends, copy, _ in entry[1:] if part >= 4 and n == 1 else entry:
            when(sends, copy.wait_send)
    for entry in fourths.values():
        for sends, copy, _ in entry:
            when(sends, copy.wait_send)
    x_pair.wait_send()

    @pl.when(sends_rim)
    def _():
        for copy in rim_out:
            copy.wait_send()

    for copy in ct_pair:
        copy.wait_send()
    pl.when(z > 0)(slope_up.wait_send)
    pl.when(z < 3)(slope_down.wait_send)
    for k in range(2):
        up_own[k].wait()
        up_pair[k].wait()
    ig_pair.wait_send()
    gf_copy.wait()
    tab_copy.wait()


def fused(features, weight, cot, shift_row, id_row):
    any_space = pl.BlockSpec(memory_space=pl.ANY)
    vmem = pl.BlockSpec(memory_space=pltpu.VMEM)
    bf16, f32 = jnp.bfloat16, jnp.float32
    dma = pltpu.SemaphoreType.DMA
    return pl.pallas_call(
        kernel,
        out_shape=(
            jax.ShapeDtypeStruct((4, 2 * WIDTH, 256), bf16),
            jax.ShapeDtypeStruct((2, 2, 2, 16, 9 * CIN), bf16),
            jax.ShapeDtypeStruct((2, WIDTH, CIN), bf16),
            jax.ShapeDtypeStruct((16, 8, 128), f32),
        ),
        in_specs=[any_space, any_space, any_space, vmem, vmem],
        out_specs=[any_space] * 4,
        scratch_shapes=[
            pltpu.VMEM((3, 6, WIDTH, CIN), bf16),
            pltpu.VMEM((3, 6, WIDTH, HALF), bf16),
            pltpu.VMEM((256, 4 * WIDTH), bf16),
            pltpu.VMEM((PARTS, 2, 2, 2, 2, 2, 16, PCOLS), bf16),
            pltpu.VMEM((PARTS, 2, 2, 2, 2, 2, 16, PCOLS), bf16),
            pltpu.VMEM((PARTS, 2, 2, 2, 2, 2, 16, PCOLS), bf16),
            pltpu.VMEM((PARTS, 2, 2, 2, 2, 2, 16, PCOLS), bf16),
            pltpu.VMEM((PARTS, 3, 2, 2, 16, PCOLS), bf16),
            pltpu.VMEM((PARTS, 3, 16, PCOLS), bf16),
            pltpu.VMEM((2, 2, 2, 16, 9 * CIN), bf16),
            pltpu.VMEM((4, 2 * WIDTH, 256), bf16),
            pltpu.VMEM((2, 4, WIDTH, 256), bf16),
            pltpu.VMEM((2, 4, WIDTH, 256), bf16),
            pltpu.VMEM((4, 2 * WIDTH, 256), bf16),
            pltpu.VMEM((2, 2 * WIDTH, 128), f32),
            pltpu.VMEM((WIDTH, 256), f32),
            pltpu.VMEM((2, WIDTH, CIN), f32),
            pltpu.VMEM((2, WIDTH, CIN), f32),
            pltpu.VMEM((2, WIDTH, CIN), f32),
            pltpu.VMEM((2, WIDTH, CIN), bf16),
            pltpu.VMEM((8, 128), f32),
            pltpu.VMEM((7, 8, 128), f32),
            pltpu.VMEM((16, 8, 128), f32),
            dma((15,)),
            dma((7,)),
            dma((7,)),
            dma((11,)),
            dma((11,)),
            dma((3,)),
            dma((3,)),
            dma((4, 3)),
            dma((4, 3)),
            dma((2,)),
            dma((2,)),
            dma((PARTS, 13)),
            dma((PARTS, 13)),
            dma((2, 7)),
            dma((2, 7)),
            dma((2,)),
            dma((2,)),
            dma((3,)),
            dma((3,)),
            dma((7,)),
            dma((7,)),
            dma((6,)),
            dma((6,)),
        ],
        compiler_params=pltpu.CompilerParams(
            collective_id=0, has_side_effects=True, vmem_limit_bytes=60 * 2**20
        ),
        cost_estimate=pl.CostEstimate(
            flops=6 * 768 * 4608 * 1024, bytes_accessed=2 * 10**7, transcendentals=3 * 768 * 1024
        ),
        name="conv_block",
    )(features, weight, cot, shift_row, id_row)


def shards(features, frame_table, frame_ids, conv_weight, cotangent):
    video_len = frame_table.shape[0]
    shift = lax.dynamic_slice_in_dim(frame_table, frame_ids[0], 1, axis=0).astype(jnp.float32)
    id_row = jnp.broadcast_to(frame_ids.astype(jnp.float32)[:, None], (8, 128))
    up, gw, gf, tab = fused(
        features[0], conv_weight.reshape(2, 2, 2, 16, 9 * CIN), cotangent[0], shift, id_row
    )
    sums = tab[:, :4].reshape(16, CIN)
    frames = tab[:, 4, 0]
    picker = (frames[:, None] == jnp.arange(video_len, dtype=jnp.float32)[None, :]).astype(jnp.float32)
    grad_table = lax.dot_general(
        picker, sums, (((0,), (0,)), ((), ())),
        precision=lax.Precision.HIGHEST, preferred_element_type=jnp.float32,
    )
    grad_weight = gw.reshape(128, 9 * CIN).astype(jnp.float32)
    return (up[None], grad_weight, gf[None], grad_table)


def solution(mesh):
    return jax.shard_map(
        shards,
        mesh=mesh,
        in_specs=(
            P(("fsdp", "dp"), "tile", None, None),
            P(),
            P(("fsdp", "dp")),
            P("fsdp", None),
            P(("fsdp", "dp"), "tile", None, None),
        ),
        out_specs=(
            P(("fsdp", "dp"), "tile", None, None),
            P("fsdp", None),
            P(("fsdp", "dp"), "tile", None, None),
            P(),
        ),
        check_vma=False,
    )
```

```python
import jax
import jax.numpy as jnp
from jax import lax
from jax.experimental import pallas as pl
from jax.experimental.pallas import tpu as pltpu
from jax.sharding import PartitionSpec as P

inv_root_two = 0.7071067811865476
inv_root_tau = 0.3989422804014327

WIDTH = 384
CIN = 512
HALF = 512
PARTS = 6
PCOLS = 768
CHUNKS = 18

DIMS = 6

FIRST = [(0, 1), (1, 0), (2, 3), (3, 2), (4, 5), (5, 4)]
NEAR_RUNS = ((0, 1, 2, 3, 4, 5),)
FAR_RUNS = ((0, 1), (2, 3), (4, 5))
SPANS = ((0, 3), (3, 2), (5, 4), (9, 4), (13, 3), (16, 2))
GCOLS = 1024
ORDER = (0, 2, 3, 4, 5, 1)

MESH = pl.DeviceIdType.MESH


def kernel(
    feat, weight, cot, shift_row_in, frame_id,
    up_out, gw_out, gf_out, tab_out,
    xs, ss, st, wall, gwb, got0, got1, got2, got3, fin, ctv, cts, actv, upb, wide, acc, igp, igo, igr, gfb,
    trow, tpeer, tall,
    loc_sem, x_send, x_recv, o_send, o_recv, n_send, n_recv, q_send, q_recv, s_send, s_recv,
    r_send, r_recv, f_send, f_recv, u_send, u_recv, i_send, i_recv, t_send, t_recv, v_send, v_recv,
):
    f = lax.axis_index("fsdp")
    t = lax.axis_index("tile")
    lo = lax.axis_index("dp")
    x, h = f // 2, f % 2
    z, c = t // 2, t % 2
    xa, xb = x // 2, x % 2
    xe = (xa + xb) % 2
    ye = (h + lo) % 2
    za = z // 2
    ze = (za + z % 2) % 2
    keep = (c + xe) % 2
    active, passive = c == xa, c != xa
    mine = {1: keep, 2: h, 3: ye, 4: za, 5: ze}
    x_flip = x + 1 - 2 * xb
    z_flip = z + 1 - 2 * (z % 2)
    partner = {
        0: {"fsdp": (3 - x) * 2 + h},
        1: {"fsdp": x_flip * 2 + h},
        2: {"fsdp": x * 2 + 1 - h, "dp": 1 - lo},
        3: {"dp": 1 - lo},
        4: {"tile": (3 - z) * 2 + c},
        5: {"tile": z_flip * 2 + c},
    }
    other_core = {"tile": 2 * z + 1 - c}
    two_away = {"fsdp": (x + 2) % 4 * 2 + h}
    quarter = (z + 2 * ye) % 4
    holders = [
        {"tile": (z + k // 2) % 4 * 2 + c, "dp": (lo + k % 2) % 2} for k in range(1, 8)
    ]

    def remote(src, dst, send_sem, recv_sem, device):
        return pltpu.make_async_remote_copy(
            src_ref=src, dst_ref=dst, send_sem=send_sem, recv_sem=recv_sem,
            device_id=device, device_id_type=MESH,
        )

    barrier = pltpu.get_barrier_semaphore()
    for k in range(1, 8):
        pl.semaphore_signal(barrier, inc=1, device_id={"tile": (t + k) % 8}, device_id_type=MESH)
    frame = f * 2 + lo
    for k in range(1, 16):
        to = (frame + k) % 16
        pl.semaphore_signal(
            barrier, inc=1, device_id={"fsdp": to // 2, "dp": to % 2}, device_id_type=MESH
        )

    for k in (3, 5, 7):
        pl.semaphore_signal(barrier, inc=1, device_id=holders[k - 1], device_id_type=MESH)

    near, far = keep, 1 - keep
    own_x = pltpu.make_async_copy(feat, xs.at[1, pl.ds(1 + 2 * c, 2)], loc_sem.at[0])
    own_x.start()
    own_w = [
        pltpu.make_async_copy(
            weight.at[:, :, :, :, pl.ds(PCOLS * part, PCOLS)], wall.at[part, near, h], loc_sem.at[1 + part]
        )
        for part in range(PARTS)
    ]

    @pl.when(active)
    def _():
        for copy in own_w:
            copy.start()

    own_ct = []
    for k in range(2):
        own_ct.append(
            pltpu.make_async_copy(cot.at[2 * k + c], ctv.at[2 * c + k], loc_sem.at[7 + k])
        )
        own_ct[-1].start()

    own_x.wait()
    for k in range(2):
        for lane in range(4):
            at = pl.ds(128 * lane, 128)
            row = xs[1, 1 + 2 * c + k, :, at].astype(jnp.float32) + shift_row_in[:, at]
            xs[1, 1 + 2 * c + k, :, at] = row.astype(jnp.bfloat16)

    pl.semaphore_wait(barrier, 25)

    def same(pair, half, number, send_sem, recv_sem, device, eighth=None):
        place = wall.at[:, pair, half, number // 2, number % 2]
        if eighth is not None:
            place = wall.at[:, pair, half, number // 2, number % 2, eighth]
        return remote(place, place, send_sem, recv_sem, device)

    turn = [(quarter + k) % 4 for k in range(4)]
    to_flip = [same(near, h, turn[k], o_send.at[k], o_recv.at[k], partner[1]) for k in range(4)]
    to_turn = [same(near, h, turn[k], o_send.at[3 + k], o_recv.at[3 + k], partner[0]) for k in range(1, 4)]
    first_turn = [same(near, h, quarter, o_send.at[9 + e], o_recv.at[9 + e], partner[0], e) for e in range(2)]
    relay = [same(near, h, quarter, o_send.at[7 + e], o_recv.at[7 + e], partner[1], e) for e in range(2)]
    from_flip = [same(far, h, turn[k], o_send.at[k], o_recv.at[k], partner[1]) for k in range(4)]
    from_far = [same(far, h, quarter, o_send.at[7 + e], o_recv.at[7 + e], partner[1], e) for e in range(2)]
    across = [same(near, h, quarter, n_send.at[e], n_recv.at[e], partner[2], e) for e in range(2)]
    crossed = [same(near, 1 - h, quarter, n_send.at[e], n_recv.at[e], partner[2], e) for e in range(2)]
    across_far = same(far, h, quarter, n_send.at[2], n_recv.at[2], partner[2])
    crossed_far = same(far, 1 - h, quarter, n_send.at[2], n_recv.at[2], partner[2])
    passed = {}
    theirs = {3: (quarter + 2) % 4, 4: (3 - z + 2 * ye) % 4, 5: (z_flip + 2 * ye) % 4}
    for k, (pair, half, e) in enumerate(((near, 1 - h, 0), (near, 1 - h, 1), (far, 1 - h, None), (far, h, None))):
        for j, dim in enumerate((3, 4, 5)):
            passed[k, j] = (
                same(pair, half, quarter, q_send.at[k, j], q_recv.at[k, j], partner[dim], e),
                same(pair, half, theirs[dim], q_send.at[k, j], q_recv.at[k, j], partner[dim], e),
            )

    def pass_on(k):
        for j in range(3):
            passed[k, j][0].start()

    def passed_in(k):
        for j in range(3):
            passed[k, j][1].wait_recv()

    @pl.when(active)
    def _():
        for copy in own_w:
            copy.wait()
        for e in range(2):
            first_turn[e].start()
            across[e].start()
        to_flip[0].start()

    x_pair = remote(
        xs.at[1, pl.ds(1 + 2 * c, 2)], xs.at[1, pl.ds(1 + 2 * c, 2)], x_send.at[0], x_recv.at[0], other_core
    )
    x_pair_in = remote(
        xs.at[1, pl.ds(3 - 2 * c, 2)], xs.at[1, pl.ds(3 - 2 * c, 2)], x_send.at[0], x_recv.at[0], other_core
    )
    rim_cols = WIDTH // 2
    sends_rim = jnp.where(c == 0, z > 0, z < 3)
    z_rim = jnp.where(c == 0, jnp.maximum(z - 1, 0), jnp.minimum(z + 1, 3))
    rim_out = [
        remote(
            xs.at[1, 1 + 3 * c, pl.ds(rim_cols * k, rim_cols)],
            xs.at[1, 5 - 5 * c, pl.ds(rim_cols * k, rim_cols)],
            x_send.at[1 + k], x_recv.at[1 + c], {"tile": 2 * z_rim + k},
        )
        for k in range(2)
    ]

    def rim_part(row, core, sem):
        at = xs.at[1, row, pl.ds(pl.multiple_of(rim_cols * core, rim_cols), rim_cols)]
        return remote(at, at, x_send.at[sem], x_recv.at[sem], other_core)

    top_in, bottom_in = rim_part(0, c, 2), rim_part(5, c, 1)
    top_swap, bottom_swap = rim_part(0, c, 5), rim_part(5, c, 6)
    top_swapped, bottom_swapped = rim_part(0, 1 - c, 5), rim_part(5, 1 - c, 6)

    @pl.when(sends_rim)
    def _():
        for copy in rim_out:
            copy.start()

    x_pair.start()

    ct_pair = []
    for k in range(2):
        ct_pair.append(
            remote(cot.at[2 * k + 1 - c], ctv.at[2 * c + k], x_send.at[3 + k], x_recv.at[3 + k], other_core)
        )
        ct_pair[-1].start()

    @pl.when(z == 0)
    def _():
        xs[1, 0] = jnp.zeros((WIDTH, CIN), jnp.bfloat16)
        ss[1, 0] = jnp.zeros((WIDTH, HALF), jnp.bfloat16)

    @pl.when(z == 3)
    def _():
        xs[1, 5] = jnp.zeros((WIDTH, CIN), jnp.bfloat16)
        ss[1, 5] = jnp.zeros((WIDTH, HALF), jnp.bfloat16)

    column = lax.broadcasted_iota(jnp.int32, (WIDTH, 128), 0)

    def shift_row(ref, row):
        for lane in range(4):
            at = pl.ds(128 * lane, 128)
            values = ref[1, row, :, at].astype(jnp.float32)
            right = jnp.where(column == 0, 0.0, pltpu.roll(values, 1, 0))
            left = jnp.where(column == WIDTH - 1, 0.0, pltpu.roll(values, WIDTH - 1, 0))
            ref[0, row, :, at] = right.astype(jnp.bfloat16)
            ref[2, row, :, at] = left.astype(jnp.bfloat16)

    def shift_rows(ref, first, count):
        @pl.loop(0, count)
        def _(k):
            shift_row(ref, first + k)

    @pl.when(active)
    def _():
        for e in range(2):
            first_turn[e].wait_send()
        to_turn[0].start()

    shift_rows(xs, 1 + 2 * c, 2)

    @pl.when(active)
    def _():
        for e in range(2):
            crossed[e].wait_recv()
            pass_on(e)
        for k in range(1, 3):
            to_turn[k].start()
        to_flip[1].start()

    @pl.when(passive)
    def _():
        for e in range(2):
            first_turn[e].wait_recv()
            across[e].start()
            relay[e].start()

    x_pair_in.wait_recv()
    shift_rows(xs, 3 - 2 * c, 2)

    @pl.when(z > 0)
    def _():
        top_in.wait_recv()
        top_swap.start()

    @pl.when(z < 3)
    def _():
        bottom_in.wait_recv()
        bottom_swap.start()

    @pl.when(passive)
    def _():
        for e in range(2):
            crossed[e].wait_recv()
            pass_on(e)

    for copy in own_ct:
        copy.wait()
    for copy in ct_pair:
        copy.wait_recv()

    @pl.loop(0, 4)
    def _(r):
        for lane in range(2):
            wide[lane] = ctv[r, :, 128 * lane : 128 * lane + 128].astype(jnp.float32)
        for v in range(2):
            for lane in range(2):
                cts[v, r, :, 128 * lane : 128 * lane + 128] = wide[lane, pl.ds(v, WIDTH, 2), :].astype(jnp.bfloat16)

    @pl.when(z > 0)
    def _():
        top_swapped.wait_recv()

    @pl.when(z < 3)
    def _():
        bottom_swapped.wait_recv()

    shift_rows(xs, 0, 1)
    shift_rows(xs, 5, 1)

    @pl.when(active)
    def _():
        from_flip[0].wait_recv()
        across_far.start()
        for k in range(2, 4):
            to_flip[k].start()

    @pl.when(passive)
    def _():
        for copy in from_far:
            copy.wait_recv()
        across_far.start()
        pass_on(3)

    def forward_row(v, r):
        lhs = jnp.concatenate(
            [
                xs[(kk // 2) % 3, r + kk // 6, :, 256 * (kk % 2) : 256 * (kk % 2) + 256]
                for kk in range(CHUNKS)
            ],
            axis=1,
        )
        rhs = jnp.concatenate(
            [
                wall[kk // 3, v, :, :, :, :, :, 256 * (kk % 3) : 256 * (kk % 3) + 256].reshape(256, 256)
                for kk in range(CHUNKS)
            ],
            axis=1,
        )
        acc[...] = lax.dot_general(
            lhs, rhs, (((1,), (1,)), ((), ())), preferred_element_type=jnp.float32
        )

        @pl.loop(0, WIDTH // 32)
        def _(j):
            rows = pl.ds(pl.multiple_of(j * 32, 32), 32)
            value = acc[rows]
            grown = 0.5 * (1.0 + lax.erf(value * inv_root_two))
            slope = grown + value * jnp.exp(-0.5 * value * value) * inv_root_tau
            actv[v, r, rows] = (value * grown).astype(jnp.bfloat16)
            out = pl.ds(pl.multiple_of(256 * v, 256), 256)
            ss[1, r + 1, rows, out] = (cts[v, r, rows].astype(jnp.float32) * slope).astype(jnp.bfloat16)

    def at(part, fixed):
        return (part,) + tuple(fixed.get(d, slice(None)) for d in range(1, 6)) + (slice(None), lanes_of(part))

    def lanes_of(part):
        return pl.ds(0, 256 * SPANS[part][1])

    def in_slot(slots, slot):
        return slot + (slice(None),) * (len(slots.shape) - 1 - len(slot)) + (lanes_of(slot[0]),)

    def when(condition, body):
        if condition is None:
            body()
        else:
            pl.when(condition)(body)

    two_y = {"fsdp": x * 2 + 1 - h}
    two_z = {"tile": (z + 2) % 4 * 2 + c}

    halves, seconds, thirds, fourths = {}, {}, {}, {}

    def half_copy(part, n, dim, there, sends):
        place = at(part, there)
        return (
            sends,
            remote(gwb.at[place], got0.at[place], r_send.at[part, n], r_recv.at[part, n], partner[dim]),
        )

    def second_copy(part, n, dim, there, sends):
        place = at(part, there)
        return (
            sends,
            remote(
                gwb.at[place], got1.at[place], r_send.at[part, 2 + n], r_recv.at[part, 2 + n], partner[dim]
            ),
        )

    def slot_copy(part, there, slots, slot, sem, device, sends):
        return (
            sends,
            remote(
                gwb.at[at(part, there)], slots.at[in_slot(slots, slot)], r_send.at[part, sem], r_recv.at[part, sem], device
            ),
            slot,
        )

    def flips(axis):
        da, db = 2 * axis, 2 * axis + 1
        there = {da: 1 - mine[da], db: 1 - mine[db]}
        return (
            ({da: there[da], db: mine[db]}, partner[da]),
            ({da: mine[da], db: there[db]}, partner[db]),
            (there, two_y if axis == 1 else two_z),
        )

    def along_x(part, kept, slots, sem):
        return [
            slot_copy(part, {**kept, 1: pair}, slots, (part, j), sem + j, device, sends)
            for j, (sends, pair, device) in enumerate(
                ((passive, near, partner[0]), (active, far, partner[1]), (passive, far, two_away))
            )
        ]

    for n, pair in enumerate((near, far)):
        halves[0, n] = (half_copy(0, n, 0, {1: pair}, passive), active, at(0, {1: pair}))
    seconds[0, 1] = (second_copy(0, 1, 1, {1: far}, active), active, at(0, {1: near}))
    across_x = [
        (
            sends,
            remote(
                gwb.at[at(1, {1: pair})], slots.at[at(1, {1: place})], r_send.at[1, j], r_recv.at[1, j], device
            ),
        )
        for j, (sends, pair, device, slots, place) in enumerate(
            (
                (passive, near, partner[0], got0, near),
                (active, far, partner[1], got1, far),
                (passive, far, two_away, got0, near),
            )
        )
    ]
    for part in (0, 1):
        thirds[part, 1] = (
            [
                slot_copy(part, {1: near, **there}, got2, (part, j), 7 + j, device, active)
                for j, (there, device) in enumerate(flips(1))
            ],
            active, at(part, {1: near, 2: h, 3: ye}),
        )
        fourths[part] = [
            slot_copy(part, {1: near, 2: h, 3: ye, **there}, got3, (part, j), 10 + j, device, active)
            for j, (there, device) in enumerate(flips(2))
        ]
    for part in range(2, 6):
        one, two = FIRST[part]
        first = {one: mine[one]}
        both = {**first, two: mine[two]}
        for n, pair in enumerate((near, far)):
            halves[part, n] = (
                half_copy(part, n, one, {1: pair, one: 1 - mine[one]}, None),
                None, at(part, {1: pair, **first}),
            )
            seconds[part, n] = (
                second_copy(part, n, two, {1: pair, **first, two: 1 - mine[two]}, None),
                None, at(part, {1: pair, **both}),
            )
            if part < 4:
                thirds[part, n] = (
                    [
                        slot_copy(
                            part, {1: pair, **both, **there}, got2, (part, j, 0, pair), 4 + 3 * n + j, device, None
                        )
                        for j, (there, device) in enumerate(flips(2))
                    ],
                    None, at(part, {1: pair, **both, 4: za, 5: ze}),
                )
        if part < 4:
            fourths[part] = along_x(part, {**both, 4: za, 5: ze}, got3, 10)
        else:
            copies = along_x(part, both, got2, 4)
            thirds[part, 0] = ([copies[0]], None, None)
            thirds[part, 1] = (copies, active, at(part, {**both, 1: near}))
            fourths[part] = [
                slot_copy(part, {1: near, **both, **there}, got3, (part, j), 10 + j, device, active)
                for j, (there, device) in enumerate(flips(1))
            ]

    def add_across():
        def add():
            for _, copy in across_x:
                copy.wait_recv()
            here, there = at(1, {1: near}), at(1, {1: far})
            total = gwb[here].astype(jnp.float32) + got0[here].astype(jnp.float32)
            total = total + got1[here].astype(jnp.float32) + got0[there].astype(jnp.float32)
            gwb[here] = total.astype(jnp.bfloat16)

        pl.when(active)(add)
        for sends, copy, _ in thirds[1, 1][0]:
            when(sends, copy.start)

    def add_half(part, n):
        if (part, n) in halves:
            (_, copy), receives, here = halves[part, n]

            def add():
                copy.wait_recv()
                total = gwb[here].astype(jnp.float32) + got0[here].astype(jnp.float32)
                gwb[here] = total.astype(jnp.bfloat16)

            when(receives, add)
        if (part, n) in seconds:
            when(seconds[part, n][0][0], seconds[part, n][0][1].start)

    def add_second(part, n):
        if (part, n) not in seconds:
            return
        (_, copy), receives, here = seconds[part, n]

        def add():
            copy.wait_recv()
            total = gwb[here].astype(jnp.float32) + got1[here].astype(jnp.float32)
            gwb[here] = total.astype(jnp.bfloat16)

        when(receives, add)
        entry = thirds[part, n][0]
        for sends, copy, _ in entry[1:] if part >= 4 and n == 1 else entry:
            when(sends, copy.start)

    def add_third(part):
        for n in range(2):
            if (part, n) in thirds and thirds[part, n][2] is not None:
                entry, receives, here = thirds[part, n]

                def add(entry=entry, here=here):
                    total = gwb[here].astype(jnp.float32)
                    for _, copy, slot in entry:
                        copy.wait_recv()
                        total = total + got2[in_slot(got2, slot)].astype(jnp.float32)
                    gwb[here] = total.astype(jnp.bfloat16)

                when(receives, add)
        for sends, copy, _ in fourths[part]:
            when(sends, copy.start)

    def add_fourth(part):
        here = at(part, {1: near, 2: h, 3: ye, 4: za, 5: ze})

        def add():
            total = gwb[here].astype(jnp.float32)
            for _, copy, slot in fourths[part]:
                copy.wait_recv()
                total = total + got3[in_slot(got3, slot)].astype(jnp.float32)
            total = total.astype(jnp.bfloat16)
            first, count = SPANS[part]
            fin[ye, za, ze, :, 256 * first : 256 * (first + count)] = total

        pl.when(active)(add)

    def weight_gradient(pair, order):
        n = 0 if pair is near else 1
        lanes = pl.ds(pl.multiple_of(256 * pair, 256), 256)
        for r in range(4):
            st[:, WIDTH * r : WIDTH * r + WIDTH] = ss[1, r + 1, :, lanes].T
        for run in order:
            for part in run:
                first, count = SPANS[part]
                for j in range(count):
                    kk = first + j
                    window = xs[(kk // 2) % 3, kk // 6 : kk // 6 + 4, :, 256 * (kk % 2) : 256 * (kk % 2) + 256]
                    term = jnp.dot(
                        st[...], window.reshape(4 * WIDTH, 256), preferred_element_type=jnp.float32
                    )
                    gwb[part, pair, :, :, :, :, :, 256 * j : 256 * j + 256] = term.astype(jnp.bfloat16).reshape(
                        2, 2, 2, 2, 16, 256
                    )
            for part in run:
                if (part, n) in halves:
                    sends, copy = halves[part, n][0]
                    when(sends, copy.start)
                if part == 1:
                    for sends, copy in across_x[1:] if n else across_x[:1]:
                        when(sends, copy.start)

    passed_in(0)
    passed_in(1)

    @pl.when(passive)
    def _():
        for copy in to_turn:
            copy.wait_recv()

    @pl.loop(0, 4)
    def _(r):
        @pl.when(r == jnp.where(active, 3, 2))
        def _():
            crossed_far.wait_recv()
            pass_on(2)

        forward_row(near, r)

    weight_gradient(near, NEAR_RUNS)

    passed_in(2)

    @pl.when(passive)
    def _():
        passed_in(3)

    @pl.when(active)
    def _():
        for k in range(1, 4):
            from_flip[k].wait_recv()

    @pl.loop(0, 2)
    def _(k):
        forward_row(far, 3 * k)

    rim_above = remote(ss.at[1, 0], ss.at[1, 0], s_send.at[1], s_recv.at[1], other_core)
    rim_below = remote(ss.at[1, 5], ss.at[1, 5], s_send.at[0], s_recv.at[0], other_core)
    slope_up = remote(ss.at[1, 1], ss.at[1, 5], s_send.at[0], s_recv.at[0], {"tile": 2 * jnp.maximum(z - 1, 0) + c})
    slope_down = remote(ss.at[1, 4], ss.at[1, 0], s_send.at[1], s_recv.at[1], {"tile": 2 * jnp.minimum(z + 1, 3) + c})
    pl.when(z > 0)(slope_up.start)
    pl.when(z < 3)(slope_down.start)

    @pl.loop(0, 2)
    def _(k):
        forward_row(far, 2 - k)

    for part in (0, 2, 3, 4, 5):
        add_half(part, 0)
    weight_gradient(far, FAR_RUNS)

    shift_rows(ss, 1, 4)

    def input_row(r, out):
        lhs = jnp.concatenate([ss[2 - tap % 3, r + 2 - tap // 3] for tap in range(9)], axis=1)
        for e in range(2):
            chunks = []
            for tap in range(9):
                kk = 2 * tap + e
                chunks.append(
                    wall[kk // 3, :, :, :, :, :, :, 256 * (kk % 3) : 256 * (kk % 3) + 256].reshape(512, 256)
                )
            out[:, 256 * e : 256 * e + 256] = jnp.dot(
                lhs, jnp.concatenate(chunks, axis=0), preferred_element_type=jnp.float32
            )

    @pl.loop(0, 2)
    def _(k):
        @pl.when(k == 1)
        def _():
            pl.when(z > 0)(rim_above.wait_recv)
            pl.when(z < 3)(rim_below.wait_recv)
            shift_row(ss, 0)
            shift_row(ss, 5)

        r = jnp.where(k == 0, 2 - c, 3 - 3 * c)
        input_row(r, igp.at[r - 2 * (1 - c)])


    ig_pair = remote(igp, igr, i_send.at[0], i_recv.at[0], other_core)
    ig_pair.start()
    for part in range(2, 6):
        add_second(part, 0)
    for part in (0, 2, 3, 4, 5):
        add_half(part, 1)
    add_across()

    trow[4:8, :] = jnp.full((4, 128), frame_id[0], jnp.int32).astype(jnp.float32)
    trow[0:4, :] = jnp.zeros((4, 128), jnp.float32)

    @pl.loop(0, 2)
    def _(k):
        input_row(2 * c + k, igo.at[k])

    for part in ORDER:
        add_second(part, 1)

    ig_pair.wait_recv()

    @pl.loop(0, 2)
    def _(k):
        total = igo[k] + igr[k]
        gfb[k] = total.astype(jnp.bfloat16)
        column_sum = jnp.sum(total, axis=0, keepdims=True)
        for lane in range(4):
            trow[lane : lane + 1, :] += column_sum[:, 128 * lane : 128 * lane + 128]

    gf_copy = pltpu.make_async_copy(gfb, gf_out, loc_sem.at[11])
    gf_copy.start()

    t_copies = []
    for k in range(1, 8):
        copy = remote(trow, tpeer.at[k - 1], t_send.at[k - 1], t_recv.at[k - 1], {"tile": (t + k) % 8})
        copy.start()
        t_copies.append(copy)

    @pl.loop(0, 4)
    def _(r):
        for lane in range(2):
            lanes = pl.ds(128 * lane, 128)
            for v in range(2):
                wide[lane, pl.ds(v, WIDTH, 2), :] = actv[v, r, :, lanes].astype(jnp.float32)
            upb[r, :, lanes] = wide[lane].astype(jnp.bfloat16)

    up_own, up_pair = [], []
    for k in range(2):
        up_own.append(pltpu.make_async_copy(upb.at[2 * c + k], up_out.at[2 * k + c], loc_sem.at[9 + k]))
        up_pair.append(
            remote(upb.at[2 * (1 - c) + k], up_out.at[2 * k + c], u_send.at[k], u_recv.at[k], other_core)
        )
        up_own[-1].start()
        up_pair[-1].start()

    for part in ORDER:
        add_third(part)

    for copy in t_copies:
        copy.wait_recv()
    for copy in t_copies:
        copy.wait_send()
    total = trow[0:4, :]
    for k in range(7):
        total = total + tpeer[k, 0:4, :]
    tall[0, 0:4, :] = total
    tall[0, 4:8, :] = trow[4:8, :]
    y = 2 * h + lo
    v_copies = []
    for k in range(1, 4):
        to = (y + k) % 4
        v_copies.append(
            remote(tall.at[0], tall.at[k], v_send.at[k - 1], v_recv.at[k - 1], {"fsdp": 2 * x + to // 2, "dp": to % 2})
        )
    for k in range(1, 4):
        to = (x + k) % 4
        v_copies.append(
            remote(
                tall.at[pl.ds(0, 4)], tall.at[pl.ds(4 * k, 4)], v_send.at[2 + k], v_recv.at[2 + k], {"fsdp": 2 * to + h}
            )
        )
    for copy in v_copies[:3]:
        copy.start()

    spreads, to_pair, to_self = [], [], []
    for g in range(2):
        first, last = SPANS[3 * g][0], SPANS[3 * g + 2][0] + SPANS[3 * g + 2][1]
        cols = pl.ds(256 * first, 256 * (last - first))
        piece_at = fin.at[ye, za, ze, :, cols]
        spreads.append(
            [remote(piece_at, piece_at, f_send.at[g, k], f_recv.at[g, k], holders[k]) for k in range(7)]
        )
        held, out = fin.at[:, :, :, :, cols], gw_out.at[:, :, :, :, cols]
        to_pair.append(remote(held, out, i_send.at[1 + g], i_recv.at[1 + g], other_core))
        to_self.append(pltpu.make_async_copy(held, out, loc_sem.at[12 + g]))

    for g in range(2):
        for part in range(3 * g, 3 * g + 3):
            add_fourth(part)

        @pl.when(active)
        def _(g=g):
            for copy in spreads[g]:
                copy.start()

    for copy in v_copies[:3]:
        copy.wait_recv()
    for copy in v_copies[3:]:
        copy.start()

    @pl.when(active)
    def _():
        for g in range(2):
            for copy in spreads[g]:
                copy.wait_recv()
            to_pair[g].start()
            to_self[g].start()
        for g in range(2):
            for copy in spreads[g]:
                copy.wait_send()
            to_self[g].wait()
            to_pair[g].wait_send()

    @pl.when(c != xa)
    def _():
        for g in range(2):
            to_pair[g].wait_recv()

    for copy in v_copies[3:]:
        copy.wait_recv()
    for copy in v_copies:
        copy.wait_send()
    tab_copy = pltpu.make_async_copy(tall, tab_out, loc_sem.at[14])
    tab_copy.start()

    @pl.when(active)
    def _():
        for copy in to_turn + to_flip:
            copy.wait_send()

    @pl.when(passive)
    def _():
        for copy in relay:
            copy.wait_send()
        for j in range(3):
            passed[3, j][0].wait_send()

    for copy in across + [across_far]:
        copy.wait_send()
    for k in range(3):
        for j in range(3):
            passed[k, j][0].wait_send()

    @pl.when(z > 0)
    def _():
        top_swap.wait_send()

    @pl.when(z < 3)
    def _():
        bottom_swap.wait_send()

    for (sends, copy), _, _ in list(halves.values()) + list(seconds.values()):
        when(sends, copy.wait_send)
    for sends, copy in across_x:
        when(sends, copy.wait_send)
    for (part, n), (entry, _, _) in thirds.items():
        for sends, copy, _ in entry[1:] if part >= 4 and n == 1 else entry:
            when(sends, copy.wait_send)
    for entry in fourths.values():
        for sends, copy, _ in entry:
            when(sends, copy.wait_send)
    x_pair.wait_send()

    @pl.when(sends_rim)
    def _():
        for copy in rim_out:
            copy.wait_send()

    for copy in ct_pair:
        copy.wait_send()
    pl.when(z > 0)(slope_up.wait_send)
    pl.when(z < 3)(slope_down.wait_send)
    for k in range(2):
        up_own[k].wait()
        up_pair[k].wait()
    ig_pair.wait_send()
    gf_copy.wait()
    tab_copy.wait()


def fused(features, weight, cot, shift_row, frame_id):
    any_space = pl.BlockSpec(memory_space=pl.ANY)
    vmem = pl.BlockSpec(memory_space=pltpu.VMEM)
    bf16, f32 = jnp.bfloat16, jnp.float32
    dma = pltpu.SemaphoreType.DMA
    return pl.pallas_call(
        kernel,
        out_shape=(
            jax.ShapeDtypeStruct((4, 2 * WIDTH, 256), bf16),
            jax.ShapeDtypeStruct((2, 2, 2, 16, 9 * CIN), bf16),
            jax.ShapeDtypeStruct((2, WIDTH, CIN), bf16),
            jax.ShapeDtypeStruct((16, 8, 128), f32),
        ),
        in_specs=[any_space, any_space, any_space, vmem, pl.BlockSpec(memory_space=pltpu.SMEM)],
        out_specs=[any_space] * 4,
        scratch_shapes=[
            pltpu.VMEM((3, 6, WIDTH, CIN), bf16),
            pltpu.VMEM((3, 6, WIDTH, HALF), bf16),
            pltpu.VMEM((256, 4 * WIDTH), bf16),
            pltpu.VMEM((PARTS, 2, 2, 2, 2, 2, 16, PCOLS), bf16),
            pltpu.VMEM((PARTS, 2, 2, 2, 2, 2, 16, GCOLS), bf16),
            pltpu.VMEM((PARTS, 2, 2, 2, 2, 2, 16, GCOLS), bf16),
            pltpu.VMEM((PARTS, 2, 2, 2, 2, 2, 16, GCOLS), bf16),
            pltpu.VMEM((PARTS, 3, 2, 2, 16, GCOLS), bf16),
            pltpu.VMEM((PARTS, 3, 16, GCOLS), bf16),
            pltpu.VMEM((2, 2, 2, 16, 9 * CIN), bf16),
            pltpu.VMEM((4, 2 * WIDTH, 256), bf16),
            pltpu.VMEM((2, 4, WIDTH, 256), bf16),
            pltpu.VMEM((2, 4, WIDTH, 256), bf16),
            pltpu.VMEM((4, 2 * WIDTH, 256), bf16),
            pltpu.VMEM((2, 2 * WIDTH, 128), f32),
            pltpu.VMEM((WIDTH, 256), f32),
            pltpu.VMEM((2, WIDTH, CIN), f32),
            pltpu.VMEM((2, WIDTH, CIN), f32),
            pltpu.VMEM((2, WIDTH, CIN), f32),
            pltpu.VMEM((2, WIDTH, CIN), bf16),
            pltpu.VMEM((8, 128), f32),
            pltpu.VMEM((7, 8, 128), f32),
            pltpu.VMEM((16, 8, 128), f32),
            dma((15,)),
            dma((7,)),
            dma((7,)),
            dma((11,)),
            dma((11,)),
            dma((3,)),
            dma((3,)),
            dma((4, 3)),
            dma((4, 3)),
            dma((2,)),
            dma((2,)),
            dma((PARTS, 13)),
            dma((PARTS, 13)),
            dma((2, 7)),
            dma((2, 7)),
            dma((2,)),
            dma((2,)),
            dma((3,)),
            dma((3,)),
            dma((7,)),
            dma((7,)),
            dma((6,)),
            dma((6,)),
        ],
        compiler_params=pltpu.CompilerParams(
            collective_id=0, has_side_effects=True, vmem_limit_bytes=60 * 2**20
        ),
        cost_estimate=pl.CostEstimate(
            flops=6 * 768 * 4608 * 1024, bytes_accessed=2 * 10**7, transcendentals=3 * 768 * 1024
        ),
        name="conv_block",
    )(features, weight, cot, shift_row, frame_id)


def shards(features, frame_table, frame_ids, conv_weight, cotangent):
    video_len = frame_table.shape[0]
    shift = lax.dynamic_slice_in_dim(frame_table, frame_ids[0], 1, axis=0).astype(jnp.float32)
    up, gw, gf, tab = fused(
        features[0], conv_weight.reshape(2, 2, 2, 16, 9 * CIN), cotangent[0], shift, frame_ids
    )
    sums = tab[:, :4].reshape(16, CIN)
    frames = tab[:, 4, 0]
    picker = (frames[:, None] == jnp.arange(video_len, dtype=jnp.float32)[None, :]).astype(jnp.float32)
    grad_table = lax.dot_general(
        picker, sums, (((0,), (0,)), ((), ())),
        precision=lax.Precision.HIGH, preferred_element_type=jnp.float32,
    )
    grad_weight = gw.reshape(128, 9 * CIN).astype(jnp.float32)
    return (up[None], grad_weight, gf[None], grad_table)


def solution(mesh):
    return jax.shard_map(
        shards,
        mesh=mesh,
        in_specs=(
            P(("fsdp", "dp"), "tile", None, None),
            P(),
            P(("fsdp", "dp")),
            P("fsdp", None),
            P(("fsdp", "dp"), "tile", None, None),
        ),
        out_specs=(
            P(("fsdp", "dp"), "tile", None, None),
            P("fsdp", None),
            P(("fsdp", "dp"), "tile", None, None),
            P(),
        ),
        check_vma=False,
    )
```

```python
import jax
import jax.numpy as jnp
from jax import lax
from jax.experimental import pallas as pl
from jax.experimental.pallas import tpu as pltpu
from jax.sharding import PartitionSpec as P

inv_root_two = 0.7071067811865476
inv_root_tau = 0.3989422804014327

WIDTH = 384
CIN = 512
HALF = 512
PARTS = 6
PCOLS = 768
CHUNKS = 18

DIMS = 6

FIRST = [None, None, (2, 3), (3, 2), (4, 5), (5, 4)]
NEAR_RUNS = ((0, 1, 2, 3, 4, 5),)
FAR_RUNS = ((0, 1), (2, 3), (4, 5))
SPANS = ((0, 2), (2, 2), (4, 4), (8, 4), (12, 3), (15, 3))
GCOLS = 1024

MESH = pl.DeviceIdType.MESH


def kernel(
    feat, weight, cot, shift_row_in, frame_id,
    up_out, gw_out, gf_out, tab_out,
    xs, ss, st, wall, gwb, got0, got1, got2, got3, fin, ctv, cts, actv, upb, wide, acc, igp, igo, igr, gfb,
    trow, tpeer, tall,
    loc_sem, x_send, x_recv, o_send, o_recv, n_send, n_recv, q_send, q_recv, s_send, s_recv,
    r_send, r_recv, f_send, f_recv, u_send, u_recv, i_send, i_recv, t_send, t_recv, v_send, v_recv,
):
    f = lax.axis_index("fsdp")
    t = lax.axis_index("tile")
    lo = lax.axis_index("dp")
    x, h = f // 2, f % 2
    z, c = t // 2, t % 2
    xa, xb = x // 2, x % 2
    xe = (xa + xb) % 2
    ye = (h + lo) % 2
    za = z // 2
    ze = (za + z % 2) % 2
    keep = (c + xe) % 2
    active, passive = c == xa, c != xa
    mine = {1: keep, 2: h, 3: ye, 4: za, 5: ze}
    x_flip = x + 1 - 2 * xb
    z_flip = z + 1 - 2 * (z % 2)
    partner = {
        0: {"fsdp": (3 - x) * 2 + h},
        1: {"fsdp": x_flip * 2 + h},
        2: {"fsdp": x * 2 + 1 - h, "dp": 1 - lo},
        3: {"dp": 1 - lo},
        4: {"tile": (3 - z) * 2 + c},
        5: {"tile": z_flip * 2 + c},
    }
    other_core = {"tile": 2 * z + 1 - c}
    two_away = {"fsdp": (x + 2) % 4 * 2 + h}
    quarter = (z + 2 * ye) % 4
    holders = [
        {"tile": (z + k // 2) % 4 * 2 + c, "dp": (lo + k % 2) % 2} for k in range(1, 8)
    ]

    def remote(src, dst, send_sem, recv_sem, device):
        return pltpu.make_async_remote_copy(
            src_ref=src, dst_ref=dst, send_sem=send_sem, recv_sem=recv_sem,
            device_id=device, device_id_type=MESH,
        )

    barrier = pltpu.get_barrier_semaphore()
    for k in range(1, 8):
        pl.semaphore_signal(barrier, inc=1, device_id={"tile": (t + k) % 8}, device_id_type=MESH)
    frame = f * 2 + lo
    for k in range(1, 16):
        to = (frame + k) % 16
        pl.semaphore_signal(
            barrier, inc=1, device_id={"fsdp": to // 2, "dp": to % 2}, device_id_type=MESH
        )

    for k in (3, 5, 7):
        pl.semaphore_signal(barrier, inc=1, device_id=holders[k - 1], device_id_type=MESH)

    near, far = keep, 1 - keep
    own_x = pltpu.make_async_copy(feat, xs.at[1, pl.ds(1 + 2 * c, 2)], loc_sem.at[0])
    own_x.start()
    own_w = [
        pltpu.make_async_copy(
            weight.at[:, :, :, :, pl.ds(PCOLS * part, PCOLS)], wall.at[part, near, h], loc_sem.at[1 + part]
        )
        for part in range(PARTS)
    ]

    @pl.when(active)
    def _():
        for copy in own_w:
            copy.start()

    own_ct = []
    for k in range(2):
        own_ct.append(
            pltpu.make_async_copy(cot.at[2 * k + c], ctv.at[2 * c + k], loc_sem.at[7 + k])
        )
        own_ct[-1].start()

    own_x.wait()
    for k in range(2):
        for lane in range(4):
            at = pl.ds(128 * lane, 128)
            row = xs[1, 1 + 2 * c + k, :, at].astype(jnp.float32) + shift_row_in[:, at]
            xs[1, 1 + 2 * c + k, :, at] = row.astype(jnp.bfloat16)

    pl.semaphore_wait(barrier, 25)

    def same(pair, half, number, send_sem, recv_sem, device, eighth=None):
        place = wall.at[:, pair, half, number // 2, number % 2]
        if eighth is not None:
            place = wall.at[:, pair, half, number // 2, number % 2, eighth]
        return remote(place, place, send_sem, recv_sem, device)

    turn = [(quarter + k) % 4 for k in range(4)]
    to_flip = [same(near, h, turn[k], o_send.at[k], o_recv.at[k], partner[1]) for k in range(4)]
    to_turn = [same(near, h, turn[k], o_send.at[3 + k], o_recv.at[3 + k], partner[0]) for k in range(1, 4)]
    first_turn = [same(near, h, quarter, o_send.at[9 + e], o_recv.at[9 + e], partner[0], e) for e in range(2)]
    relay = [same(near, h, quarter, o_send.at[7 + e], o_recv.at[7 + e], partner[1], e) for e in range(2)]
    from_flip = [same(far, h, turn[k], o_send.at[k], o_recv.at[k], partner[1]) for k in range(4)]
    from_far = [same(far, h, quarter, o_send.at[7 + e], o_recv.at[7 + e], partner[1], e) for e in range(2)]
    across = [same(near, h, quarter, n_send.at[e], n_recv.at[e], partner[2], e) for e in range(2)]
    crossed = [same(near, 1 - h, quarter, n_send.at[e], n_recv.at[e], partner[2], e) for e in range(2)]
    across_far = same(far, h, quarter, n_send.at[2], n_recv.at[2], partner[2])
    crossed_far = same(far, 1 - h, quarter, n_send.at[2], n_recv.at[2], partner[2])
    passed = {}
    theirs = {3: (quarter + 2) % 4, 4: (3 - z + 2 * ye) % 4, 5: (z_flip + 2 * ye) % 4}
    for k, (pair, half, e) in enumerate(((near, 1 - h, 0), (near, 1 - h, 1), (far, 1 - h, None), (far, h, None))):
        for j, dim in enumerate((3, 4, 5)):
            passed[k, j] = (
                same(pair, half, quarter, q_send.at[k, j], q_recv.at[k, j], partner[dim], e),
                same(pair, half, theirs[dim], q_send.at[k, j], q_recv.at[k, j], partner[dim], e),
            )

    def pass_on(k):
        for j in range(3):
            passed[k, j][0].start()

    def passed_in(k):
        for j in range(3):
            passed[k, j][1].wait_recv()

    @pl.when(active)
    def _():
        for copy in own_w:
            copy.wait()
        for e in range(2):
            first_turn[e].start()
            across[e].start()
        to_flip[0].start()

    x_pair = remote(
        xs.at[1, pl.ds(1 + 2 * c, 2)], xs.at[1, pl.ds(1 + 2 * c, 2)], x_send.at[0], x_recv.at[0], other_core
    )
    x_pair_in = remote(
        xs.at[1, pl.ds(3 - 2 * c, 2)], xs.at[1, pl.ds(3 - 2 * c, 2)], x_send.at[0], x_recv.at[0], other_core
    )
    rim_cols = WIDTH // 2
    sends_rim = jnp.where(c == 0, z > 0, z < 3)
    z_rim = jnp.where(c == 0, jnp.maximum(z - 1, 0), jnp.minimum(z + 1, 3))
    rim_out = [
        remote(
            xs.at[1, 1 + 3 * c, pl.ds(rim_cols * k, rim_cols)],
            xs.at[1, 5 - 5 * c, pl.ds(rim_cols * k, rim_cols)],
            x_send.at[1 + k], x_recv.at[1 + c], {"tile": 2 * z_rim + k},
        )
        for k in range(2)
    ]

    def rim_part(row, core, sem):
        at = xs.at[1, row, pl.ds(pl.multiple_of(rim_cols * core, rim_cols), rim_cols)]
        return remote(at, at, x_send.at[sem], x_recv.at[sem], other_core)

    top_in, bottom_in = rim_part(0, c, 2), rim_part(5, c, 1)
    top_swap, bottom_swap = rim_part(0, c, 5), rim_part(5, c, 6)
    top_swapped, bottom_swapped = rim_part(0, 1 - c, 5), rim_part(5, 1 - c, 6)

    @pl.when(sends_rim)
    def _():
        for copy in rim_out:
            copy.start()

    x_pair.start()

    ct_pair = []
    for k in range(2):
        ct_pair.append(
            remote(cot.at[2 * k + 1 - c], ctv.at[2 * c + k], x_send.at[3 + k], x_recv.at[3 + k], other_core)
        )
        ct_pair[-1].start()

    @pl.when(z == 0)
    def _():
        xs[1, 0] = jnp.zeros((WIDTH, CIN), jnp.bfloat16)
        ss[1, 0] = jnp.zeros((WIDTH, HALF), jnp.bfloat16)

    @pl.when(z == 3)
    def _():
        xs[1, 5] = jnp.zeros((WIDTH, CIN), jnp.bfloat16)
        ss[1, 5] = jnp.zeros((WIDTH, HALF), jnp.bfloat16)

    column = lax.broadcasted_iota(jnp.int32, (WIDTH, 128), 0)

    def shift_row(ref, row):
        for lane in range(4):
            at = pl.ds(128 * lane, 128)
            values = ref[1, row, :, at].astype(jnp.float32)
            right = jnp.where(column == 0, 0.0, pltpu.roll(values, 1, 0))
            left = jnp.where(column == WIDTH - 1, 0.0, pltpu.roll(values, WIDTH - 1, 0))
            ref[0, row, :, at] = right.astype(jnp.bfloat16)
            ref[2, row, :, at] = left.astype(jnp.bfloat16)

    def shift_rows(ref, first, count):
        @pl.loop(0, count)
        def _(k):
            shift_row(ref, first + k)

    @pl.when(active)
    def _():
        for e in range(2):
            first_turn[e].wait_send()
        to_turn[0].start()

    shift_rows(xs, 1 + 2 * c, 2)

    @pl.when(active)
    def _():
        for e in range(2):
            crossed[e].wait_recv()
            pass_on(e)
        for k in range(1, 3):
            to_turn[k].start()
        to_flip[1].start()

    @pl.when(passive)
    def _():
        for e in range(2):
            first_turn[e].wait_recv()
            across[e].start()
            relay[e].start()

    x_pair_in.wait_recv()
    shift_rows(xs, 3 - 2 * c, 2)

    @pl.when(z > 0)
    def _():
        top_in.wait_recv()
        top_swap.start()

    @pl.when(z < 3)
    def _():
        bottom_in.wait_recv()
        bottom_swap.start()

    @pl.when(passive)
    def _():
        for e in range(2):
            crossed[e].wait_recv()
            pass_on(e)

    for copy in own_ct:
        copy.wait()
    for copy in ct_pair:
        copy.wait_recv()

    @pl.loop(0, 4)
    def _(r):
        for lane in range(2):
            wide[lane] = ctv[r, :, 128 * lane : 128 * lane + 128].astype(jnp.float32)
        for v in range(2):
            for lane in range(2):
                cts[v, r, :, 128 * lane : 128 * lane + 128] = wide[lane, pl.ds(v, WIDTH, 2), :].astype(jnp.bfloat16)

    @pl.when(z > 0)
    def _():
        top_swapped.wait_recv()

    @pl.when(z < 3)
    def _():
        bottom_swapped.wait_recv()

    shift_rows(xs, 0, 1)
    shift_rows(xs, 5, 1)

    @pl.when(active)
    def _():
        from_flip[0].wait_recv()
        across_far.start()
        for k in range(2, 4):
            to_flip[k].start()

    @pl.when(passive)
    def _():
        for copy in from_far:
            copy.wait_recv()
        across_far.start()
        pass_on(3)

    def forward_row(v, r):
        lhs = jnp.concatenate(
            [
                xs[(kk // 2) % 3, r + kk // 6, :, 256 * (kk % 2) : 256 * (kk % 2) + 256]
                for kk in range(CHUNKS)
            ],
            axis=1,
        )
        rhs = jnp.concatenate(
            [
                wall[kk // 3, v, :, :, :, :, :, 256 * (kk % 3) : 256 * (kk % 3) + 256].reshape(256, 256)
                for kk in range(CHUNKS)
            ],
            axis=1,
        )
        acc[...] = lax.dot_general(
            lhs, rhs, (((1,), (1,)), ((), ())), preferred_element_type=jnp.float32
        )

        @pl.loop(0, WIDTH // 32)
        def _(j):
            rows = pl.ds(pl.multiple_of(j * 32, 32), 32)
            value = acc[rows]
            grown = 0.5 * (1.0 + lax.erf(value * inv_root_two))
            slope = grown + value * jnp.exp(-0.5 * value * value) * inv_root_tau
            actv[v, r, rows] = (value * grown).astype(jnp.bfloat16)
            out = pl.ds(pl.multiple_of(256 * v, 256), 256)
            ss[1, r + 1, rows, out] = (cts[v, r, rows].astype(jnp.float32) * slope).astype(jnp.bfloat16)

    def at(part, fixed):
        return (part,) + tuple(fixed.get(d, slice(None)) for d in range(1, 6)) + (slice(None), lanes_of(part))

    def lanes_of(part):
        return pl.ds(0, 256 * SPANS[part][1])

    def in_slot(slots, slot):
        return slot + (slice(None),) * (len(slots.shape) - 1 - len(slot)) + (lanes_of(slot[0]),)

    def when(condition, body):
        if condition is None:
            body()
        else:
            pl.when(condition)(body)

    two_y = {"fsdp": x * 2 + 1 - h}
    two_z = {"tile": (z + 2) % 4 * 2 + c}

    halves, seconds, thirds, fourths = {}, {}, {}, {}

    def half_copy(part, n, dim, there, sends):
        place = at(part, there)
        return (
            sends,
            remote(gwb.at[place], got0.at[place], r_send.at[part, n], r_recv.at[part, n], partner[dim]),
        )

    def second_copy(part, n, dim, there, sends):
        place = at(part, there)
        return (
            sends,
            remote(
                gwb.at[place], got1.at[place], r_send.at[part, 2 + n], r_recv.at[part, 2 + n], partner[dim]
            ),
        )

    def slot_copy(part, there, slots, slot, sem, device, sends):
        return (
            sends,
            remote(
                gwb.at[at(part, there)], slots.at[in_slot(slots, slot)], r_send.at[part, sem], r_recv.at[part, sem], device
            ),
            slot,
        )

    def flips(axis):
        da, db = 2 * axis, 2 * axis + 1
        there = {da: 1 - mine[da], db: 1 - mine[db]}
        return (
            ({da: there[da], db: mine[db]}, partner[da]),
            ({da: mine[da], db: there[db]}, partner[db]),
            (there, two_y if axis == 1 else two_z),
        )

    def along_x(part, kept, slots, sem):
        return [
            slot_copy(part, {**kept, 1: pair}, slots, (part, j), sem + j, device, sends)
            for j, (sends, pair, device) in enumerate(
                ((passive, near, partner[0]), (active, far, partner[1]), (passive, far, two_away))
            )
        ]

    across_x = {
        part: [
            (
                sends,
                remote(
                    gwb.at[at(part, {1: pair})], slots.at[at(part, {1: place})],
                    r_send.at[part, j], r_recv.at[part, j], device,
                ),
            )
            for j, (sends, pair, device, slots, place) in enumerate(
                (
                    (passive, near, partner[0], got0, near),
                    (active, far, partner[1], got1, far),
                    (passive, far, two_away, got0, near),
                )
            )
        ]
        for part in (0, 1)
    }
    for part in (0, 1):
        thirds[part, 1] = (
            [
                slot_copy(part, {1: near, **there}, got2, (part, j), 7 + j, device, active)
                for j, (there, device) in enumerate(flips(1))
            ],
            active, at(part, {1: near, 2: h, 3: ye}),
        )
        fourths[part] = [
            slot_copy(part, {1: near, 2: h, 3: ye, **there}, got3, (part, j), 10 + j, device, active)
            for j, (there, device) in enumerate(flips(2))
        ]
    for part in range(2, 6):
        one, two = FIRST[part]
        first = {one: mine[one]}
        both = {**first, two: mine[two]}
        for n, pair in enumerate((near, far)):
            halves[part, n] = (
                half_copy(part, n, one, {1: pair, one: 1 - mine[one]}, None),
                None, at(part, {1: pair, **first}),
            )
            seconds[part, n] = (
                second_copy(part, n, two, {1: pair, **first, two: 1 - mine[two]}, None),
                None, at(part, {1: pair, **both}),
            )
            if part < 4:
                thirds[part, n] = (
                    [
                        slot_copy(
                            part, {1: pair, **both, **there}, got2, (part, j, 0, pair), 4 + 3 * n + j, device, None
                        )
                        for j, (there, device) in enumerate(flips(2))
                    ],
                    None, at(part, {1: pair, **both, 4: za, 5: ze}),
                )
        if part < 4:
            fourths[part] = along_x(part, {**both, 4: za, 5: ze}, got3, 10)
        else:
            copies = along_x(part, both, got2, 4)
            thirds[part, 0] = ([copies[0]], None, None)
            thirds[part, 1] = (copies, active, at(part, {**both, 1: near}))
            fourths[part] = [
                slot_copy(part, {1: near, **both, **there}, got3, (part, j), 10 + j, device, active)
                for j, (there, device) in enumerate(flips(1))
            ]

    def add_across(part):
        def add():
            for _, copy in across_x[part]:
                copy.wait_recv()
            here, there = at(part, {1: near}), at(part, {1: far})
            total = gwb[here].astype(jnp.float32) + got0[here].astype(jnp.float32)
            total = total + got1[here].astype(jnp.float32) + got0[there].astype(jnp.float32)
            gwb[here] = total.astype(jnp.bfloat16)

        pl.when(active)(add)
        for sends, copy, _ in thirds[part, 1][0]:
            when(sends, copy.start)

    def add_half(part, n):
        if (part, n) in halves:
            (_, copy), receives, here = halves[part, n]

            def add():
                copy.wait_recv()
                total = gwb[here].astype(jnp.float32) + got0[here].astype(jnp.float32)
                gwb[here] = total.astype(jnp.bfloat16)

            when(receives, add)
        if (part, n) in seconds:
            when(seconds[part, n][0][0], seconds[part, n][0][1].start)

    def add_second(part, n):
        if (part, n) not in seconds:
            return
        (_, copy), receives, here = seconds[part, n]

        def add():
            copy.wait_recv()
            total = gwb[here].astype(jnp.float32) + got1[here].astype(jnp.float32)
            gwb[here] = total.astype(jnp.bfloat16)

        when(receives, add)
        entry = thirds[part, n][0]
        for sends, copy, _ in entry[1:] if part >= 4 and n == 1 else entry:
            when(sends, copy.start)

    def add_third(part):
        for n in range(2):
            if (part, n) in thirds and thirds[part, n][2] is not None:
                entry, receives, here = thirds[part, n]

                def add(entry=entry, here=here):
                    total = gwb[here].astype(jnp.float32)
                    for _, copy, slot in entry:
                        copy.wait_recv()
                        total = total + got2[in_slot(got2, slot)].astype(jnp.float32)
                    gwb[here] = total.astype(jnp.bfloat16)

                when(receives, add)
        for sends, copy, _ in fourths[part]:
            when(sends, copy.start)

    def add_fourth(part):
        here = at(part, {1: near, 2: h, 3: ye, 4: za, 5: ze})

        def add():
            total = gwb[here].astype(jnp.float32)
            for _, copy, slot in fourths[part]:
                copy.wait_recv()
                total = total + got3[in_slot(got3, slot)].astype(jnp.float32)
            total = total.astype(jnp.bfloat16)
            first, count = SPANS[part]
            fin[ye, za, ze, :, 256 * first : 256 * (first + count)] = total

        pl.when(active)(add)

    def weight_gradient(pair, order):
        n = 0 if pair is near else 1
        lanes = pl.ds(pl.multiple_of(256 * pair, 256), 256)
        for r in range(4):
            st[:, WIDTH * r : WIDTH * r + WIDTH] = ss[1, r + 1, :, lanes].T
        for run in order:
            for part in run:
                first, count = SPANS[part]
                for j in range(count):
                    kk = first + j
                    window = xs[(kk // 2) % 3, kk // 6 : kk // 6 + 4, :, 256 * (kk % 2) : 256 * (kk % 2) + 256]
                    term = jnp.dot(
                        st[...], window.reshape(4 * WIDTH, 256), preferred_element_type=jnp.float32
                    )
                    gwb[part, pair, :, :, :, :, :, 256 * j : 256 * j + 256] = term.astype(jnp.bfloat16).reshape(
                        2, 2, 2, 2, 16, 256
                    )
            for part in run:
                if (part, n) in halves:
                    sends, copy = halves[part, n][0]
                    when(sends, copy.start)
                if part in across_x:
                    for sends, copy in across_x[part][1:] if n else across_x[part][:1]:
                        when(sends, copy.start)

    passed_in(0)
    passed_in(1)

    @pl.when(passive)
    def _():
        for copy in to_turn:
            copy.wait_recv()

    @pl.loop(0, 4)
    def _(r):
        @pl.when(r == jnp.where(active, 3, 2))
        def _():
            crossed_far.wait_recv()
            pass_on(2)

        forward_row(near, r)

    weight_gradient(near, NEAR_RUNS)

    passed_in(2)

    @pl.when(passive)
    def _():
        passed_in(3)

    @pl.when(active)
    def _():
        for k in range(1, 4):
            from_flip[k].wait_recv()

    @pl.loop(0, 2)
    def _(k):
        forward_row(far, 3 * k)

    rim_above = remote(ss.at[1, 0], ss.at[1, 0], s_send.at[1], s_recv.at[1], other_core)
    rim_below = remote(ss.at[1, 5], ss.at[1, 5], s_send.at[0], s_recv.at[0], other_core)
    slope_up = remote(ss.at[1, 1], ss.at[1, 5], s_send.at[0], s_recv.at[0], {"tile": 2 * jnp.maximum(z - 1, 0) + c})
    slope_down = remote(ss.at[1, 4], ss.at[1, 0], s_send.at[1], s_recv.at[1], {"tile": 2 * jnp.minimum(z + 1, 3) + c})
    pl.when(z > 0)(slope_up.start)
    pl.when(z < 3)(slope_down.start)

    @pl.loop(0, 2)
    def _(k):
        forward_row(far, 2 - k)

    for part in range(2, 6):
        add_half(part, 0)
    weight_gradient(far, FAR_RUNS)

    shift_rows(ss, 1, 4)

    def input_row(r, out):
        lhs = jnp.concatenate([ss[2 - tap % 3, r + 2 - tap // 3] for tap in range(9)], axis=1)
        for e in range(2):
            chunks = []
            for tap in range(9):
                kk = 2 * tap + e
                chunks.append(
                    wall[kk // 3, :, :, :, :, :, :, 256 * (kk % 3) : 256 * (kk % 3) + 256].reshape(512, 256)
                )
            out[:, 256 * e : 256 * e + 256] = jnp.dot(
                lhs, jnp.concatenate(chunks, axis=0), preferred_element_type=jnp.float32
            )

    @pl.loop(0, 2)
    def _(k):
        @pl.when(k == 1)
        def _():
            pl.when(z > 0)(rim_above.wait_recv)
            pl.when(z < 3)(rim_below.wait_recv)
            shift_row(ss, 0)
            shift_row(ss, 5)

        r = jnp.where(k == 0, 2 - c, 3 - 3 * c)
        input_row(r, igp.at[r - 2 * (1 - c)])


    ig_pair = remote(igp, igr, i_send.at[0], i_recv.at[0], other_core)
    ig_pair.start()
    for part in range(2, 6):
        add_second(part, 0)
    for part in range(2, 6):
        add_half(part, 1)
    for part in range(2):
        add_across(part)

    trow[4:8, :] = jnp.full((4, 128), frame_id[0], jnp.int32).astype(jnp.float32)
    trow[0:4, :] = jnp.zeros((4, 128), jnp.float32)

    @pl.loop(0, 2)
    def _(k):
        input_row(2 * c + k, igo.at[k])

    for part in range(2, 6):
        add_second(part, 1)

    ig_pair.wait_recv()

    @pl.loop(0, 2)
    def _(k):
        total = igo[k] + igr[k]
        gfb[k] = total.astype(jnp.bfloat16)
        column_sum = jnp.sum(total, axis=0, keepdims=True)
        for lane in range(4):
            trow[lane : lane + 1, :] += column_sum[:, 128 * lane : 128 * lane + 128]

    gf_copy = pltpu.make_async_copy(gfb, gf_out, loc_sem.at[11])
    gf_copy.start()

    t_copies = []
    for k in range(1, 8):
        copy = remote(trow, tpeer.at[k - 1], t_send.at[k - 1], t_recv.at[k - 1], {"tile": (t + k) % 8})
        copy.start()
        t_copies.append(copy)

    @pl.loop(0, 4)
    def _(r):
        for lane in range(2):
            lanes = pl.ds(128 * lane, 128)
            for v in range(2):
                wide[lane, pl.ds(v, WIDTH, 2), :] = actv[v, r, :, lanes].astype(jnp.float32)
            upb[r, :, lanes] = wide[lane].astype(jnp.bfloat16)

    up_own, up_pair = [], []
    for k in range(2):
        up_own.append(pltpu.make_async_copy(upb.at[2 * c + k], up_out.at[2 * k + c], loc_sem.at[9 + k]))
        up_pair.append(
            remote(upb.at[2 * (1 - c) + k], up_out.at[2 * k + c], u_send.at[k], u_recv.at[k], other_core)
        )
        up_own[-1].start()
        up_pair[-1].start()

    for part in range(PARTS):
        add_third(part)

    for copy in t_copies:
        copy.wait_recv()
    for copy in t_copies:
        copy.wait_send()
    total = trow[0:4, :]
    for k in range(7):
        total = total + tpeer[k, 0:4, :]
    tall[0, 0:4, :] = total
    tall[0, 4:8, :] = trow[4:8, :]
    y = 2 * h + lo
    v_copies = []
    for k in range(1, 4):
        to = (y + k) % 4
        v_copies.append(
            remote(tall.at[0], tall.at[k], v_send.at[k - 1], v_recv.at[k - 1], {"fsdp": 2 * x + to // 2, "dp": to % 2})
        )
    for k in range(1, 4):
        to = (x + k) % 4
        v_copies.append(
            remote(
                tall.at[pl.ds(0, 4)], tall.at[pl.ds(4 * k, 4)], v_send.at[2 + k], v_recv.at[2 + k], {"fsdp": 2 * to + h}
            )
        )
    for copy in v_copies[:3]:
        copy.start()

    spreads, to_pair, to_self = [], [], []
    for g in range(2):
        first, last = SPANS[3 * g][0], SPANS[3 * g + 2][0] + SPANS[3 * g + 2][1]
        cols = pl.ds(256 * first, 256 * (last - first))
        piece_at = fin.at[ye, za, ze, :, cols]
        spreads.append(
            [remote(piece_at, piece_at, f_send.at[g, k], f_recv.at[g, k], holders[k]) for k in range(7)]
        )
        held, out = fin.at[:, :, :, :, cols], gw_out.at[:, :, :, :, cols]
        to_pair.append(remote(held, out, i_send.at[1 + g], i_recv.at[1 + g], other_core))
        to_self.append(pltpu.make_async_copy(held, out, loc_sem.at[12 + g]))

    for g in range(2):
        for part in range(3 * g, 3 * g + 3):
            add_fourth(part)

        @pl.when(active)
        def _(g=g):
            for copy in spreads[g]:
                copy.start()

    for copy in v_copies[:3]:
        copy.wait_recv()
    for copy in v_copies[3:]:
        copy.start()

    @pl.when(active)
    def _():
        for g in range(2):
            for copy in spreads[g]:
                copy.wait_recv()
            to_pair[g].start()
            to_self[g].start()
        for g in range(2):
            for copy in spreads[g]:
                copy.wait_send()
            to_self[g].wait()
            to_pair[g].wait_send()

    @pl.when(c != xa)
    def _():
        for g in range(2):
            to_pair[g].wait_recv()

    for copy in v_copies[3:]:
        copy.wait_recv()
    for copy in v_copies:
        copy.wait_send()
    tab_copy = pltpu.make_async_copy(tall, tab_out, loc_sem.at[14])
    tab_copy.start()

    @pl.when(active)
    def _():
        for copy in to_turn + to_flip:
            copy.wait_send()

    @pl.when(passive)
    def _():
        for copy in relay:
            copy.wait_send()
        for j in range(3):
            passed[3, j][0].wait_send()

    for copy in across + [across_far]:
        copy.wait_send()
    for k in range(3):
        for j in range(3):
            passed[k, j][0].wait_send()

    @pl.when(z > 0)
    def _():
        top_swap.wait_send()

    @pl.when(z < 3)
    def _():
        bottom_swap.wait_send()

    for (sends, copy), _, _ in list(halves.values()) + list(seconds.values()):
        when(sends, copy.wait_send)
    for sends, copy in across_x[0] + across_x[1]:
        when(sends, copy.wait_send)
    for (part, n), (entry, _, _) in thirds.items():
        for sends, copy, _ in entry[1:] if part >= 4 and n == 1 else entry:
            when(sends, copy.wait_send)
    for entry in fourths.values():
        for sends, copy, _ in entry:
            when(sends, copy.wait_send)
    x_pair.wait_send()

    @pl.when(sends_rim)
    def _():
        for copy in rim_out:
            copy.wait_send()

    for copy in ct_pair:
        copy.wait_send()
    pl.when(z > 0)(slope_up.wait_send)
    pl.when(z < 3)(slope_down.wait_send)
    for k in range(2):
        up_own[k].wait()
        up_pair[k].wait()
    ig_pair.wait_send()
    gf_copy.wait()
    tab_copy.wait()


def fused(features, weight, cot, shift_row, frame_id):
    any_space = pl.BlockSpec(memory_space=pl.ANY)
    vmem = pl.BlockSpec(memory_space=pltpu.VMEM)
    bf16, f32 = jnp.bfloat16, jnp.float32
    dma = pltpu.SemaphoreType.DMA
    return pl.pallas_call(
        kernel,
        out_shape=(
            jax.ShapeDtypeStruct((4, 2 * WIDTH, 256), bf16),
            jax.ShapeDtypeStruct((2, 2, 2, 16, 9 * CIN), bf16),
            jax.ShapeDtypeStruct((2, WIDTH, CIN), bf16),
            jax.ShapeDtypeStruct((16, 8, 128), f32),
        ),
        in_specs=[any_space, any_space, any_space, vmem, pl.BlockSpec(memory_space=pltpu.SMEM)],
        out_specs=[any_space] * 4,
        scratch_shapes=[
            pltpu.VMEM((3, 6, WIDTH, CIN), bf16),
            pltpu.VMEM((3, 6, WIDTH, HALF), bf16),
            pltpu.VMEM((256, 4 * WIDTH), bf16),
            pltpu.VMEM((PARTS, 2, 2, 2, 2, 2, 16, PCOLS), bf16),
            pltpu.VMEM((PARTS, 2, 2, 2, 2, 2, 16, GCOLS), bf16),
            pltpu.VMEM((PARTS, 2, 2, 2, 2, 2, 16, GCOLS), bf16),
            pltpu.VMEM((PARTS, 2, 2, 2, 2, 2, 16, GCOLS), bf16),
            pltpu.VMEM((PARTS, 3, 2, 2, 16, GCOLS), bf16),
            pltpu.VMEM((PARTS, 3, 16, GCOLS), bf16),
            pltpu.VMEM((2, 2, 2, 16, 9 * CIN), bf16),
            pltpu.VMEM((4, 2 * WIDTH, 256), bf16),
            pltpu.VMEM((2, 4, WIDTH, 256), bf16),
            pltpu.VMEM((2, 4, WIDTH, 256), bf16),
            pltpu.VMEM((4, 2 * WIDTH, 256), bf16),
            pltpu.VMEM((2, 2 * WIDTH, 128), f32),
            pltpu.VMEM((WIDTH, 256), f32),
            pltpu.VMEM((2, WIDTH, CIN), f32),
            pltpu.VMEM((2, WIDTH, CIN), f32),
            pltpu.VMEM((2, WIDTH, CIN), f32),
            pltpu.VMEM((2, WIDTH, CIN), bf16),
            pltpu.VMEM((8, 128), f32),
            pltpu.VMEM((7, 8, 128), f32),
            pltpu.VMEM((16, 8, 128), f32),
            dma((15,)),
            dma((7,)),
            dma((7,)),
            dma((11,)),
            dma((11,)),
            dma((3,)),
            dma((3,)),
            dma((4, 3)),
            dma((4, 3)),
            dma((2,)),
            dma((2,)),
            dma((PARTS, 13)),
            dma((PARTS, 13)),
            dma((2, 7)),
            dma((2, 7)),
            dma((2,)),
            dma((2,)),
            dma((3,)),
            dma((3,)),
            dma((7,)),
            dma((7,)),
            dma((6,)),
            dma((6,)),
        ],
        compiler_params=pltpu.CompilerParams(
            collective_id=0, has_side_effects=True, vmem_limit_bytes=60 * 2**20
        ),
        cost_estimate=pl.CostEstimate(
            flops=6 * 768 * 4608 * 1024, bytes_accessed=2 * 10**7, transcendentals=3 * 768 * 1024
        ),
        name="conv_block",
    )(features, weight, cot, shift_row, frame_id)


def shards(features, frame_table, frame_ids, conv_weight, cotangent):
    video_len = frame_table.shape[0]
    shift = lax.dynamic_slice_in_dim(frame_table, frame_ids[0], 1, axis=0).astype(jnp.float32)
    up, gw, gf, tab = fused(
        features[0], conv_weight.reshape(2, 2, 2, 16, 9 * CIN), cotangent[0], shift, frame_ids
    )
    sums = tab[:, :4].reshape(16, CIN)
    frames = tab[:, 4, 0]
    picker = (frames[:, None] == jnp.arange(video_len, dtype=jnp.float32)[None, :]).astype(jnp.float32)
    grad_table = lax.dot_general(
        picker, sums, (((0,), (0,)), ((), ())),
        precision=lax.Precision.HIGH, preferred_element_type=jnp.float32,
    )
    grad_weight = gw.reshape(128, 9 * CIN).astype(jnp.float32)
    return (up[None], grad_weight, gf[None], grad_table)


def solution(mesh):
    return jax.shard_map(
        shards,
        mesh=mesh,
        in_specs=(
            P(("fsdp", "dp"), "tile", None, None),
            P(),
            P(("fsdp", "dp")),
            P("fsdp", None),
            P(("fsdp", "dp"), "tile", None, None),
        ),
        out_specs=(
            P(("fsdp", "dp"), "tile", None, None),
            P("fsdp", None),
            P(("fsdp", "dp"), "tile", None, None),
            P(),
        ),
        check_vma=False,
    )
```

```python
import jax
import jax.numpy as jnp
from jax import lax
from jax.experimental import pallas as pl
from jax.experimental.pallas import tpu as pltpu
from jax.sharding import PartitionSpec as P

inv_root_two = 0.7071067811865476
inv_root_tau = 0.3989422804014327

WIDTH = 384
CIN = 512
HALF = 512
PARTS = 6
PCOLS = 768
CHUNKS = 18

DIMS = 6

FIRST = [None, None, (2, 3), (3, 2), (4, 5), (5, 4)]
NEAR_RUNS = ((0, 1, 2, 3, 4, 5),)
FAR_RUNS = ((0, 1), (2, 3), (4, 5))
SPANS = ((0, 2), (2, 2), (4, 4), (8, 4), (12, 3), (15, 3))
GCOLS = 1024

MESH = pl.DeviceIdType.MESH


def kernel(
    feat, weight, cot, shift_row_in, frame_id,
    up_out, gw_out, gf_out, tab_out,
    xs, ss, st, wall, gwb, got0, got1, got2, got3, fin, ctv, cts, actv, upb, wide, acc, igp, igo, igr, gfb,
    trow, tpeer, tall,
    loc_sem, x_send, x_recv, o_send, o_recv, n_send, n_recv, q_send, q_recv, s_send, s_recv,
    r_send, r_recv, f_send, f_recv, u_send, u_recv, i_send, i_recv, t_send, t_recv, v_send, v_recv,
):
    f = lax.axis_index("fsdp")
    t = lax.axis_index("tile")
    lo = lax.axis_index("dp")
    x, h = f // 2, f % 2
    z, c = t // 2, t % 2
    xa, xb = x // 2, x % 2
    xe = (xa + xb) % 2
    ye = (h + lo) % 2
    za = z // 2
    ze = (za + z % 2) % 2
    keep = (c + xe) % 2
    active, passive = c == xa, c != xa
    mine = {1: keep, 2: h, 3: ye, 4: za, 5: ze}
    x_flip = x + 1 - 2 * xb
    z_flip = z + 1 - 2 * (z % 2)
    partner = {
        0: {"fsdp": (3 - x) * 2 + h},
        1: {"fsdp": x_flip * 2 + h},
        2: {"fsdp": x * 2 + 1 - h, "dp": 1 - lo},
        3: {"dp": 1 - lo},
        4: {"tile": (3 - z) * 2 + c},
        5: {"tile": z_flip * 2 + c},
    }
    other_core = {"tile": 2 * z + 1 - c}
    two_away = {"fsdp": (x + 2) % 4 * 2 + h}
    quarter = (z + 2 * ye) % 4
    holders = [
        {"tile": (z + k // 2) % 4 * 2 + c, "dp": (lo + k % 2) % 2} for k in range(1, 8)
    ]

    def remote(src, dst, send_sem, recv_sem, device):
        return pltpu.make_async_remote_copy(
            src_ref=src, dst_ref=dst, send_sem=send_sem, recv_sem=recv_sem,
            device_id=device, device_id_type=MESH,
        )

    barrier = pltpu.get_barrier_semaphore()
    for k in range(1, 8):
        pl.semaphore_signal(barrier, inc=1, device_id={"tile": (t + k) % 8}, device_id_type=MESH)
    frame = f * 2 + lo
    for k in range(1, 16):
        to = (frame + k) % 16
        pl.semaphore_signal(
            barrier, inc=1, device_id={"fsdp": to // 2, "dp": to % 2}, device_id_type=MESH
        )

    for k in (3, 5, 7):
        pl.semaphore_signal(barrier, inc=1, device_id=holders[k - 1], device_id_type=MESH)

    near, far = keep, 1 - keep
    own_x = pltpu.make_async_copy(feat, xs.at[1, pl.ds(1 + 2 * c, 2)], loc_sem.at[0])
    own_x.start()
    own_w = [
        pltpu.make_async_copy(
            weight.at[:, :, :, :, pl.ds(PCOLS * part, PCOLS)], wall.at[part, near, h], loc_sem.at[1 + part]
        )
        for part in range(PARTS)
    ]

    @pl.when(active)
    def _():
        for copy in own_w:
            copy.start()

    own_ct = []
    for k in range(2):
        own_ct.append(
            pltpu.make_async_copy(cot.at[2 * k + c], ctv.at[2 * c + k], loc_sem.at[7 + k])
        )
        own_ct[-1].start()

    own_x.wait()
    for k in range(2):
        for lane in range(4):
            at = pl.ds(128 * lane, 128)
            row = xs[1, 1 + 2 * c + k, :, at].astype(jnp.float32) + shift_row_in[:, at]
            xs[1, 1 + 2 * c + k, :, at] = row.astype(jnp.bfloat16)

    pl.semaphore_wait(barrier, 25)

    def same(pair, half, number, send_sem, recv_sem, device, eighth=None):
        place = wall.at[:, pair, half, number // 2, number % 2]
        if eighth is not None:
            place = wall.at[:, pair, half, number // 2, number % 2, eighth]
        return remote(place, place, send_sem, recv_sem, device)

    turn = [(quarter + k) % 4 for k in range(4)]
    to_flip = [same(near, h, turn[k], o_send.at[k], o_recv.at[k], partner[1]) for k in range(4)]
    to_turn = [same(near, h, turn[k], o_send.at[3 + k], o_recv.at[3 + k], partner[0]) for k in range(1, 4)]
    first_turn = [same(near, h, quarter, o_send.at[9 + e], o_recv.at[9 + e], partner[0], e) for e in range(2)]
    relay = [same(near, h, quarter, o_send.at[7 + e], o_recv.at[7 + e], partner[1], e) for e in range(2)]
    from_flip = [same(far, h, turn[k], o_send.at[k], o_recv.at[k], partner[1]) for k in range(4)]
    from_far = [same(far, h, quarter, o_send.at[7 + e], o_recv.at[7 + e], partner[1], e) for e in range(2)]
    across = [same(near, h, quarter, n_send.at[e], n_recv.at[e], partner[2], e) for e in range(2)]
    crossed = [same(near, 1 - h, quarter, n_send.at[e], n_recv.at[e], partner[2], e) for e in range(2)]
    across_far = same(far, h, quarter, n_send.at[2], n_recv.at[2], partner[2])
    crossed_far = same(far, 1 - h, quarter, n_send.at[2], n_recv.at[2], partner[2])
    passed = {}
    theirs = {3: (quarter + 2) % 4, 4: (3 - z + 2 * ye) % 4, 5: (z_flip + 2 * ye) % 4}
    for k, (pair, half, e) in enumerate(((near, 1 - h, 0), (near, 1 - h, 1), (far, 1 - h, None), (far, h, None))):
        for j, dim in enumerate((3, 4, 5)):
            passed[k, j] = (
                same(pair, half, quarter, q_send.at[k, j], q_recv.at[k, j], partner[dim], e),
                same(pair, half, theirs[dim], q_send.at[k, j], q_recv.at[k, j], partner[dim], e),
            )

    def pass_on(k):
        for j in range(3):
            passed[k, j][0].start()

    def passed_in(k):
        for j in range(3):
            passed[k, j][1].wait_recv()

    @pl.when(active)
    def _():
        for copy in own_w:
            copy.wait()
        for e in range(2):
            first_turn[e].start()
            across[e].start()
        to_flip[0].start()

    x_pair = remote(
        xs.at[1, pl.ds(1 + 2 * c, 2)], xs.at[1, pl.ds(1 + 2 * c, 2)], x_send.at[0], x_recv.at[0], other_core
    )
    x_pair_in = remote(
        xs.at[1, pl.ds(3 - 2 * c, 2)], xs.at[1, pl.ds(3 - 2 * c, 2)], x_send.at[0], x_recv.at[0], other_core
    )
    rim_cols = WIDTH // 2
    sends_rim = jnp.where(c == 0, z > 0, z < 3)
    z_rim = jnp.where(c == 0, jnp.maximum(z - 1, 0), jnp.minimum(z + 1, 3))
    rim_out = [
        remote(
            xs.at[1, 1 + 3 * c, pl.ds(rim_cols * k, rim_cols)],
            xs.at[1, 5 - 5 * c, pl.ds(rim_cols * k, rim_cols)],
            x_send.at[1 + k], x_recv.at[1 + c], {"tile": 2 * z_rim + k},
        )
        for k in range(2)
    ]

    def rim_part(row, core, sem):
        at = xs.at[1, row, pl.ds(pl.multiple_of(rim_cols * core, rim_cols), rim_cols)]
        return remote(at, at, x_send.at[sem], x_recv.at[sem], other_core)

    top_in, bottom_in = rim_part(0, c, 2), rim_part(5, c, 1)
    top_swap, bottom_swap = rim_part(0, c, 5), rim_part(5, c, 6)
    top_swapped, bottom_swapped = rim_part(0, 1 - c, 5), rim_part(5, 1 - c, 6)

    @pl.when(sends_rim)
    def _():
        for copy in rim_out:
            copy.start()

    x_pair.start()

    ct_pair = []
    for k in range(2):
        ct_pair.append(
            remote(cot.at[2 * k + 1 - c], ctv.at[2 * c + k], x_send.at[3 + k], x_recv.at[3 + k], other_core)
        )
        ct_pair[-1].start()

    @pl.when(z == 0)
    def _():
        xs[1, 0] = jnp.zeros((WIDTH, CIN), jnp.bfloat16)
        ss[1, 0] = jnp.zeros((WIDTH, HALF), jnp.bfloat16)

    @pl.when(z == 3)
    def _():
        xs[1, 5] = jnp.zeros((WIDTH, CIN), jnp.bfloat16)
        ss[1, 5] = jnp.zeros((WIDTH, HALF), jnp.bfloat16)

    column = lax.broadcasted_iota(jnp.int32, (WIDTH, 128), 0)

    def shift_row(ref, row):
        for lane in range(4):
            at = pl.ds(128 * lane, 128)
            values = ref[1, row, :, at].astype(jnp.float32)
            right = jnp.where(column == 0, 0.0, pltpu.roll(values, 1, 0))
            left = jnp.where(column == WIDTH - 1, 0.0, pltpu.roll(values, WIDTH - 1, 0))
            ref[0, row, :, at] = right.astype(jnp.bfloat16)
            ref[2, row, :, at] = left.astype(jnp.bfloat16)

    def shift_rows(ref, first, count):
        @pl.loop(0, count)
        def _(k):
            shift_row(ref, first + k)

    @pl.when(active)
    def _():
        for e in range(2):
            first_turn[e].wait_send()
        to_turn[0].start()

    shift_rows(xs, 1 + 2 * c, 2)

    @pl.when(active)
    def _():
        for e in range(2):
            crossed[e].wait_recv()
            pass_on(e)
        for k in range(1, 3):
            to_turn[k].start()
        to_flip[1].start()

    @pl.when(passive)
    def _():
        for e in range(2):
            first_turn[e].wait_recv()
            across[e].start()
            relay[e].start()

    x_pair_in.wait_recv()
    shift_rows(xs, 3 - 2 * c, 2)

    @pl.when(z > 0)
    def _():
        top_in.wait_recv()
        top_swap.start()

    @pl.when(z < 3)
    def _():
        bottom_in.wait_recv()
        bottom_swap.start()

    @pl.when(passive)
    def _():
        for e in range(2):
            crossed[e].wait_recv()
            pass_on(e)

    for copy in own_ct:
        copy.wait()
    for copy in ct_pair:
        copy.wait_recv()

    @pl.loop(0, 4)
    def _(r):
        for lane in range(2):
            wide[lane] = ctv[r, :, 128 * lane : 128 * lane + 128].astype(jnp.float32)
        for v in range(2):
            for lane in range(2):
                cts[v, r, :, 128 * lane : 128 * lane + 128] = wide[lane, pl.ds(v, WIDTH, 2), :].astype(jnp.bfloat16)

    @pl.when(z > 0)
    def _():
        top_swapped.wait_recv()

    @pl.when(z < 3)
    def _():
        bottom_swapped.wait_recv()

    shift_rows(xs, 0, 1)
    shift_rows(xs, 5, 1)

    @pl.when(active)
    def _():
        from_flip[0].wait_recv()
        across_far.start()
        for k in range(2, 4):
            to_flip[k].start()

    @pl.when(passive)
    def _():
        for copy in from_far:
            copy.wait_recv()
        across_far.start()
        pass_on(3)

    def forward_row(v, r):
        lhs = jnp.concatenate(
            [
                xs[(kk // 2) % 3, r + kk // 6, :, 256 * (kk % 2) : 256 * (kk % 2) + 256]
                for kk in range(CHUNKS)
            ],
            axis=1,
        )
        rhs = jnp.concatenate(
            [
                wall[kk // 3, v, :, :, :, :, :, 256 * (kk % 3) : 256 * (kk % 3) + 256].reshape(256, 256)
                for kk in range(CHUNKS)
            ],
            axis=1,
        )
        acc[...] = lax.dot_general(
            lhs, rhs, (((1,), (1,)), ((), ())), preferred_element_type=jnp.float32
        )

        @pl.loop(0, WIDTH // 32)
        def _(j):
            rows = pl.ds(pl.multiple_of(j * 32, 32), 32)
            value = acc[rows]
            grown = 0.5 * (1.0 + lax.erf(value * inv_root_two))
            slope = grown + value * jnp.exp(-0.5 * value * value) * inv_root_tau
            actv[v, r, rows] = (value * grown).astype(jnp.bfloat16)
            out = pl.ds(pl.multiple_of(256 * v, 256), 256)
            ss[1, r + 1, rows, out] = (cts[v, r, rows].astype(jnp.float32) * slope).astype(jnp.bfloat16)

    def at(part, fixed):
        return (part,) + tuple(fixed.get(d, slice(None)) for d in range(1, 6)) + (slice(None), lanes_of(part))

    def lanes_of(part):
        return pl.ds(0, 256 * SPANS[part][1])

    def in_slot(slots, slot):
        return slot + (slice(None),) * (len(slots.shape) - 1 - len(slot)) + (lanes_of(slot[0]),)

    def when(condition, body):
        if condition is None:
            body()
        else:
            pl.when(condition)(body)

    two_y = {"fsdp": x * 2 + 1 - h}
    two_z = {"tile": (z + 2) % 4 * 2 + c}

    halves, seconds, thirds, fourths = {}, {}, {}, {}

    def half_copy(part, n, dim, there, sends):
        place = at(part, there)
        return (
            sends,
            remote(gwb.at[place], got0.at[place], r_send.at[part, n], r_recv.at[part, n], partner[dim]),
        )

    def second_copy(part, n, dim, there, sends):
        place = at(part, there)
        return (
            sends,
            remote(
                gwb.at[place], got1.at[place], r_send.at[part, 2 + n], r_recv.at[part, 2 + n], partner[dim]
            ),
        )

    def slot_copy(part, there, slots, slot, sem, device, sends):
        return (
            sends,
            remote(
                gwb.at[at(part, there)], slots.at[in_slot(slots, slot)], r_send.at[part, sem], r_recv.at[part, sem], device
            ),
            slot,
        )

    def flips(axis):
        da, db = 2 * axis, 2 * axis + 1
        there = {da: 1 - mine[da], db: 1 - mine[db]}
        return (
            ({da: there[da], db: mine[db]}, partner[da]),
            ({da: mine[da], db: there[db]}, partner[db]),
            (there, two_y if axis == 1 else two_z),
        )

    def along_x(part, kept, slots, sem):
        return [
            slot_copy(part, {**kept, 1: pair}, slots, (part, j), sem + j, device, sends)
            for j, (sends, pair, device) in enumerate(
                ((passive, near, partner[0]), (active, far, partner[1]), (passive, far, two_away))
            )
        ]

    across_x = {
        part: [
            (
                sends,
                remote(
                    gwb.at[at(part, {1: pair})], slots.at[at(part, {1: place})],
                    r_send.at[part, j], r_recv.at[part, j], device,
                ),
            )
            for j, (sends, pair, device, slots, place) in enumerate(
                (
                    (passive, near, partner[0], got0, near),
                    (active, far, partner[1], got1, far),
                    (passive, far, two_away, got0, near),
                )
            )
        ]
        for part in (0, 1)
    }
    for part in (0, 1):
        thirds[part, 1] = (
            [
                slot_copy(part, {1: near, **there}, got2, (part, j), 7 + j, device, active)
                for j, (there, device) in enumerate(flips(1))
            ],
            active, at(part, {1: near, 2: h, 3: ye}),
        )
        fourths[part] = [
            slot_copy(part, {1: near, 2: h, 3: ye, **there}, got3, (part, j), 10 + j, device, active)
            for j, (there, device) in enumerate(flips(2))
        ]
    for part in range(2, 6):
        one, two = FIRST[part]
        first = {one: mine[one]}
        both = {**first, two: mine[two]}
        for n, pair in enumerate((near, far)):
            halves[part, n] = (
                half_copy(part, n, one, {1: pair, one: 1 - mine[one]}, None),
                None, at(part, {1: pair, **first}),
            )
            seconds[part, n] = (
                second_copy(part, n, two, {1: pair, **first, two: 1 - mine[two]}, None),
                None, at(part, {1: pair, **both}),
            )
            if part < 4:
                thirds[part, n] = (
                    [
                        slot_copy(
                            part, {1: pair, **both, **there}, got2, (part, j, 0, pair), 4 + 3 * n + j, device, None
                        )
                        for j, (there, device) in enumerate(flips(2))
                    ],
                    None, at(part, {1: pair, **both, 4: za, 5: ze}),
                )
        if part < 4:
            fourths[part] = along_x(part, {**both, 4: za, 5: ze}, got3, 10)
        else:
            copies = along_x(part, both, got2, 4)
            thirds[part, 0] = ([copies[0]], None, None)
            thirds[part, 1] = (copies, active, at(part, {**both, 1: near}))
            fourths[part] = [
                slot_copy(part, {1: near, **both, **there}, got3, (part, j), 10 + j, device, active)
                for j, (there, device) in enumerate(flips(1))
            ]

    def add_across(part):
        def add():
            for _, copy in across_x[part]:
                copy.wait_recv()
            here, there = at(part, {1: near}), at(part, {1: far})
            total = gwb[here].astype(jnp.float32) + got0[here].astype(jnp.float32)
            total = total + got1[here].astype(jnp.float32) + got0[there].astype(jnp.float32)
            gwb[here] = total.astype(jnp.bfloat16)

        pl.when(active)(add)
        for sends, copy, _ in thirds[part, 1][0]:
            when(sends, copy.start)

    def add_half(part, n):
        if (part, n) in halves:
            (_, copy), receives, here = halves[part, n]

            def add():
                copy.wait_recv()
                total = gwb[here].astype(jnp.float32) + got0[here].astype(jnp.float32)
                gwb[here] = total.astype(jnp.bfloat16)

            when(receives, add)
        if (part, n) in seconds:
            when(seconds[part, n][0][0], seconds[part, n][0][1].start)

    def add_second(part, n):
        if (part, n) not in seconds:
            return
        (_, copy), receives, here = seconds[part, n]

        def add():
            copy.wait_recv()
            total = gwb[here].astype(jnp.float32) + got1[here].astype(jnp.float32)
            gwb[here] = total.astype(jnp.bfloat16)

        when(receives, add)
        entry = thirds[part, n][0]
        for sends, copy, _ in entry[1:] if part >= 4 and n == 1 else entry:
            when(sends, copy.start)

    def add_third(part):
        for n in range(2):
            if (part, n) in thirds and thirds[part, n][2] is not None:
                entry, receives, here = thirds[part, n]

                def add(entry=entry, here=here):
                    total = gwb[here].astype(jnp.float32)
                    for _, copy, slot in entry:
                        copy.wait_recv()
                        total = total + got2[in_slot(got2, slot)].astype(jnp.float32)
                    gwb[here] = total.astype(jnp.bfloat16)

                when(receives, add)
        for sends, copy, _ in fourths[part]:
            when(sends, copy.start)

    def add_fourth(part):
        here = at(part, {1: near, 2: h, 3: ye, 4: za, 5: ze})

        def add():
            total = gwb[here].astype(jnp.float32)
            for _, copy, slot in fourths[part]:
                copy.wait_recv()
                total = total + got3[in_slot(got3, slot)].astype(jnp.float32)
            total = total.astype(jnp.bfloat16)
            first, count = SPANS[part]
            fin[ye, za, ze, :, 256 * first : 256 * (first + count)] = total

        pl.when(active)(add)

    def weight_gradient(pair, order):
        n = 0 if pair is near else 1
        lanes = pl.ds(pl.multiple_of(256 * pair, 256), 256)
        for r in range(4):
            st[:, WIDTH * r : WIDTH * r + WIDTH] = ss[1, r + 1, :, lanes].T
        for run in order:
            for part in run:
                first, count = SPANS[part]
                for j in range(count):
                    kk = first + j
                    window = xs[(kk // 2) % 3, kk // 6 : kk // 6 + 4, :, 256 * (kk % 2) : 256 * (kk % 2) + 256]
                    term = jnp.dot(
                        st[...], window.reshape(4 * WIDTH, 256), preferred_element_type=jnp.float32
                    )
                    gwb[part, pair, :, :, :, :, :, 256 * j : 256 * j + 256] = term.astype(jnp.bfloat16).reshape(
                        2, 2, 2, 2, 16, 256
                    )
            for part in run:
                if (part, n) in halves:
                    sends, copy = halves[part, n][0]
                    when(sends, copy.start)
                if part in across_x:
                    for sends, copy in across_x[part][1:] if n else across_x[part][:1]:
                        when(sends, copy.start)

    passed_in(0)
    passed_in(1)

    @pl.when(passive)
    def _():
        for copy in to_turn:
            copy.wait_recv()

    @pl.loop(0, 4)
    def _(r):
        @pl.when(r == jnp.where(active, 3, 2))
        def _():
            crossed_far.wait_recv()
            pass_on(2)

        forward_row(near, r)

    weight_gradient(near, NEAR_RUNS)

    passed_in(2)

    @pl.when(passive)
    def _():
        passed_in(3)

    @pl.when(active)
    def _():
        for k in range(1, 4):
            from_flip[k].wait_recv()

    @pl.loop(0, 2)
    def _(k):
        forward_row(far, 3 * k)

    rim_above = remote(ss.at[1, 0], ss.at[1, 0], s_send.at[1], s_recv.at[1], other_core)
    rim_below = remote(ss.at[1, 5], ss.at[1, 5], s_send.at[0], s_recv.at[0], other_core)
    slope_up = remote(ss.at[1, 1], ss.at[1, 5], s_send.at[0], s_recv.at[0], {"tile": 2 * jnp.maximum(z - 1, 0) + c})
    slope_down = remote(ss.at[1, 4], ss.at[1, 0], s_send.at[1], s_recv.at[1], {"tile": 2 * jnp.minimum(z + 1, 3) + c})
    pl.when(z > 0)(slope_up.start)
    pl.when(z < 3)(slope_down.start)

    @pl.loop(0, 2)
    def _(k):
        forward_row(far, 2 - k)

    for part in range(2, 6):
        add_half(part, 0)
    weight_gradient(far, FAR_RUNS)

    shift_rows(ss, 1, 4)

    def input_row(r, out):
        lhs = jnp.concatenate([ss[2 - tap % 3, r + 2 - tap // 3] for tap in range(9)], axis=1)
        for e in range(2):
            chunks = []
            for tap in range(9):
                kk = 2 * tap + e
                chunks.append(
                    wall[kk // 3, :, :, :, :, :, :, 256 * (kk % 3) : 256 * (kk % 3) + 256].reshape(512, 256)
                )
            out[:, 256 * e : 256 * e + 256] = jnp.dot(
                lhs, jnp.concatenate(chunks, axis=0), preferred_element_type=jnp.float32
            )

    @pl.loop(0, 2)
    def _(k):
        @pl.when(k == 1)
        def _():
            pl.when(z > 0)(rim_above.wait_recv)
            pl.when(z < 3)(rim_below.wait_recv)
            shift_row(ss, 0)
            shift_row(ss, 5)

        r = jnp.where(k == 0, 2 - c, 3 - 3 * c)
        input_row(r, igp.at[r - 2 * (1 - c)])


    ig_pair = remote(igp, igr, i_send.at[0], i_recv.at[0], other_core)
    ig_pair.start()
    for part in range(2, 6):
        add_second(part, 0)
    for part in range(2, 6):
        add_half(part, 1)
    for part in range(2):
        add_across(part)

    trow[4:8, :] = jnp.full((4, 128), frame_id[0], jnp.int32).astype(jnp.float32)
    trow[0:4, :] = jnp.zeros((4, 128), jnp.float32)

    @pl.loop(0, 2)
    def _(k):
        input_row(2 * c + k, igo.at[k])

    for part in range(2, 6):
        add_second(part, 1)

    ig_pair.wait_recv()

    @pl.loop(0, 2)
    def _(k):
        total = igo[k] + igr[k]
        gfb[k] = total.astype(jnp.bfloat16)
        column_sum = jnp.sum(total, axis=0, keepdims=True)
        for lane in range(4):
            trow[lane : lane + 1, :] += column_sum[:, 128 * lane : 128 * lane + 128]

    gf_copy = pltpu.make_async_copy(gfb, gf_out, loc_sem.at[11])
    gf_copy.start()

    t_copies = []
    for k in range(1, 8):
        copy = remote(trow, tpeer.at[k - 1], t_send.at[k - 1], t_recv.at[k - 1], {"tile": (t + k) % 8})
        copy.start()
        t_copies.append(copy)

    @pl.loop(0, 4)
    def _(r):
        for lane in range(2):
            lanes = pl.ds(128 * lane, 128)
            for v in range(2):
                wide[lane, pl.ds(v, WIDTH, 2), :] = actv[v, r, :, lanes].astype(jnp.float32)
            upb[r, :, lanes] = wide[lane].astype(jnp.bfloat16)

    up_own, up_pair = [], []
    for k in range(2):
        up_own.append(pltpu.make_async_copy(upb.at[2 * c + k], up_out.at[2 * k + c], loc_sem.at[9 + k]))
        up_pair.append(
            remote(upb.at[2 * (1 - c) + k], up_out.at[2 * k + c], u_send.at[k], u_recv.at[k], other_core)
        )
        up_own[-1].start()
        up_pair[-1].start()

    for part in range(PARTS):
        add_third(part)

    for copy in t_copies:
        copy.wait_recv()
    for copy in t_copies:
        copy.wait_send()
    total = trow[0:4, :]
    for k in range(7):
        total = total + tpeer[k, 0:4, :]
    tall[0, 0:4, :] = total
    tall[0, 4:8, :] = trow[4:8, :]
    y = 2 * h + lo
    v_copies = []
    for k in range(1, 4):
        to = (y + k) % 4
        v_copies.append(
            remote(tall.at[0], tall.at[k], v_send.at[k - 1], v_recv.at[k - 1], {"fsdp": 2 * x + to // 2, "dp": to % 2})
        )
    for k in range(1, 4):
        to = (x + k) % 4
        v_copies.append(
            remote(
                tall.at[pl.ds(0, 4)], tall.at[pl.ds(4 * k, 4)], v_send.at[2 + k], v_recv.at[2 + k], {"fsdp": 2 * to + h}
            )
        )
    for copy in v_copies[:3]:
        copy.start()

    spreads, to_pair, to_self = [], [], []
    groups = ((0, 1, 2), (3, 4, 5))
    for g, parts in enumerate(groups):
        first, last = SPANS[parts[0]][0], SPANS[parts[-1]][0] + SPANS[parts[-1]][1]
        cols = pl.ds(256 * first, 256 * (last - first))
        piece_at = fin.at[ye, za, ze, :, cols]
        spreads.append(
            [remote(piece_at, piece_at, f_send.at[g, k], f_recv.at[g, k], holders[k]) for k in range(7)]
        )
        for n, row in enumerate((ye, 1 - ye)):
            held, out = fin.at[row, :, :, :, cols], gw_out.at[row, :, :, :, cols]
            sem = 2 * g + n
            to_pair.append(remote(held, out, i_send.at[1 + sem], i_recv.at[1 + sem], other_core))
            to_self.append(pltpu.make_async_copy(held, out, loc_sem.at[12 + sem]))

    for g, parts in enumerate(groups):
        for part in parts:
            add_fourth(part)

        @pl.when(active)
        def _(g=g):
            for copy in spreads[g]:
                copy.start()

    for copy in v_copies[:3]:
        copy.wait_recv()
    for copy in v_copies[3:]:
        copy.start()

    @pl.when(active)
    def _():
        for g in range(2):
            for n in range(2):
                for k in range(1 - n, 7, 2):
                    spreads[g][k].wait_recv()
                to_pair[2 * g + n].start()
                to_self[2 * g + n].start()
        for g in range(2):
            for copy in spreads[g]:
                copy.wait_send()
        for n in range(4):
            to_self[n].wait()
            to_pair[n].wait_send()

    @pl.when(passive)
    def _():
        for n in range(4):
            to_pair[n].wait_recv()

    for copy in v_copies[3:]:
        copy.wait_recv()
    for copy in v_copies:
        copy.wait_send()
    tab_copy = pltpu.make_async_copy(tall, tab_out, loc_sem.at[16])
    tab_copy.start()

    @pl.when(active)
    def _():
        for copy in to_turn + to_flip:
            copy.wait_send()

    @pl.when(passive)
    def _():
        for copy in relay:
            copy.wait_send()
        for j in range(3):
            passed[3, j][0].wait_send()

    for copy in across + [across_far]:
        copy.wait_send()
    for k in range(3):
        for j in range(3):
            passed[k, j][0].wait_send()

    @pl.when(z > 0)
    def _():
        top_swap.wait_send()

    @pl.when(z < 3)
    def _():
        bottom_swap.wait_send()

    for (sends, copy), _, _ in list(halves.values()) + list(seconds.values()):
        when(sends, copy.wait_send)
    for sends, copy in across_x[0] + across_x[1]:
        when(sends, copy.wait_send)
    for (part, n), (entry, _, _) in thirds.items():
        for sends, copy, _ in entry[1:] if part >= 4 and n == 1 else entry:
            when(sends, copy.wait_send)
    for entry in fourths.values():
        for sends, copy, _ in entry:
            when(sends, copy.wait_send)
    x_pair.wait_send()

    @pl.when(sends_rim)
    def _():
        for copy in rim_out:
            copy.wait_send()

    for copy in ct_pair:
        copy.wait_send()
    pl.when(z > 0)(slope_up.wait_send)
    pl.when(z < 3)(slope_down.wait_send)
    for k in range(2):
        up_own[k].wait()
        up_pair[k].wait()
    ig_pair.wait_send()
    gf_copy.wait()
    tab_copy.wait()


def fused(features, weight, cot, shift_row, frame_id):
    any_space = pl.BlockSpec(memory_space=pl.ANY)
    vmem = pl.BlockSpec(memory_space=pltpu.VMEM)
    bf16, f32 = jnp.bfloat16, jnp.float32
    dma = pltpu.SemaphoreType.DMA
    return pl.pallas_call(
        kernel,
        out_shape=(
            jax.ShapeDtypeStruct((4, 2 * WIDTH, 256), bf16),
            jax.ShapeDtypeStruct((2, 2, 2, 16, 9 * CIN), bf16),
            jax.ShapeDtypeStruct((2, WIDTH, CIN), bf16),
            jax.ShapeDtypeStruct((16, 8, 128), f32),
        ),
        in_specs=[any_space, any_space, any_space, vmem, pl.BlockSpec(memory_space=pltpu.SMEM)],
        out_specs=[any_space] * 4,
        scratch_shapes=[
            pltpu.VMEM((3, 6, WIDTH, CIN), bf16),
            pltpu.VMEM((3, 6, WIDTH, HALF), bf16),
            pltpu.VMEM((256, 4 * WIDTH), bf16),
            pltpu.VMEM((PARTS, 2, 2, 2, 2, 2, 16, PCOLS), bf16),
            pltpu.VMEM((PARTS, 2, 2, 2, 2, 2, 16, GCOLS), bf16),
            pltpu.VMEM((PARTS, 2, 2, 2, 2, 2, 16, GCOLS), bf16),
            pltpu.VMEM((PARTS, 2, 2, 2, 2, 2, 16, GCOLS), bf16),
            pltpu.VMEM((PARTS, 3, 2, 2, 16, GCOLS), bf16),
            pltpu.VMEM((PARTS, 3, 16, GCOLS), bf16),
            pltpu.VMEM((2, 2, 2, 16, 9 * CIN), bf16),
            pltpu.VMEM((4, 2 * WIDTH, 256), bf16),
            pltpu.VMEM((2, 4, WIDTH, 256), bf16),
            pltpu.VMEM((2, 4, WIDTH, 256), bf16),
            pltpu.VMEM((4, 2 * WIDTH, 256), bf16),
            pltpu.VMEM((2, 2 * WIDTH, 128), f32),
            pltpu.VMEM((WIDTH, 256), f32),
            pltpu.VMEM((2, WIDTH, CIN), f32),
            pltpu.VMEM((2, WIDTH, CIN), f32),
            pltpu.VMEM((2, WIDTH, CIN), f32),
            pltpu.VMEM((2, WIDTH, CIN), bf16),
            pltpu.VMEM((8, 128), f32),
            pltpu.VMEM((7, 8, 128), f32),
            pltpu.VMEM((16, 8, 128), f32),
            dma((17,)),
            dma((7,)),
            dma((7,)),
            dma((11,)),
            dma((11,)),
            dma((3,)),
            dma((3,)),
            dma((4, 3)),
            dma((4, 3)),
            dma((2,)),
            dma((2,)),
            dma((PARTS, 13)),
            dma((PARTS, 13)),
            dma((2, 7)),
            dma((2, 7)),
            dma((2,)),
            dma((2,)),
            dma((5,)),
            dma((5,)),
            dma((7,)),
            dma((7,)),
            dma((6,)),
            dma((6,)),
        ],
        compiler_params=pltpu.CompilerParams(
            collective_id=0, has_side_effects=True, vmem_limit_bytes=60 * 2**20
        ),
        cost_estimate=pl.CostEstimate(
            flops=6 * 768 * 4608 * 1024, bytes_accessed=2 * 10**7, transcendentals=3 * 768 * 1024
        ),
        name="conv_block",
    )(features, weight, cot, shift_row, frame_id)


def finish(up, gw, gf, tab, up_out, gw_out, gf_out, table_out, gw_in, gw_wide, tab_in, table, up_in, gf_in, sems):
    moves = [
        (
            pltpu.make_async_copy(source.at[k], held.at[k], sems.at[2 * (first + k)]),
            pltpu.make_async_copy(held.at[k], out.at[k], sems.at[2 * (first + k) + 1]),
        )
        for source, held, out, first, count in ((up, up_in, up_out, 0, 4), (gf, gf_in, gf_out, 4, 2))
        for k in range(count)
    ]
    loads = [
        pltpu.make_async_copy(gw.at[k // 4, k // 2 % 2, k % 2], gw_in.at[k], sems.at[12 + k]) for k in range(8)
    ]
    stores = [
        pltpu.make_async_copy(gw_wide.at[pl.ds(16 * k, 16)], gw_out.at[pl.ds(16 * k, 16)], sems.at[20 + k])
        for k in range(8)
    ]
    tab_load = pltpu.make_async_copy(tab, tab_in, sems.at[28])
    table_store = pltpu.make_async_copy(table, table_out, sems.at[29])
    tab_load.start()
    for copy in loads + [load for load, _ in moves]:
        copy.start()

    tab_load.wait()
    sums = jnp.concatenate([tab_in[:, k, :] for k in range(4)], axis=1)
    frames = tab_in[:, 4, 0:1]
    rows = 128 * -(-table.shape[0] // 128)
    video = lax.broadcasted_iota(jnp.int32, (16, rows), 1).astype(jnp.float32)
    picker = jnp.where(frames == video, 1.0, 0.0)
    total = lax.dot_general(
        picker, sums, (((0,), (0,)), ((), ())),
        precision=lax.Precision.HIGHEST, preferred_element_type=jnp.float32,
    )
    table[...] = total[: table.shape[0]]
    table_store.start()

    for k in range(8):
        loads[k].wait()
        gw_wide[16 * k : 16 * k + 16, :] = gw_in[k].astype(jnp.float32)
        stores[k].start()
    for load, store in moves:
        load.wait()
        store.start()
    for copy in stores + [store for _, store in moves] + [table_store]:
        copy.wait()


def finished(up, gw, gf, tab, video_len):
    hbm = pl.BlockSpec(memory_space=pltpu.HBM)
    bf16, f32 = jnp.bfloat16, jnp.float32
    return pl.pallas_call(
        finish,
        out_shape=(
            jax.ShapeDtypeStruct((4, 2 * WIDTH, 256), bf16),
            jax.ShapeDtypeStruct((128, 9 * CIN), f32),
            jax.ShapeDtypeStruct((2, WIDTH, CIN), bf16),
            jax.ShapeDtypeStruct((video_len, CIN), f32),
        ),
        in_specs=[hbm] * 4,
        out_specs=[hbm] * 4,
        scratch_shapes=[
            pltpu.VMEM((8, 16, 9 * CIN), bf16),
            pltpu.VMEM((128, 9 * CIN), f32),
            pltpu.VMEM((16, 8, 128), f32),
            pltpu.VMEM((video_len, CIN), f32),
            pltpu.VMEM((4, 2 * WIDTH, 256), bf16),
            pltpu.VMEM((2, WIDTH, CIN), bf16),
            pltpu.SemaphoreType.DMA((30,)),
        ],
        compiler_params=pltpu.CompilerParams(vmem_limit_bytes=60 * 2**20),
        cost_estimate=pl.CostEstimate(flops=10**8, bytes_accessed=10**7, transcendentals=0),
        name="finish",
    )(up, gw, gf, tab)


def shards(features, frame_table, frame_ids, conv_weight, cotangent):
    video_len = frame_table.shape[0]
    shift = lax.dynamic_slice_in_dim(frame_table, frame_ids[0], 1, axis=0).astype(jnp.float32)
    up, gw, gf, tab = fused(
        features[0], conv_weight.reshape(2, 2, 2, 16, 9 * CIN), cotangent[0], shift, frame_ids
    )
    up, grad_weight, gf, grad_table = finished(up, gw, gf, tab, video_len)
    return (up[None], grad_weight, gf[None], grad_table)


def solution(mesh):
    return jax.shard_map(
        shards,
        mesh=mesh,
        in_specs=(
            P(("fsdp", "dp"), "tile", None, None),
            P(),
            P(("fsdp", "dp")),
            P("fsdp", None),
            P(("fsdp", "dp"), "tile", None, None),
        ),
        out_specs=(
            P(("fsdp", "dp"), "tile", None, None),
            P("fsdp", None),
            P(("fsdp", "dp"), "tile", None, None),
            P(),
        ),
        check_vma=False,
    )
```

```python
import jax
import jax.numpy as jnp
from jax import lax
from jax.experimental import pallas as pl
from jax.experimental.pallas import tpu as pltpu
from jax.sharding import PartitionSpec as P

inv_root_two = 0.7071067811865476
inv_root_tau = 0.3989422804014327

WIDTH = 384
CIN = 512
HALF = 512
PARTS = 6
PCOLS = 768
CHUNKS = 18

DIMS = 6

FIRST = [None, None, (2, 3), (3, 2), (4, 5), (5, 4)]
NEAR_RUNS = ((0, 1, 2, 3, 4, 5),)
FAR_RUNS = ((0, 1), (2, 3), (4, 5))
SPANS = ((0, 2), (2, 2), (4, 4), (8, 4), (12, 3), (15, 3))
GCOLS = 1024

MESH = pl.DeviceIdType.MESH


def kernel(
    feat, weight, cot, shift_row_in, frame_id,
    up_out, gw_out, gf_out, tab_out,
    xs, ss, st, wall, gwb, got0, got1, got2, got3, fin, ctv, cts, actv, upb, wide, acc, igp, igo, igr, gfb,
    trow, tpeer, tall,
    loc_sem, x_send, x_recv, o_send, o_recv, n_send, n_recv, q_send, q_recv, s_send, s_recv,
    r_send, r_recv, f_send, f_recv, u_send, u_recv, i_send, i_recv, t_send, t_recv, v_send, v_recv,
):
    f = lax.axis_index("fsdp")
    t = lax.axis_index("tile")
    lo = lax.axis_index("dp")
    x, h = f // 2, f % 2
    z, c = t // 2, t % 2
    xa, xb = x // 2, x % 2
    xe = (xa + xb) % 2
    ye = (h + lo) % 2
    za = z // 2
    ze = (za + z % 2) % 2
    keep = (c + xe) % 2
    active, passive = c == xa, c != xa
    mine = {1: keep, 2: h, 3: ye, 4: za, 5: ze}
    x_flip = x + 1 - 2 * xb
    z_flip = z + 1 - 2 * (z % 2)
    partner = {
        0: {"fsdp": (3 - x) * 2 + h},
        1: {"fsdp": x_flip * 2 + h},
        2: {"fsdp": x * 2 + 1 - h, "dp": 1 - lo},
        3: {"dp": 1 - lo},
        4: {"tile": (3 - z) * 2 + c},
        5: {"tile": z_flip * 2 + c},
    }
    other_core = {"tile": 2 * z + 1 - c}
    two_away = {"fsdp": (x + 2) % 4 * 2 + h}
    quarter = (z + 2 * ye) % 4
    holders = [
        {"tile": (z + k // 2) % 4 * 2 + c, "dp": (lo + k % 2) % 2} for k in range(1, 8)
    ]

    def remote(src, dst, send_sem, recv_sem, device):
        return pltpu.make_async_remote_copy(
            src_ref=src, dst_ref=dst, send_sem=send_sem, recv_sem=recv_sem,
            device_id=device, device_id_type=MESH,
        )

    barrier = pltpu.get_barrier_semaphore()
    for k in range(1, 8):
        pl.semaphore_signal(barrier, inc=1, device_id={"tile": (t + k) % 8}, device_id_type=MESH)
    frame = f * 2 + lo
    for k in range(1, 16):
        to = (frame + k) % 16
        pl.semaphore_signal(
            barrier, inc=1, device_id={"fsdp": to // 2, "dp": to % 2}, device_id_type=MESH
        )

    for k in (3, 5, 7):
        pl.semaphore_signal(barrier, inc=1, device_id=holders[k - 1], device_id_type=MESH)

    near, far = keep, 1 - keep
    own_x = pltpu.make_async_copy(feat, xs.at[1, pl.ds(1 + 2 * c, 2)], loc_sem.at[0])
    own_x.start()
    own_w = [
        pltpu.make_async_copy(
            weight.at[:, :, :, :, pl.ds(PCOLS * part, PCOLS)], wall.at[part, near, h], loc_sem.at[1 + part]
        )
        for part in range(PARTS)
    ]

    @pl.when(active)
    def _():
        for copy in own_w:
            copy.start()

    own_ct = []
    for k in range(2):
        own_ct.append(
            pltpu.make_async_copy(cot.at[2 * k + c], ctv.at[2 * c + k], loc_sem.at[7 + k])
        )
        own_ct[-1].start()

    own_x.wait()
    for k in range(2):
        for lane in range(4):
            at = pl.ds(128 * lane, 128)
            row = xs[1, 1 + 2 * c + k, :, at].astype(jnp.float32) + shift_row_in[:, at]
            xs[1, 1 + 2 * c + k, :, at] = row.astype(jnp.bfloat16)

    pl.semaphore_wait(barrier, 25)

    def same(pair, half, number, send_sem, recv_sem, device, eighth=None):
        place = wall.at[:, pair, half, number // 2, number % 2]
        if eighth is not None:
            place = wall.at[:, pair, half, number // 2, number % 2, eighth]
        return remote(place, place, send_sem, recv_sem, device)

    turn = [(quarter + k) % 4 for k in range(4)]
    to_flip = [same(near, h, turn[k], o_send.at[k], o_recv.at[k], partner[1]) for k in range(4)]
    to_turn = [same(near, h, turn[k], o_send.at[3 + k], o_recv.at[3 + k], partner[0]) for k in range(1, 4)]
    first_turn = [same(near, h, quarter, o_send.at[9 + e], o_recv.at[9 + e], partner[0], e) for e in range(2)]
    relay = [same(near, h, quarter, o_send.at[7 + e], o_recv.at[7 + e], partner[1], e) for e in range(2)]
    from_flip = [same(far, h, turn[k], o_send.at[k], o_recv.at[k], partner[1]) for k in range(4)]
    from_far = [same(far, h, quarter, o_send.at[7 + e], o_recv.at[7 + e], partner[1], e) for e in range(2)]
    across = [same(near, h, quarter, n_send.at[e], n_recv.at[e], partner[2], e) for e in range(2)]
    crossed = [same(near, 1 - h, quarter, n_send.at[e], n_recv.at[e], partner[2], e) for e in range(2)]
    across_far = [same(far, h, quarter, n_send.at[2 + e], n_recv.at[2 + e], partner[2], e) for e in range(2)]
    crossed_far = [same(far, 1 - h, quarter, n_send.at[2 + e], n_recv.at[2 + e], partner[2], e) for e in range(2)]
    passed = {}
    theirs = {3: (quarter + 2) % 4, 4: (3 - z + 2 * ye) % 4, 5: (z_flip + 2 * ye) % 4}
    for k, (pair, half, e) in enumerate(((near, 1 - h, 0), (near, 1 - h, 1), (far, 1 - h, 0), (far, 1 - h, 1), (far, h, None))):
        for j, dim in enumerate((3, 4, 5)):
            passed[k, j] = (
                same(pair, half, quarter, q_send.at[k, j], q_recv.at[k, j], partner[dim], e),
                same(pair, half, theirs[dim], q_send.at[k, j], q_recv.at[k, j], partner[dim], e),
            )

    def pass_on(k):
        for j in range(3):
            passed[k, j][0].start()

    def passed_in(k):
        for j in range(3):
            passed[k, j][1].wait_recv()

    @pl.when(active)
    def _():
        for copy in own_w:
            copy.wait()
        for e in range(2):
            first_turn[e].start()
            across[e].start()
        to_flip[0].start()

    x_pair = remote(
        xs.at[1, pl.ds(1 + 2 * c, 2)], xs.at[1, pl.ds(1 + 2 * c, 2)], x_send.at[0], x_recv.at[0], other_core
    )
    x_pair_in = remote(
        xs.at[1, pl.ds(3 - 2 * c, 2)], xs.at[1, pl.ds(3 - 2 * c, 2)], x_send.at[0], x_recv.at[0], other_core
    )
    rim_cols = WIDTH // 2
    sends_rim = jnp.where(c == 0, z > 0, z < 3)
    z_rim = jnp.where(c == 0, jnp.maximum(z - 1, 0), jnp.minimum(z + 1, 3))
    rim_out = [
        remote(
            xs.at[1, 1 + 3 * c, pl.ds(rim_cols * k, rim_cols)],
            xs.at[1, 5 - 5 * c, pl.ds(rim_cols * k, rim_cols)],
            x_send.at[1 + k], x_recv.at[1 + c], {"tile": 2 * z_rim + k},
        )
        for k in range(2)
    ]

    def rim_part(row, core, sem):
        at = xs.at[1, row, pl.ds(pl.multiple_of(rim_cols * core, rim_cols), rim_cols)]
        return remote(at, at, x_send.at[sem], x_recv.at[sem], other_core)

    top_in, bottom_in = rim_part(0, c, 2), rim_part(5, c, 1)
    top_swap, bottom_swap = rim_part(0, c, 5), rim_part(5, c, 6)
    top_swapped, bottom_swapped = rim_part(0, 1 - c, 5), rim_part(5, 1 - c, 6)

    @pl.when(sends_rim)
    def _():
        for copy in rim_out:
            copy.start()

    x_pair.start()

    ct_pair = []
    for k in range(2):
        ct_pair.append(
            remote(cot.at[2 * k + 1 - c], ctv.at[2 * c + k], x_send.at[3 + k], x_recv.at[3 + k], other_core)
        )
        ct_pair[-1].start()

    @pl.when(z == 0)
    def _():
        xs[1, 0] = jnp.zeros((WIDTH, CIN), jnp.bfloat16)
        ss[1, 0] = jnp.zeros((WIDTH, HALF), jnp.bfloat16)

    @pl.when(z == 3)
    def _():
        xs[1, 5] = jnp.zeros((WIDTH, CIN), jnp.bfloat16)
        ss[1, 5] = jnp.zeros((WIDTH, HALF), jnp.bfloat16)

    column = lax.broadcasted_iota(jnp.int32, (WIDTH, 128), 0)

    def shift_row(ref, row):
        for lane in range(4):
            at = pl.ds(128 * lane, 128)
            values = ref[1, row, :, at].astype(jnp.float32)
            right = jnp.where(column == 0, 0.0, pltpu.roll(values, 1, 0))
            left = jnp.where(column == WIDTH - 1, 0.0, pltpu.roll(values, WIDTH - 1, 0))
            ref[0, row, :, at] = right.astype(jnp.bfloat16)
            ref[2, row, :, at] = left.astype(jnp.bfloat16)

    def shift_rows(ref, first, count):
        @pl.loop(0, count)
        def _(k):
            shift_row(ref, first + k)

    @pl.when(active)
    def _():
        for e in range(2):
            first_turn[e].wait_send()
        to_turn[0].start()

    shift_rows(xs, 1 + 2 * c, 2)

    @pl.when(active)
    def _():
        for e in range(2):
            crossed[e].wait_recv()
            pass_on(e)
        for k in range(1, 3):
            to_turn[k].start()
        to_flip[1].start()

    @pl.when(passive)
    def _():
        for e in range(2):
            first_turn[e].wait_recv()
            across[e].start()
            relay[e].start()

    x_pair_in.wait_recv()
    shift_rows(xs, 3 - 2 * c, 2)

    @pl.when(z > 0)
    def _():
        top_in.wait_recv()
        top_swap.start()

    @pl.when(z < 3)
    def _():
        bottom_in.wait_recv()
        bottom_swap.start()

    @pl.when(passive)
    def _():
        for e in range(2):
            crossed[e].wait_recv()
            pass_on(e)

    for copy in own_ct:
        copy.wait()
    for copy in ct_pair:
        copy.wait_recv()

    @pl.loop(0, 4)
    def _(r):
        for lane in range(2):
            wide[lane] = ctv[r, :, 128 * lane : 128 * lane + 128].astype(jnp.float32)
        for v in range(2):
            for lane in range(2):
                cts[v, r, :, 128 * lane : 128 * lane + 128] = wide[lane, pl.ds(v, WIDTH, 2), :].astype(jnp.bfloat16)

    @pl.when(z > 0)
    def _():
        top_swapped.wait_recv()

    @pl.when(z < 3)
    def _():
        bottom_swapped.wait_recv()

    shift_rows(xs, 0, 1)
    shift_rows(xs, 5, 1)

    @pl.when(active)
    def _():
        from_flip[0].wait_recv()
        for copy in across_far:
            copy.start()
        for k in range(2, 4):
            to_flip[k].start()

    @pl.when(passive)
    def _():
        for e in range(2):
            from_far[e].wait_recv()
            across_far[e].start()
        pass_on(4)

    def forward_row(v, r):
        lhs = jnp.concatenate(
            [
                xs[(kk // 2) % 3, r + kk // 6, :, 256 * (kk % 2) : 256 * (kk % 2) + 256]
                for kk in range(CHUNKS)
            ],
            axis=1,
        )
        rhs = jnp.concatenate(
            [
                wall[kk // 3, v, :, :, :, :, :, 256 * (kk % 3) : 256 * (kk % 3) + 256].reshape(256, 256)
                for kk in range(CHUNKS)
            ],
            axis=1,
        )
        acc[...] = lax.dot_general(
            lhs, rhs, (((1,), (1,)), ((), ())), preferred_element_type=jnp.float32
        )

        @pl.loop(0, WIDTH // 32)
        def _(j):
            rows = pl.ds(pl.multiple_of(j * 32, 32), 32)
            value = acc[rows]
            grown = 0.5 * (1.0 + lax.erf(value * inv_root_two))
            slope = grown + value * jnp.exp(-0.5 * value * value) * inv_root_tau
            actv[v, r, rows] = (value * grown).astype(jnp.bfloat16)
            out = pl.ds(pl.multiple_of(256 * v, 256), 256)
            ss[1, r + 1, rows, out] = (cts[v, r, rows].astype(jnp.float32) * slope).astype(jnp.bfloat16)

    def at(part, fixed):
        return (part,) + tuple(fixed.get(d, slice(None)) for d in range(1, 6)) + (slice(None), lanes_of(part))

    def lanes_of(part):
        return pl.ds(0, 256 * SPANS[part][1])

    def in_slot(slots, slot):
        return slot + (slice(None),) * (len(slots.shape) - 1 - len(slot)) + (lanes_of(slot[0]),)

    def when(condition, body):
        if condition is None:
            body()
        else:
            pl.when(condition)(body)

    two_y = {"fsdp": x * 2 + 1 - h}
    two_z = {"tile": (z + 2) % 4 * 2 + c}

    halves, seconds, thirds, fourths = {}, {}, {}, {}

    def half_copy(part, n, dim, there, sends):
        place = at(part, there)
        return (
            sends,
            remote(gwb.at[place], got0.at[place], r_send.at[part, n], r_recv.at[part, n], partner[dim]),
        )

    def second_copy(part, n, dim, there, sends):
        place = at(part, there)
        return (
            sends,
            remote(
                gwb.at[place], got1.at[place], r_send.at[part, 2 + n], r_recv.at[part, 2 + n], partner[dim]
            ),
        )

    def slot_copy(part, there, slots, slot, sem, device, sends):
        return (
            sends,
            remote(
                gwb.at[at(part, there)], slots.at[in_slot(slots, slot)], r_send.at[part, sem], r_recv.at[part, sem], device
            ),
            slot,
        )

    def flips(axis):
        da, db = 2 * axis, 2 * axis + 1
        there = {da: 1 - mine[da], db: 1 - mine[db]}
        return (
            ({da: there[da], db: mine[db]}, partner[da]),
            ({da: mine[da], db: there[db]}, partner[db]),
            (there, two_y if axis == 1 else two_z),
        )

    def along_x(part, kept, slots, sem):
        return [
            slot_copy(part, {**kept, 1: pair}, slots, (part, j), sem + j, device, sends)
            for j, (sends, pair, device) in enumerate(
                ((passive, near, partner[0]), (active, far, partner[1]), (passive, far, two_away))
            )
        ]

    across_x = {
        part: [
            (
                sends,
                remote(
                    gwb.at[at(part, {1: pair})], slots.at[at(part, {1: place})],
                    r_send.at[part, j], r_recv.at[part, j], device,
                ),
            )
            for j, (sends, pair, device, slots, place) in enumerate(
                (
                    (passive, near, partner[0], got0, near),
                    (active, far, partner[1], got1, far),
                    (passive, far, two_away, got0, near),
                )
            )
        ]
        for part in (0, 1)
    }
    for part in (0, 1):
        thirds[part, 1] = (
            [
                slot_copy(part, {1: near, **there}, got2, (part, j), 7 + j, device, active)
                for j, (there, device) in enumerate(flips(1))
            ],
            active, at(part, {1: near, 2: h, 3: ye}),
        )
        fourths[part] = [
            slot_copy(part, {1: near, 2: h, 3: ye, **there}, got3, (part, j), 10 + j, device, active)
            for j, (there, device) in enumerate(flips(2))
        ]
    for part in range(2, 6):
        one, two = FIRST[part]
        first = {one: mine[one]}
        both = {**first, two: mine[two]}
        for n, pair in enumerate((near, far)):
            halves[part, n] = (
                half_copy(part, n, one, {1: pair, one: 1 - mine[one]}, None),
                None, at(part, {1: pair, **first}),
            )
            seconds[part, n] = (
                second_copy(part, n, two, {1: pair, **first, two: 1 - mine[two]}, None),
                None, at(part, {1: pair, **both}),
            )
            if part < 4:
                thirds[part, n] = (
                    [
                        slot_copy(
                            part, {1: pair, **both, **there}, got2, (part, j, 0, pair), 4 + 3 * n + j, device, None
                        )
                        for j, (there, device) in enumerate(flips(2))
                    ],
                    None, at(part, {1: pair, **both, 4: za, 5: ze}),
                )
        if part < 4:
            fourths[part] = along_x(part, {**both, 4: za, 5: ze}, got3, 10)
        else:
            copies = along_x(part, both, got2, 4)
            thirds[part, 0] = ([copies[0]], None, None)
            thirds[part, 1] = (copies, active, at(part, {**both, 1: near}))
            fourths[part] = [
                slot_copy(part, {1: near, **both, **there}, got3, (part, j), 10 + j, device, active)
                for j, (there, device) in enumerate(flips(1))
            ]

    def add_across(part):
        def add():
            for _, copy in across_x[part]:
                copy.wait_recv()
            here, there = at(part, {1: near}), at(part, {1: far})
            total = gwb[here].astype(jnp.float32) + got0[here].astype(jnp.float32)
            total = total + got1[here].astype(jnp.float32) + got0[there].astype(jnp.float32)
            gwb[here] = total.astype(jnp.bfloat16)

        pl.when(active)(add)
        for sends, copy, _ in thirds[part, 1][0]:
            when(sends, copy.start)

    def add_half(part, n):
        if (part, n) in halves:
            (_, copy), receives, here = halves[part, n]

            def add():
                copy.wait_recv()
                total = gwb[here].astype(jnp.float32) + got0[here].astype(jnp.float32)
                gwb[here] = total.astype(jnp.bfloat16)

            when(receives, add)
        if (part, n) in seconds:
            when(seconds[part, n][0][0], seconds[part, n][0][1].start)

    def add_second(part, n):
        if (part, n) not in seconds:
            return
        (_, copy), receives, here = seconds[part, n]

        def add():
            copy.wait_recv()
            total = gwb[here].astype(jnp.float32) + got1[here].astype(jnp.float32)
            gwb[here] = total.astype(jnp.bfloat16)

        when(receives, add)
        entry = thirds[part, n][0]
        for sends, copy, _ in entry[1:] if part >= 4 and n == 1 else entry:
            when(sends, copy.start)

    def add_third(part):
        for n in range(2):
            if (part, n) in thirds and thirds[part, n][2] is not None:
                entry, receives, here = thirds[part, n]

                def add(entry=entry, here=here):
                    total = gwb[here].astype(jnp.float32)
                    for _, copy, slot in entry:
                        copy.wait_recv()
                        total = total + got2[in_slot(got2, slot)].astype(jnp.float32)
                    gwb[here] = total.astype(jnp.bfloat16)

                when(receives, add)
        for sends, copy, _ in fourths[part]:
            when(sends, copy.start)

    def add_fourth(part):
        here = at(part, {1: near, 2: h, 3: ye, 4: za, 5: ze})

        def add():
            total = gwb[here].astype(jnp.float32)
            for _, copy, slot in fourths[part]:
                copy.wait_recv()
                total = total + got3[in_slot(got3, slot)].astype(jnp.float32)
            total = total.astype(jnp.bfloat16)
            first, count = SPANS[part]
            fin[ye, za, ze, :, 256 * first : 256 * (first + count)] = total

        pl.when(active)(add)

    def weight_gradient(pair, order):
        n = 0 if pair is near else 1
        lanes = pl.ds(pl.multiple_of(256 * pair, 256), 256)
        for r in range(4):
            st[:, WIDTH * r : WIDTH * r + WIDTH] = ss[1, r + 1, :, lanes].T
        for run in order:
            for part in run:
                first, count = SPANS[part]
                for j in range(count):
                    kk = first + j
                    window = xs[(kk // 2) % 3, kk // 6 : kk // 6 + 4, :, 256 * (kk % 2) : 256 * (kk % 2) + 256]
                    term = jnp.dot(
                        st[...], window.reshape(4 * WIDTH, 256), preferred_element_type=jnp.float32
                    )
                    gwb[part, pair, :, :, :, :, :, 256 * j : 256 * j + 256] = term.astype(jnp.bfloat16).reshape(
                        2, 2, 2, 2, 16, 256
                    )
            for part in run:
                if (part, n) in halves:
                    sends, copy = halves[part, n][0]
                    when(sends, copy.start)
                if part in across_x:
                    for sends, copy in across_x[part][1:] if n else across_x[part][:1]:
                        when(sends, copy.start)

    passed_in(0)
    passed_in(1)

    @pl.when(passive)
    def _():
        for copy in to_turn:
            copy.wait_recv()

    @pl.loop(0, 4)
    def _(r):
        for e in range(2):

            @pl.when(r == jnp.where(active, 2 + e, 1 + e))
            def _(e=e):
                crossed_far[e].wait_recv()
                pass_on(2 + e)

        forward_row(near, r)

    weight_gradient(near, NEAR_RUNS)

    passed_in(2)
    passed_in(3)

    @pl.when(passive)
    def _():
        passed_in(4)

    @pl.when(active)
    def _():
        for k in range(1, 4):
            from_flip[k].wait_recv()

    @pl.loop(0, 2)
    def _(k):
        forward_row(far, 3 * k)

    rim_above = remote(ss.at[1, 0], ss.at[1, 0], s_send.at[1], s_recv.at[1], other_core)
    rim_below = remote(ss.at[1, 5], ss.at[1, 5], s_send.at[0], s_recv.at[0], other_core)
    slope_up = remote(ss.at[1, 1], ss.at[1, 5], s_send.at[0], s_recv.at[0], {"tile": 2 * jnp.maximum(z - 1, 0) + c})
    slope_down = remote(ss.at[1, 4], ss.at[1, 0], s_send.at[1], s_recv.at[1], {"tile": 2 * jnp.minimum(z + 1, 3) + c})
    pl.when(z > 0)(slope_up.start)
    pl.when(z < 3)(slope_down.start)

    @pl.loop(0, 2)
    def _(k):
        forward_row(far, 2 - k)

    for part in range(2, 6):
        add_half(part, 0)
    weight_gradient(far, FAR_RUNS)

    shift_rows(ss, 1, 4)

    def input_row(r, out):
        lhs = jnp.concatenate([ss[2 - tap % 3, r + 2 - tap // 3] for tap in range(9)], axis=1)
        for e in range(2):
            chunks = []
            for tap in range(9):
                kk = 2 * tap + e
                chunks.append(
                    wall[kk // 3, :, :, :, :, :, :, 256 * (kk % 3) : 256 * (kk % 3) + 256].reshape(512, 256)
                )
            out[:, 256 * e : 256 * e + 256] = jnp.dot(
                lhs, jnp.concatenate(chunks, axis=0), preferred_element_type=jnp.float32
            )

    @pl.loop(0, 2)
    def _(k):
        @pl.when(k == 1)
        def _():
            pl.when(z > 0)(rim_above.wait_recv)
            pl.when(z < 3)(rim_below.wait_recv)
            shift_row(ss, 0)
            shift_row(ss, 5)

        r = jnp.where(k == 0, 2 - c, 3 - 3 * c)
        input_row(r, igp.at[r - 2 * (1 - c)])


    ig_pair = remote(igp, igr, i_send.at[0], i_recv.at[0], other_core)
    ig_pair.start()
    for part in range(2, 6):
        add_second(part, 0)
    for part in range(2, 6):
        add_half(part, 1)
    for part in range(2):
        add_across(part)

    trow[4:8, :] = jnp.full((4, 128), frame_id[0], jnp.int32).astype(jnp.float32)
    trow[0:4, :] = jnp.zeros((4, 128), jnp.float32)

    @pl.loop(0, 2)
    def _(k):
        input_row(2 * c + k, igo.at[k])

    for part in range(2, 6):
        add_second(part, 1)

    ig_pair.wait_recv()

    @pl.loop(0, 2)
    def _(k):
        total = igo[k] + igr[k]
        gfb[k] = total.astype(jnp.bfloat16)
        column_sum = jnp.sum(total, axis=0, keepdims=True)
        for lane in range(4):
            trow[lane : lane + 1, :] += column_sum[:, 128 * lane : 128 * lane + 128]

    gf_copy = pltpu.make_async_copy(gfb, gf_out, loc_sem.at[11])
    gf_copy.start()

    t_copies = []
    for k in range(1, 8):
        copy = remote(trow, tpeer.at[k - 1], t_send.at[k - 1], t_recv.at[k - 1], {"tile": (t + k) % 8})
        copy.start()
        t_copies.append(copy)

    @pl.loop(0, 4)
    def _(r):
        for lane in range(2):
            lanes = pl.ds(128 * lane, 128)
            for v in range(2):
                wide[lane, pl.ds(v, WIDTH, 2), :] = actv[v, r, :, lanes].astype(jnp.float32)
            upb[r, :, lanes] = wide[lane].astype(jnp.bfloat16)

    up_own, up_pair = [], []
    for k in range(2):
        up_own.append(pltpu.make_async_copy(upb.at[2 * c + k], up_out.at[2 * k + c], loc_sem.at[9 + k]))
        up_pair.append(
            remote(upb.at[2 * (1 - c) + k], up_out.at[2 * k + c], u_send.at[k], u_recv.at[k], other_core)
        )
        up_own[-1].start()
        up_pair[-1].start()

    for part in range(PARTS):
        add_third(part)

    for copy in t_copies:
        copy.wait_recv()
    for copy in t_copies:
        copy.wait_send()
    total = trow[0:4, :]
    for k in range(7):
        total = total + tpeer[k, 0:4, :]
    tall[0, 0:4, :] = total
    tall[0, 4:8, :] = trow[4:8, :]
    y = 2 * h + lo
    v_copies = []
    for k in range(1, 4):
        to = (y + k) % 4
        v_copies.append(
            remote(tall.at[0], tall.at[k], v_send.at[k - 1], v_recv.at[k - 1], {"fsdp": 2 * x + to // 2, "dp": to % 2})
        )
    for k in range(1, 4):
        to = (x + k) % 4
        v_copies.append(
            remote(
                tall.at[pl.ds(0, 4)], tall.at[pl.ds(4 * k, 4)], v_send.at[2 + k], v_recv.at[2 + k], {"fsdp": 2 * to + h}
            )
        )
    for copy in v_copies[:3]:
        copy.start()

    spreads, to_pair, to_self = [], [], []
    groups = ((0, 1, 2), (3, 4, 5))
    for g, parts in enumerate(groups):
        first, last = SPANS[parts[0]][0], SPANS[parts[-1]][0] + SPANS[parts[-1]][1]
        cols = pl.ds(256 * first, 256 * (last - first))
        piece_at = fin.at[ye, za, ze, :, cols]
        spreads.append(
            [remote(piece_at, piece_at, f_send.at[g, k], f_recv.at[g, k], holders[k]) for k in range(7)]
        )
        for n, row in enumerate((ye, 1 - ye)):
            held, out = fin.at[row, :, :, :, cols], gw_out.at[row, :, :, :, cols]
            sem = 2 * g + n
            to_pair.append(remote(held, out, i_send.at[1 + sem], i_recv.at[1 + sem], other_core))
            to_self.append(pltpu.make_async_copy(held, out, loc_sem.at[12 + sem]))

    for g, parts in enumerate(groups):
        for part in parts:
            add_fourth(part)

        @pl.when(active)
        def _(g=g):
            for copy in spreads[g]:
                copy.start()

    for copy in v_copies[:3]:
        copy.wait_recv()
    for copy in v_copies[3:]:
        copy.start()

    @pl.when(active)
    def _():
        for g in range(2):
            for n in range(2):
                for k in range(1 - n, 7, 2):
                    spreads[g][k].wait_recv()
                to_pair[2 * g + n].start()
                to_self[2 * g + n].start()
        for g in range(2):
            for copy in spreads[g]:
                copy.wait_send()
        for n in range(4):
            to_self[n].wait()
            to_pair[n].wait_send()

    @pl.when(passive)
    def _():
        for n in range(4):
            to_pair[n].wait_recv()

    for copy in v_copies[3:]:
        copy.wait_recv()
    for copy in v_copies:
        copy.wait_send()
    tab_copy = pltpu.make_async_copy(tall, tab_out, loc_sem.at[16])
    tab_copy.start()

    @pl.when(active)
    def _():
        for copy in to_turn + to_flip:
            copy.wait_send()

    @pl.when(passive)
    def _():
        for copy in relay:
            copy.wait_send()
        for j in range(3):
            passed[4, j][0].wait_send()

    for copy in across + across_far:
        copy.wait_send()
    for k in range(4):
        for j in range(3):
            passed[k, j][0].wait_send()

    @pl.when(z > 0)
    def _():
        top_swap.wait_send()

    @pl.when(z < 3)
    def _():
        bottom_swap.wait_send()

    for (sends, copy), _, _ in list(halves.values()) + list(seconds.values()):
        when(sends, copy.wait_send)
    for sends, copy in across_x[0] + across_x[1]:
        when(sends, copy.wait_send)
    for (part, n), (entry, _, _) in thirds.items():
        for sends, copy, _ in entry[1:] if part >= 4 and n == 1 else entry:
            when(sends, copy.wait_send)
    for entry in fourths.values():
        for sends, copy, _ in entry:
            when(sends, copy.wait_send)
    x_pair.wait_send()

    @pl.when(sends_rim)
    def _():
        for copy in rim_out:
            copy.wait_send()

    for copy in ct_pair:
        copy.wait_send()
    pl.when(z > 0)(slope_up.wait_send)
    pl.when(z < 3)(slope_down.wait_send)
    for k in range(2):
        up_own[k].wait()
        up_pair[k].wait()
    ig_pair.wait_send()
    gf_copy.wait()
    tab_copy.wait()


def fused(features, weight, cot, shift_row, frame_id):
    any_space = pl.BlockSpec(memory_space=pl.ANY)
    vmem = pl.BlockSpec(memory_space=pltpu.VMEM)
    bf16, f32 = jnp.bfloat16, jnp.float32
    dma = pltpu.SemaphoreType.DMA
    return pl.pallas_call(
        kernel,
        out_shape=(
            jax.ShapeDtypeStruct((4, 2 * WIDTH, 256), bf16),
            jax.ShapeDtypeStruct((2, 2, 2, 16, 9 * CIN), bf16),
            jax.ShapeDtypeStruct((2, WIDTH, CIN), bf16),
            jax.ShapeDtypeStruct((16, 8, 128), f32),
        ),
        in_specs=[any_space, any_space, any_space, vmem, pl.BlockSpec(memory_space=pltpu.SMEM)],
        out_specs=[any_space] * 4,
        scratch_shapes=[
            pltpu.VMEM((3, 6, WIDTH, CIN), bf16),
            pltpu.VMEM((3, 6, WIDTH, HALF), bf16),
            pltpu.VMEM((256, 4 * WIDTH), bf16),
            pltpu.VMEM((PARTS, 2, 2, 2, 2, 2, 16, PCOLS), bf16),
            pltpu.VMEM((PARTS, 2, 2, 2, 2, 2, 16, GCOLS), bf16),
            pltpu.VMEM((PARTS, 2, 2, 2, 2, 2, 16, GCOLS), bf16),
            pltpu.VMEM((PARTS, 2, 2, 2, 2, 2, 16, GCOLS), bf16),
            pltpu.VMEM((PARTS, 3, 2, 2, 16, GCOLS), bf16),
            pltpu.VMEM((PARTS, 3, 16, GCOLS), bf16),
            pltpu.VMEM((2, 2, 2, 16, 9 * CIN), bf16),
            pltpu.VMEM((4, 2 * WIDTH, 256), bf16),
            pltpu.VMEM((2, 4, WIDTH, 256), bf16),
            pltpu.VMEM((2, 4, WIDTH, 256), bf16),
            pltpu.VMEM((4, 2 * WIDTH, 256), bf16),
            pltpu.VMEM((2, 2 * WIDTH, 128), f32),
            pltpu.VMEM((WIDTH, 256), f32),
            pltpu.VMEM((2, WIDTH, CIN), f32),
            pltpu.VMEM((2, WIDTH, CIN), f32),
            pltpu.VMEM((2, WIDTH, CIN), f32),
            pltpu.VMEM((2, WIDTH, CIN), bf16),
            pltpu.VMEM((8, 128), f32),
            pltpu.VMEM((7, 8, 128), f32),
            pltpu.VMEM((16, 8, 128), f32),
            dma((17,)),
            dma((7,)),
            dma((7,)),
            dma((11,)),
            dma((11,)),
            dma((4,)),
            dma((4,)),
            dma((5, 3)),
            dma((5, 3)),
            dma((2,)),
            dma((2,)),
            dma((PARTS, 13)),
            dma((PARTS, 13)),
            dma((2, 7)),
            dma((2, 7)),
            dma((2,)),
            dma((2,)),
            dma((5,)),
            dma((5,)),
            dma((7,)),
            dma((7,)),
            dma((6,)),
            dma((6,)),
        ],
        compiler_params=pltpu.CompilerParams(
            collective_id=0, has_side_effects=True, vmem_limit_bytes=60 * 2**20
        ),
        cost_estimate=pl.CostEstimate(
            flops=6 * 768 * 4608 * 1024, bytes_accessed=2 * 10**7, transcendentals=3 * 768 * 1024
        ),
        name="conv_block",
    )(features, weight, cot, shift_row, frame_id)


def finish(up, gw, gf, tab, up_out, gw_out, gf_out, table_out, gw_in, gw_wide, tab_in, table, up_in, gf_in, sems):
    moves = [
        (
            pltpu.make_async_copy(source.at[k], held.at[k], sems.at[2 * (first + k)]),
            pltpu.make_async_copy(held.at[k], out.at[k], sems.at[2 * (first + k) + 1]),
        )
        for source, held, out, first, count in ((up, up_in, up_out, 0, 4), (gf, gf_in, gf_out, 4, 2))
        for k in range(count)
    ]
    loads = [
        pltpu.make_async_copy(gw.at[k // 4, k // 2 % 2, k % 2], gw_in.at[k], sems.at[12 + k]) for k in range(8)
    ]
    stores = [
        pltpu.make_async_copy(gw_wide.at[pl.ds(16 * k, 16)], gw_out.at[pl.ds(16 * k, 16)], sems.at[20 + k])
        for k in range(8)
    ]
    tab_load = pltpu.make_async_copy(tab, tab_in, sems.at[28])
    table_store = pltpu.make_async_copy(table, table_out, sems.at[29])
    tab_load.start()
    for copy in loads + [load for load, _ in moves]:
        copy.start()

    tab_load.wait()
    sums = jnp.concatenate([tab_in[:, k, :] for k in range(4)], axis=1)
    frames = tab_in[:, 4, 0:1]
    rows = 128 * -(-table.shape[0] // 128)
    video = lax.broadcasted_iota(jnp.int32, (16, rows), 1).astype(jnp.float32)
    picker = jnp.where(frames == video, 1.0, 0.0)
    total = lax.dot_general(
        picker, sums, (((0,), (0,)), ((), ())),
        precision=lax.Precision.HIGHEST, preferred_element_type=jnp.float32,
    )
    table[...] = total[: table.shape[0]]
    table_store.start()

    for k in range(8):
        loads[k].wait()
        gw_wide[16 * k : 16 * k + 16, :] = gw_in[k].astype(jnp.float32)
        stores[k].start()
    for load, store in moves:
        load.wait()
        store.start()
    for copy in stores + [store for _, store in moves] + [table_store]:
        copy.wait()


def finished(up, gw, gf, tab, video_len):
    hbm = pl.BlockSpec(memory_space=pltpu.HBM)
    bf16, f32 = jnp.bfloat16, jnp.float32
    return pl.pallas_call(
        finish,
        out_shape=(
            jax.ShapeDtypeStruct((4, 2 * WIDTH, 256), bf16),
            jax.ShapeDtypeStruct((128, 9 * CIN), f32),
            jax.ShapeDtypeStruct((2, WIDTH, CIN), bf16),
            jax.ShapeDtypeStruct((video_len, CIN), f32),
        ),
        in_specs=[hbm] * 4,
        out_specs=[hbm] * 4,
        scratch_shapes=[
            pltpu.VMEM((8, 16, 9 * CIN), bf16),
            pltpu.VMEM((128, 9 * CIN), f32),
            pltpu.VMEM((16, 8, 128), f32),
            pltpu.VMEM((video_len, CIN), f32),
            pltpu.VMEM((4, 2 * WIDTH, 256), bf16),
            pltpu.VMEM((2, WIDTH, CIN), bf16),
            pltpu.SemaphoreType.DMA((30,)),
        ],
        compiler_params=pltpu.CompilerParams(vmem_limit_bytes=60 * 2**20),
        cost_estimate=pl.CostEstimate(flops=10**8, bytes_accessed=10**7, transcendentals=0),
        name="finish",
    )(up, gw, gf, tab)


def shards(features, frame_table, frame_ids, conv_weight, cotangent):
    video_len = frame_table.shape[0]
    shift = lax.dynamic_slice_in_dim(frame_table, frame_ids[0], 1, axis=0).astype(jnp.float32)
    up, gw, gf, tab = fused(
        features[0], conv_weight.reshape(2, 2, 2, 16, 9 * CIN), cotangent[0], shift, frame_ids
    )
    up, grad_weight, gf, grad_table = finished(up, gw, gf, tab, video_len)
    return (up[None], grad_weight, gf[None], grad_table)


def solution(mesh):
    return jax.shard_map(
        shards,
        mesh=mesh,
        in_specs=(
            P(("fsdp", "dp"), "tile", None, None),
            P(),
            P(("fsdp", "dp")),
            P("fsdp", None),
            P(("fsdp", "dp"), "tile", None, None),
        ),
        out_specs=(
            P(("fsdp", "dp"), "tile", None, None),
            P("fsdp", None),
            P(("fsdp", "dp"), "tile", None, None),
            P(),
        ),
        check_vma=False,
    )
```
